32 devices in a mesh: grp: 1, row: 32 (over z, y, x, core).
Axes of the slice: x: 2, y: 2, z: 4, core: 2. Of those that a mesh axis runs over, the one named last changes fastest.
Arguments:
- pair: float32 [128, 128, 128], P(('grp', 'row')), may hold values from -6 to 6
- single: float32 [128, 384], P(('grp', 'row')), may hold values from -6 to 6
- quats: float32 [3, 128], P(None, ('grp', 'row')), may hold values from -6 to 6
- translate: float32 [3, 128], P(None, ('grp', 'row')), may hold values from -12 to 12
- res_mask: int32 [128], P(('grp', 'row')), may hold values 0 or 1
- chain_ids: int32 [128], P(('grp', 'row')), may hold values from 0 to 3, never falling along the last dimension, each value on 1 to 64 neighbouring positions
- tri_weight: bfloat16 [128, 640], replicated, may hold values from -0.5 to 0.5
- tri_out_weight: bfloat16 [128, 128], replicated, may hold values from -0.5 to 0.5
- qkv_weight: bfloat16 [384, 1152], replicated, may hold values from -0.3125 to 0.3125
- bias_weight: float32 [128, 12], replicated, may hold values from -0.5 to 0.5
- head_gamma: float32 [12], replicated, may hold values from 0.05 to 1
- chain_bias: float32 [2, 12], replicated, may hold values from -4 to 4
- out_weight: bfloat16 [2112, 384], replicated, may hold values from -0.125 to 0.125
- frame_weight: float32 [384, 6], replicated, may hold values from -0.3125 to 0.3125
Outputs:
- pair_out: float32 [128, 128, 128], P(('grp', 'row'))
- single_out: float32 [128, 384], P(('grp', 'row'))
- rotation_out: float32 [9, 128], P(None, ('grp', 'row'))
- translation_out: float32 [3, 128], P(None, ('grp', 'row'))
The draws below stay inside these ranges and needn't reach their ends.
Inputs may be any that keep to these rules, and one draw needn't show every extreme that they name: `chain_ids`: chains are contiguous runs of residues, the longest 128 // 2.
All inputs are finite; a program needn't handle non-finite values. No bound on the sum of `res_mask` on one device may be relied on, other than what follows from the above.
Results may differ from the reference program's by a relative error of at most 0.0078.
Values may be sent and summed in bfloat16 or wider, within the bound.
No kernel may reach another device: no remote copies, remote signals or barrier semaphores. Data moves between devices by JAX's collectives and lax.ppermute only.
A program may use at most 64 MiB of HBM per device.

```python
import math
import jax
import jax.numpy as jnp
import numpy as np
from jax import lax

CZ = 128
CH = 128
CS = 384
H = 12
CHEAD = 16
PQ = 4
PV = 8
ITERS = 2
RES_DEV = 4
NRES = 128
N_ROW = 32


def place_ends(values, rng, least, top_value):
    longest = values.shape.index(max(values.shape))
    spots = []
    for shift in (0, 1):
        where = [jax.random.randint(jax.random.fold_in(rng, axis), (), 0, length) for axis, length in enumerate(values.shape)]
        where[longest] = (where[longest] + shift) % values.shape[longest]
        spots.append(tuple(where))
    return values.at[spots[0]].set(least).at[spots[1]].set(top_value)


def steps_of(key, shape, shards, least, largest):
    def one(dim, shards_of):
        draws = jax.random.uniform(jax.random.fold_in(jax.random.fold_in(key, 6), dim), (shards_of,), jnp.float32, least / len(shards), largest / len(shards))
        return jnp.repeat(jnp.exp(draws), shape[dim] // shards_of).reshape((-1,) + (1,) * (len(shape) - dim - 1))

    level = one(*shards[0])
    for cut in shards[1:]:
        level = level * one(*cut)
    return level


def profile(count, total, most, lean):
    weights = [(1 << 20) // math.isqrt(rank ** lean) + 1 for rank in range(2, count + 1)]
    rest, given = total - most - (count - 1), [1] * (count - 1)
    while rest > 0:
        movable = [i for i in range(count - 1) if given[i] < most]
        mass, remaining = sum([weights[i] for i in movable]), rest
        for i in movable:
            addition = min(most - given[i], max(1, remaining * weights[i] // mass), rest)
            given[i] = given[i] + addition
            rest = rest - addition
    return np.array([most] + given)


def uneven(rng, count, total, most, skew):
    if count == 2:
        one = jax.random.randint(rng, (), max(1, total - most), min(most, total - 1) + 1)
        return jnp.stack([one, total - one])
    lengths = jnp.asarray(profile(count, total, most, skew), jnp.int32)
    twos = (count - 1) // 2
    donor, receiver = lengths[1:1 + 2 * twos:2], lengths[2:2 + 2 * twos:2]
    margin = jnp.minimum(donor - 1, most - receiver)
    shifted = jax.random.randint(jax.random.fold_in(rng, 1), (twos,), 0, 1 << 20) % (margin + 1)
    lengths = lengths.at[1:1 + 2 * twos:2].set(donor - shifted).at[2:2 + 2 * twos:2].set(receiver + shifted)
    return lengths[jax.random.permutation(jax.random.fold_in(rng, 2), count)]


def scatter_about(stream_key, dims, deviation, most, cuts=(), held_as=jnp.bfloat16):
    values = deviation * jax.random.normal(stream_key, dims, jnp.float32)
    if cuts:
        values = values * steps_of(stream_key, dims, cuts, -0.22, 0.18)
    return jnp.clip(values, -most, most).astype(held_as)


def setup_inputs(seed: int = 0, part: int = 0) -> dict:
    key_list = jax.random.split(jax.random.key(seed), 15)
    part_splits = jax.random.split(jax.random.fold_in(key_list[14], part), 15)
    return {
        "pair": scatter_about(part_splits[0], (NRES, NRES, CZ), 1.0, 6.0, ((0, 32),), jnp.float32),
        "single": scatter_about(part_splits[1], (NRES, CS), 1.0, 6.0, ((0, 32),), jnp.float32),
        "quats": scatter_about(part_splits[2], (3, NRES), 1.0, 6.0, ((1, 32),), jnp.float32),
        "translate": scatter_about(part_splits[3], (3, NRES), 3.0, 12.0, ((1, 32),), jnp.float32),
        "res_mask": place_ends((jax.random.randint(part_splits[4], (NRES,), 0, 8) < 7).astype(jnp.int32), jax.random.fold_in(part_splits[4], 1), 0, 1),
        "chain_ids": jnp.searchsorted(jnp.cumsum(uneven(part_splits[5], 4, NRES, NRES // 2, 0)), jnp.arange(NRES), side="right").astype(jnp.int32),
        "tri_weight": scatter_about(key_list[6], (CZ, 4 * CH + CZ), CZ ** -0.5, 0.5),
        "tri_out_weight": scatter_about(key_list[7], (CH, CZ), CH ** -0.5, 0.5),
        "qkv_weight": scatter_about(key_list[8], (CS, 3 * H * CHEAD + 6 * H * PQ + 3 * H * PV), CS ** -0.5, 0.3125),
        "bias_weight": scatter_about(key_list[9], (CZ, H), CZ ** -0.5, 0.5, (), jnp.float32),
        "head_gamma": jnp.clip(jnp.exp(jax.random.uniform(key_list[10], (H,), jnp.float32, math.log(0.05), math.log(1.0))), 0.05, 1.0),
        "chain_bias": scatter_about(key_list[11], (2, H), 1.0, 4.0, (), jnp.float32),
        "out_weight": scatter_about(key_list[12], (H * CHEAD + 4 * H * PV + H * CZ, CS), (H * CHEAD + 4 * H * PV + H * CZ) ** -0.5, 0.125),
        "frame_weight": scatter_about(key_list[13], (CS, 6), CS ** -0.5, 0.3125, (), jnp.float32),
    }


highest = lax.Precision.HIGHEST
epsilon = 1e-05
mask_fill = 100000.0

def layer_norm(values):
    center = values - lax.optimization_barrier(jnp.mean(values, axis=-1, keepdims=True))
    spread = lax.optimization_barrier(jnp.mean(center * center, axis=-1, keepdims=True))
    return center * lax.rsqrt(spread + epsilon)

def quat_rotation(vector):
    inverse_norm = lax.rsqrt(1.0 + lax.optimization_barrier(jnp.sum(vector * vector, axis=0)))
    real_part = inverse_norm
    axis_one = vector[0] * inverse_norm
    axis_two = vector[1] * inverse_norm
    axis_three = vector[2] * inverse_norm
    entries = [1.0 - 2.0 * (axis_two * axis_two + axis_three * axis_three), 2.0 * (axis_one * axis_two - real_part * axis_three), 2.0 * (axis_one * axis_three + real_part * axis_two), 2.0 * (axis_one * axis_two + real_part * axis_three), 1.0 - 2.0 * (axis_one * axis_one + axis_three * axis_three), 2.0 * (axis_two * axis_three - real_part * axis_one), 2.0 * (axis_one * axis_three - real_part * axis_two), 2.0 * (axis_two * axis_three + real_part * axis_one), 1.0 - 2.0 * (axis_one * axis_one + axis_two * axis_two)]
    return jnp.stack(entries, axis=0)

def rotate(rotation, points):
    output_rows = []
    for target in range(3):
        summed = rotation[target * 3][:, None] * points[:, 0] + rotation[target * 3 + 1][:, None] * points[:, 1] + rotation[target * 3 + 2][:, None] * points[:, 2]
        output_rows.append(summed)
    return jnp.stack(output_rows, axis=1)

def rotate_back(rotation, points):
    output_rows = []
    for target in range(3):
        summed = rotation[target][:, None] * points[:, 0] + rotation[3 + target][:, None] * points[:, 1] + rotation[6 + target][:, None] * points[:, 2]
        output_rows.append(summed)
    return jnp.stack(output_rows, axis=1)

def compose(rotation, step_rotation):
    entries = []
    for target in range(3):
        for column in range(3):
            entries.append(rotation[target * 3] * step_rotation[column] + rotation[target * 3 + 1] * step_rotation[3 + column] + rotation[target * 3 + 2] * step_rotation[6 + column])
    return jnp.stack(entries, axis=0)

def project_single(single_state, rotation, translation, qkv_weight):
    row_count = single_state.shape[0]
    projected = jnp.dot(single_state.astype(jnp.bfloat16), qkv_weight, preferred_element_type=jnp.float32)
    head_width = H * CHEAD
    queries = projected[:, :head_width].reshape(row_count, H, CHEAD)
    key_part = projected[:, head_width:3 * head_width]
    point_start = 3 * head_width
    query_local = projected[:, point_start:point_start + 3 * H * PQ].reshape(row_count, 3, H * PQ)
    key_local = projected[:, point_start + 3 * H * PQ:point_start + 6 * H * PQ].reshape(row_count, 3, H * PQ)
    value_local = projected[:, point_start + 6 * H * PQ:].reshape(row_count, 3, H * PV)
    offset_global = translation.T[:, :, None]
    query_global = rotate(rotation, query_local) + offset_global
    key_global = rotate(rotation, key_local) + offset_global
    value_global = rotate(rotation, value_local) + offset_global
    key_rows = jnp.concatenate([key_part, key_global.reshape(row_count, -1), value_global.reshape(row_count, -1)], axis=1)
    return (queries, query_global, key_rows)

def attend(queries, query_global, rotation_own, translate_own, pair_bias, pair_half, chain_own, key_rows, mask_all, chain_all, head_gamma, chain_bias):
    row_count = queries.shape[0]
    head_width = H * CHEAD
    key_heads = key_rows[:, :head_width].reshape(-1, H, CHEAD)
    values_all = key_rows[:, head_width:2 * head_width].reshape(-1, H, CHEAD)
    point_start = 2 * head_width
    key_global = key_rows[:, point_start:point_start + 3 * H * PQ].reshape(-1, 3, H, PQ)
    value_global = key_rows[:, point_start + 3 * H * PQ:].reshape(-1, 3, H, PV)
    query_points = query_global.reshape(row_count, 3, H, PQ)
    scalar_dots = jnp.einsum('ihc,jhc->hij', queries, key_heads, precision=highest) / math.sqrt(CHEAD)
    difference = query_points[:, None] - key_global[None, :]
    distance = jnp.transpose(lax.optimization_barrier(jnp.sum(difference * difference, axis=(2, 4))), (2, 0, 1))
    point_weight = head_gamma * (math.sqrt(2.0 / (9.0 * PQ)) * 0.5)
    same_chain = chain_own[:, None] == chain_all[None, :]
    chain_term = jnp.where(same_chain[None], chain_bias[1][:, None, None], chain_bias[0][:, None, None])
    logits = math.sqrt(1.0 / 3.0) * (scalar_dots + jnp.transpose(pair_bias, (2, 0, 1)) - point_weight[:, None, None] * distance)
    logits = logits + chain_term + mask_fill * (mask_all - 1.0)[None, None, :]
    attention = jax.nn.softmax(logits, axis=-1)
    out_scalar = jnp.einsum('hij,jhc->ihc', attention, values_all, precision=highest)
    out_global = jnp.einsum('hij,jahv->iahv', attention, value_global, precision=highest)
    relative = out_global - translate_own.T[:, :, None, None]
    out_local = rotate_back(rotation_own, relative.reshape(row_count, 3, H * PV))
    out_norm = jnp.sqrt(lax.optimization_barrier(jnp.sum(out_local * out_local, axis=1)) + 1e-08)
    attention_half = lax.optimization_barrier(attention.astype(jnp.bfloat16)).astype(jnp.float32)
    pair_wide = lax.optimization_barrier(pair_half).astype(jnp.float32)
    out_pair = jnp.einsum('hij,ijc->ihc', attention_half, pair_wide, precision=highest)
    return jnp.concatenate([out_scalar.reshape(row_count, -1), out_local.reshape(row_count, -1), out_norm, out_pair.reshape(row_count, -1)], axis=1)

def reference(pair, single, quats, translate, res_mask, chain_ids, tri_weight, tri_out_weight, qkv_weight, bias_weight, head_gamma, chain_bias, out_weight, frame_weight):
    mask_float = res_mask.astype(jnp.float32)

    def row_inputs(inputs):
        row_pair, row_mask = inputs
        normed = layer_norm(row_pair).astype(jnp.bfloat16)
        projected = jnp.dot(normed, tri_weight, preferred_element_type=jnp.float32)
        pair_mask = (row_mask * mask_float)[:, None]
        left_side = (jax.nn.sigmoid(projected[:, :CH]) * projected[:, CH:2 * CH] * pair_mask).astype(jnp.bfloat16)
        right_side = (jax.nn.sigmoid(projected[:, 2 * CH:3 * CH]) * projected[:, 3 * CH:4 * CH] * pair_mask).astype(jnp.bfloat16)
        out_gate = jax.nn.sigmoid(projected[:, 4 * CH:])
        return (left_side, right_side, out_gate)
    left_side, right_side, out_gate = lax.map(row_inputs, (pair, mask_float))

    def channel_dot(pieces):
        return jnp.dot(pieces[0], pieces[1].T, preferred_element_type=jnp.float32)
    product = lax.map(channel_dot, (jnp.moveaxis(left_side, 2, 0), jnp.moveaxis(right_side, 2, 0)))
    product = jnp.moveaxis(product, 0, 2)

    def row_output(inputs):
        row_product, row_gate, row_pair = inputs
        update = jnp.dot(layer_norm(row_product).astype(jnp.bfloat16), tri_out_weight, preferred_element_type=jnp.float32)
        return row_pair + row_gate * update
    pair_out = lax.map(row_output, (product, out_gate, pair))
    normed_pair = layer_norm(pair_out)
    pair_bias = jnp.dot(normed_pair, bias_weight, precision=highest, preferred_element_type=jnp.float32)
    pair_half = normed_pair.astype(jnp.bfloat16)
    single_state = single
    rotation = quat_rotation(quats)
    translation = translate
    for iteration in range(ITERS):
        queries, query_global, key_rows = project_single(single_state, rotation, translation, qkv_weight)
        blocked = (queries.reshape(N_ROW, RES_DEV, H, CHEAD), query_global.reshape(N_ROW, RES_DEV, 3, H * PQ), jnp.transpose(rotation.reshape(9, N_ROW, RES_DEV), (1, 0, 2)), jnp.transpose(translation.reshape(3, N_ROW, RES_DEV), (1, 0, 2)), pair_bias.reshape(N_ROW, RES_DEV, NRES, H), pair_half.reshape(N_ROW, RES_DEV, NRES, CZ), chain_ids.reshape(N_ROW, RES_DEV))

        def block_attend(inputs):
            return attend(inputs[0], inputs[1], inputs[2], inputs[3], inputs[4], inputs[5], inputs[6], key_rows, mask_float, chain_ids, head_gamma, chain_bias)
        gathered = lax.map(block_attend, blocked).reshape(NRES, -1)
        update = jnp.dot(gathered.astype(jnp.bfloat16), out_weight, preferred_element_type=jnp.float32)
        single_state = layer_norm(single_state + update)
        frame_update = jnp.dot(single_state, frame_weight, precision=highest, preferred_element_type=jnp.float32)
        shift_step = rotate(rotation, frame_update[:, 3:][:, :, None])[:, :, 0].T
        translation = translation + shift_step
        rotation = compose(rotation, quat_rotation(frame_update[:, :3].T))
    return (pair_out, single_state, rotation, translation)
```

```python
import functools
import math

import jax
import jax.numpy as jnp
from jax import lax
from jax.experimental import pallas as pl
from jax.experimental.pallas import tpu as pltpu
from jax.sharding import PartitionSpec as P

CH = 128
CS = 384
H = 12
HP = 16
CHEAD = 16
PQ = 4
PV = 8
SLOT = 512
IP = 8
MASK_AT = 12
CHAIN_AT = 13

f32 = jnp.float32
bf16 = jnp.bfloat16
highest = lax.Precision.HIGHEST
epsilon = 1e-05
mask_fill = 100000.0
third = math.sqrt(1.0 / 3.0)


def layer_norm(values, axis=-1):
    center = values - jnp.mean(values, axis=axis, keepdims=True)
    spread = jnp.mean(center * center, axis=axis, keepdims=True)
    return center * lax.rsqrt(spread + epsilon)


def quat_entries(one, two, three, real):
    return [
        1.0 - 2.0 * (two * two + three * three),
        2.0 * (one * two - real * three),
        2.0 * (one * three + real * two),
        2.0 * (one * two + real * three),
        1.0 - 2.0 * (one * one + three * three),
        2.0 * (two * three - real * one),
        2.0 * (one * three - real * two),
        2.0 * (two * three + real * one),
        1.0 - 2.0 * (one * one + two * two),
    ]


def dot(a, b, precision=None):
    return lax.dot_general(
        a, b, (((1,), (0,)), ((), ())), precision=precision, preferred_element_type=f32
    )


def dot_nt(a, b, precision=None):
    return lax.dot_general(
        a, b, (((1,), (1,)), ((), ())), precision=precision, preferred_element_type=f32
    )


def dot_tn(a, b):
    return lax.dot_general(a, b, (((0,), (0,)), ((), ())), preferred_element_type=f32)


def log2(number):
    assert number & (number - 1) == 0
    return number.bit_length() - 1


def grid_of(shape):
    return lax.broadcasted_iota(jnp.int32, shape, 0), lax.broadcasted_iota(jnp.int32, shape, 1)


def onehot(match):
    return jnp.where(match, 1.0, 0.0).astype(bf16)


def swap_rows(count, minor_count):
    row, column = grid_of((count, count))
    major_count = count // minor_count
    minor = row >> log2(major_count)
    major = row & (major_count - 1)
    return onehot(column == major * minor_count + minor)


def spread_rows(slots, w, r):
    rows = 2 * w
    lanes = r * SLOT // rows
    x, i = grid_of((16, 16))
    q = x & (rows - 1)
    if lanes <= SLOT:
        total = None
        for t in range(SLOT // lanes):
            one = dot(onehot((q == t * r + i) & (i < r)), slots[:, t * lanes : (t + 1) * lanes])
            total = one if total is None else total + one
        return total.astype(bf16)
    return jnp.concatenate(
        [dot(onehot(i == t * rows + q), slots) for t in range(lanes // SLOT)], axis=1
    ).astype(bf16)


def natural_rows(x_ref, first, w, r, n, start=0, stop=SLOT):
    rows = 2 * w
    lanes = r * SLOT // rows
    count = n * r
    j, x = grid_of((count, n * rows))
    s = x >> log2(rows)
    q = x & (rows - 1)
    if lanes <= SLOT:
        pieces = []
        for t in range(SLOT // lanes):
            low, high = max(start, t * lanes), min(stop, (t + 1) * lanes)
            if low < high:
                values = x_ref[:, first + low - t * lanes : first + high - t * lanes]
                pieces.append(dot(onehot((j == s * r + q - t * r) & ((q >> log2(r)) == t)), values))
        return (pieces[0] if len(pieces) == 1 else jnp.concatenate(pieces, axis=1)).astype(bf16)
    total = None
    for t in range(lanes // SLOT):
        values = x_ref[:, first + t * SLOT + start : first + t * SLOT + stop]
        one = dot(onehot(j == s * r + t * rows + q), values)
        total = one if total is None else total + one
    return total.astype(bf16)


def frame_pieces(frame):
    high = frame.astype(bf16).astype(f32)
    rest = frame - high
    middle = rest.astype(bf16).astype(f32)
    low = (rest - middle).astype(bf16).astype(f32)
    return high + pltpu.roll(middle, 32, 1) + pltpu.roll(low, 64, 1)


def slots_of(state, frame):
    both = jnp.concatenate([state, frame_pieces(frame)], axis=1)
    return jnp.concatenate([both, jnp.zeros_like(both)], axis=0).astype(bf16)


def fill_rows(out_ref, first, tile):
    lanes = tile.shape[1]
    for t in range(out_ref.shape[0] // 16):
        out_ref[t * 16 : (t + 1) * 16, first : first + lanes] = tile


def piece_select(row_count, transposed=False):
    if transposed:
        lane, entry = grid_of((128, row_count))
    else:
        entry, lane = grid_of((row_count, 128))
    return onehot(((lane & 31) == entry) & (lane < 96))


def gate_kernel(
    w, n, pair_ref, tri_ref, single_ref, quats_ref, translate_ref, mask_ref, chain_ref, send_ref, frame_ref, scr
):
    r, count, _ = pair_ref.shape
    scr[...] = jnp.zeros_like(scr)
    quats = quats_ref[...]
    real = lax.rsqrt(1.0 + jnp.sum(quats * quats, axis=0, keepdims=True))
    unit = quats * real
    entries = quat_entries(unit[0:1], unit[1:2], unit[2:3], real)
    for at, entry in enumerate(entries):
        scr[at : at + 1, 0:r] = entry
    scr[9:12, 0:r] = translate_ref[...]
    frame = scr[...].T[0:IP, :]
    row, lane = grid_of((IP, 128))
    for i in range(r):
        frame = jnp.where((row == i) & (lane == MASK_AT), mask_ref[i].astype(f32), frame)
        frame = jnp.where((row == i) & (lane == CHAIN_AT), chain_ref[i].astype(f32), frame)
    frame_ref[...] = frame
    state = jnp.concatenate([single_ref[...], jnp.zeros((IP - r, CS), f32)], axis=0)
    fill_rows(send_ref, r * count, spread_rows(slots_of(state, frame), w, r))

    row, column = grid_of((2 * CH, 2 * CH))
    d = row >> log2(2 * w)
    side = (row >> log2(w)) & 1
    take = onehot(column == side * CH + d * w + (row & (w - 1)))
    gate_weight = jnp.concatenate([tri_ref[:, 0:CH], tri_ref[:, 2 * CH : 3 * CH]], axis=1)
    value_weight = jnp.concatenate([tri_ref[:, CH : 2 * CH], tri_ref[:, 3 * CH : 4 * CH]], axis=1)
    gate_weight = dot_nt(take, gate_weight).astype(bf16)
    value_weight = dot_nt(take, value_weight).astype(bf16)
    for i in range(r):
        normed = layer_norm(pair_ref[i]).astype(bf16)
        gates = dot_nt(gate_weight, normed)
        values = dot_nt(value_weight, normed)
        side_values = jax.nn.sigmoid(gates) * values * mask_ref[i].astype(f32)
        send_ref[:, i * count : (i + 1) * count] = side_values.astype(bf16)


def product_kernel(w, n, r, recv_ref, send_ref):
    count = n * r
    rows = 2 * w
    pieces = natural_rows(recv_ref, r * count, w, r, n, CS, SLOT)
    mask = dot_nt(piece_select(16), pieces)[MASK_AT : MASK_AT + 1, :]
    mask = jnp.concatenate([mask] * r, axis=1)
    order = swap_rows(n * rows, rows)
    sides = (dot(order, recv_ref[:, 0 : r * count]) * mask).astype(bf16)
    row, column = grid_of((count, count))
    to_natural = onehot(row == (column & (n - 1)) * r + (column >> log2(n)))

    def stacked(block):
        part = sides[block * n : (block + 1) * n]
        return jnp.concatenate([part[:, i * count : (i + 1) * count] for i in range(r)], axis=0)

    half = r // 2
    products = []
    for c in range(w):
        right = dot(to_natural, stacked(w + c)).astype(bf16)
        products.append(dot_nt(stacked(c), right).astype(bf16))
    blocks = []
    for high in range(2):
        for c in range(w):
            first = high * half
            blocks.append(
                jnp.concatenate(
                    [products[c][(first + low) * n : (first + low + 1) * n] for low in range(half)], axis=1
                )
            )
    send_ref[...] = dot(swap_rows(n * rows, n), jnp.concatenate(blocks, axis=0)).astype(bf16)


def head_masks():
    h, lane = grid_of((HP, 256))
    scalar = jnp.where((lane >> log2(CHEAD)) == h, 1.0, 0.0)
    scalar = jnp.where(h < H, scalar, 0.0)
    h, lane = grid_of((HP, 128))
    query = jnp.where(((lane >> log2(PQ)) == h) & (h < H), 1.0, 0.0)
    value = jnp.where(((lane >> log2(PV)) == h) & (h < H), 1.0, 0.0)
    return scalar, query, value


def logits_and_values(r, slots, state, frame, chain_ref, key_weight, query_weight, columns):
    pieces = slots[:, CS:SLOT]
    entry = dot(pieces, piece_select(128, True))
    rows = dot_nt(piece_select(16), pieces)
    keys = dot(slots[:, 0:CS], key_weight)
    local = [keys[:, 512 + 256 * a : 768 + 256 * a] for a in range(3)]
    placed = []
    for a in range(3):
        placed.append(
            entry[:, 3 * a : 3 * a + 1] * local[0]
            + entry[:, 3 * a + 1 : 3 * a + 2] * local[1]
            + entry[:, 3 * a + 2 : 3 * a + 3] * local[2]
            + entry[:, 9 + a : 10 + a]
        )
    values = jnp.concatenate([keys[:, 256:512]] + [p[:, 0:128] for p in placed], axis=1)
    key_points = [p[:, 128:256] for p in placed]
    key_side = jnp.concatenate([keys[:, 0:256]] + key_points + [p * p for p in key_points], axis=1)

    both = jnp.concatenate([state, jnp.zeros_like(state)], axis=0).astype(bf16)
    own = dot(both, query_weight)[0:IP]
    own_local = [own[:, 256 + 128 * a : 384 + 128 * a] for a in range(3)]
    own_points = []
    for a in range(3):
        own_points.append(
            frame[:, 3 * a : 3 * a + 1] * own_local[0]
            + frame[:, 3 * a + 1 : 3 * a + 2] * own_local[1]
            + frame[:, 3 * a + 2 : 3 * a + 3] * own_local[2]
            + frame[:, 9 + a : 10 + a]
        )
    scalar_mask, query_mask, _ = head_masks()
    weight = columns[:, 0:1]
    query_rows = []
    constants = []
    for i in range(r):
        scalar = own[i : i + 1, 0:256] * (third / math.sqrt(CHEAD)) * scalar_mask
        points = [p[i : i + 1] * query_mask for p in own_points]
        query_rows.append(
            jnp.concatenate(
                [scalar] + [2.0 * weight * p for p in points] + [-weight * query_mask] * 3, axis=1
            )
        )
        length = points[0] * points[0] + points[1] * points[1] + points[2] * points[2]
        own_chain = chain_ref[i].astype(f32)
        same = rows[CHAIN_AT : CHAIN_AT + 1, :] == own_chain
        constants.append(
            jnp.where(same, columns[:, 2:3], columns[:, 1:2])
            + mask_fill * (rows[MASK_AT : MASK_AT + 1, :] - 1.0)
            - weight * jnp.sum(length, axis=1, keepdims=True)
        )
    logits = dot_nt(jnp.concatenate(query_rows, axis=0), key_side, highest)
    return logits + jnp.concatenate(constants, axis=0), values


def attend(r, logits, values, pair_half, state, frame, out_weight, frame_weight):
    top = jnp.max(logits, axis=1, keepdims=True)
    raised = jnp.exp(logits - top)
    attention = raised / jnp.sum(raised, axis=1, keepdims=True)
    summed = dot(attention, values, highest)
    scalar_mask, _, value_mask = head_masks()
    masks = jnp.concatenate([scalar_mask, value_mask, value_mask, value_mask], axis=1)
    summed = summed * jnp.concatenate([masks] * r, axis=0)
    row, column = grid_of((IP, r * HP))
    gathered = dot(jnp.where((column >> log2(HP)) == row, 1.0, 0.0), summed, highest)
    relative = [
        gathered[:, 256 + 128 * a : 256 + 128 * a + H * PV] - frame[:, 9 + a : 10 + a] for a in range(3)
    ]
    out_local = [
        frame[:, a : a + 1] * relative[0]
        + frame[:, 3 + a : 4 + a] * relative[1]
        + frame[:, 6 + a : 7 + a] * relative[2]
        for a in range(3)
    ]
    out_norm = jnp.sqrt(
        out_local[0] * out_local[0] + out_local[1] * out_local[1] + out_local[2] * out_local[2] + 1e-08
    )
    half = attention.astype(bf16)
    out_pair = jnp.concatenate(
        [dot(half[i * HP : (i + 1) * HP], pair_half[i]) for i in range(r)], axis=0
    ).astype(bf16)
    row, column = grid_of((H * IP, r * HP))
    by_head = dot(onehot(column == (row & (IP - 1)) * HP + (row >> log2(IP))), out_pair)
    combined = jnp.concatenate(
        [gathered[:, 0 : H * CHEAD]]
        + out_local
        + [out_norm]
        + [by_head[h * IP : (h + 1) * IP] for h in range(H)],
        axis=1,
    )
    combined = jnp.concatenate([combined, jnp.zeros_like(combined)], axis=0).astype(bf16)
    state = layer_norm(state + dot(combined, out_weight)[0:IP])
    update = dot(state, frame_weight, highest)
    quat = [update[:, a : a + 1] for a in range(3)]
    real = lax.rsqrt(1.0 + (quat[0] * quat[0] + quat[1] * quat[1] + quat[2] * quat[2]))
    step = quat_entries(quat[0] * real, quat[1] * real, quat[2] * real, real)
    old = [frame[:, e : e + 1] for e in range(9)]
    columns = []
    for target in range(3):
        for column in range(3):
            columns.append(
                old[target * 3] * step[column]
                + old[target * 3 + 1] * step[3 + column]
                + old[target * 3 + 2] * step[6 + column]
            )
    for target in range(3):
        columns.append(
            frame[:, 9 + target : 10 + target]
            + old[target * 3] * update[:, 3:4]
            + old[target * 3 + 1] * update[:, 4:5]
            + old[target * 3 + 2] * update[:, 5:6]
        )
    _, lane = grid_of((IP, 128))
    for at, column in enumerate(columns):
        frame = jnp.where(lane == at, column, frame)
    return state, frame


def pad_state(single_ref):
    r = single_ref.shape[0]
    return jnp.concatenate([single_ref[...], jnp.zeros((IP - r, CS), f32)], axis=0)


def prepare_kernel(
    w, n, recv_ref, pair_ref, gate_weight_ref, single_ref, frame_ref, chain_ref, key_ref, query_ref, columns_ref,
    gate_ref, logits_ref, values_ref,
):
    r, count, _ = pair_ref.shape
    slots = natural_rows(recv_ref, r * count, w, r, n)
    logits, values = logits_and_values(
        r, slots, pad_state(single_ref), frame_ref[...], chain_ref, key_ref[...], query_ref[...], columns_ref[...]
    )
    logits_ref[...] = logits
    values_ref[...] = values
    for i in range(r):
        normed = layer_norm(pair_ref[i]).astype(bf16)
        gate_ref[i] = jax.nn.sigmoid(dot(normed, gate_weight_ref[...]))


def update_kernel(
    w, n, recv_ref, pair_ref, gate_ref, logits_ref, values_ref, tri_out_ref, bias_weight_ref, single_ref, frame_ref,
    out_weight_ref, frame_weight_ref, pair_out_ref, half_ref, bias_ref, state_ref, new_frame_ref, send_ref,
):
    r, count, _ = pair_ref.shape
    half = r // 2
    row, column = grid_of((2 * CH, 2 * CH))
    c = row & (CH - 1)
    take = onehot(column == (c >> log2(w)) * 2 * w + (row >> log2(CH)) * w + (c & (w - 1)))
    product = dot(take, recv_ref[...])
    biases = []
    halves = []
    for high in range(2):
        normed = layer_norm(product[high * CH : (high + 1) * CH], axis=0).astype(bf16)
        update = dot_tn(normed, tri_out_ref[...])
        for low in range(half):
            i = high * half + low
            pair_out = pair_ref[i] + gate_ref[i] * update[low * count : (low + 1) * count]
            pair_out_ref[i] = pair_out
            normed_pair = layer_norm(pair_out)
            biases.append(dot_nt(bias_weight_ref[...], normed_pair, highest) * third)
            halves.append(normed_pair.astype(bf16))
            half_ref[i] = halves[-1]
    bias = jnp.concatenate(biases, axis=0)
    bias_ref[...] = bias
    state, frame = attend(
        r, logits_ref[...] + bias, values_ref[...], halves, pad_state(single_ref), frame_ref[...],
        out_weight_ref[...], frame_weight_ref[...],
    )
    state_ref[...] = state
    new_frame_ref[...] = frame
    fill_rows(send_ref, 0, spread_rows(slots_of(state, frame), w, r))


def last_kernel(
    w, n, recv_ref, half_ref, bias_ref, state_ref, frame_ref, chain_ref, key_ref, query_ref, columns_ref,
    out_weight_ref, frame_weight_ref, single_out_ref, rotation_ref, translation_ref, scr,
):
    r = half_ref.shape[0]
    slots = natural_rows(recv_ref, 0, w, r, n)
    state, frame = state_ref[...], frame_ref[...]
    logits, values = logits_and_values(
        r, slots, state, frame, chain_ref, key_ref[...], query_ref[...], columns_ref[...]
    )
    state, frame = attend(
        r, logits + bias_ref[...], values, [half_ref[i] for i in range(r)], state, frame,
        out_weight_ref[...], frame_weight_ref[...],
    )
    single_out_ref[...] = state[0:r]
    scr[...] = jnp.concatenate([frame, jnp.zeros((128 - IP, 128), f32)], axis=0).T
    rotation_ref[...] = scr[0:9, 0:r]
    translation_ref[...] = scr[9:12, 0:r]


VMEM = pl.BlockSpec(memory_space=pltpu.VMEM)
SMEM = pl.BlockSpec(memory_space=pltpu.SMEM)


def call(body, name, outs, args, small=(), scratch=(), limit=32, flops=0, moved=0):
    return pl.pallas_call(
        body,
        name=name,
        out_shape=[jax.ShapeDtypeStruct(s, d) for s, d in outs],
        in_specs=[SMEM if at in small else VMEM for at in range(len(args))],
        out_specs=[VMEM] * len(outs),
        scratch_shapes=list(scratch),
        compiler_params=pltpu.CompilerParams(vmem_limit_bytes=limit * 2**20),
        cost_estimate=pl.CostEstimate(flops=flops, bytes_accessed=moved, transcendentals=0),
    )(*args)


def pad_lanes(block, width):
    return jnp.pad(block, ((0, 0), (0, width - block.shape[1])))


def local(
    pair, single, quats, translate, res_mask, chain_ids, tri_weight, tri_out_weight, qkv_weight, bias_weight,
    head_gamma, chain_bias, out_weight, frame_weight,
):
    n = lax.axis_size("row")
    r, count, _ = pair.shape
    w = CH // n
    rows = 2 * w
    lanes = r * SLOT // rows
    scale = count // 128
    limit = 24 if scale == 1 else 56

    def exchange(sent):
        width = sent.shape[1]
        got = lax.all_to_all(sent.reshape(n, rows, width), "row", 0, 0, tiled=True)
        return got.reshape(n * rows, width)

    sent, frame = call(
        functools.partial(gate_kernel, w, n),
        "gate",
        [((n * rows, r * count + lanes), bf16), ((IP, 128), f32)],
        [pair, tri_weight, single, quats, translate, res_mask, chain_ids],
        small=(5, 6),
        scratch=[pltpu.VMEM((128, 128), f32)],
        limit=limit,
    )
    received = exchange(sent)

    width = H * CHEAD
    start = 3 * width
    query_points = qkv_weight[:, start : start + 3 * H * PQ]
    key_points = qkv_weight[:, start + 3 * H * PQ : start + 6 * H * PQ]
    value_points = qkv_weight[:, start + 6 * H * PQ :]
    key_weight = [pad_lanes(qkv_weight[:, width : 2 * width], 256), pad_lanes(qkv_weight[:, 2 * width : start], 256)]
    query_weight = [pad_lanes(qkv_weight[:, :width], 256)]
    for a in range(3):
        key_weight.append(pad_lanes(value_points[:, a * H * PV : (a + 1) * H * PV], 128))
        key_weight.append(pad_lanes(key_points[:, a * H * PQ : (a + 1) * H * PQ], 128))
        query_weight.append(pad_lanes(query_points[:, a * H * PQ : (a + 1) * H * PQ], 128))
    key_weight = jnp.concatenate(key_weight, axis=1)
    query_weight = jnp.concatenate(query_weight, axis=1)
    point_weight = head_gamma * (math.sqrt(2.0 / (9.0 * PQ)) * 0.5 * third)
    columns = jnp.stack([point_weight, chain_bias[0], chain_bias[1]], axis=1)
    columns = jnp.pad(columns, ((0, HP - H), (0, 125)))
    bias_rows = jnp.pad(bias_weight.T, ((0, HP - H), (0, 0)))
    gate_weight = tri_weight[:, 4 * CH :]

    (formed,) = call(
        functools.partial(product_kernel, w, n, r),
        "product",
        [((n * rows, (r // 2) * count), bf16)],
        [received],
        limit=limit,
    )
    products = exchange(formed)
    gate, logits, values = call(
        functools.partial(prepare_kernel, w, n),
        "prepare",
        [((r, count, CH), f32), ((r * HP, count), f32), ((count, 640), f32)],
        [received, pair, gate_weight, single, frame, chain_ids, key_weight, query_weight, columns],
        small=(5,),
        limit=limit,
        flops=2 * count * CS * 1280,
        moved=8 * 2**20,
    )
    pair_out, pair_half, bias, state, frame, sent = call(
        functools.partial(update_kernel, w, n),
        "update",
        [
            ((r, count, CH), f32),
            ((r, count, CH), bf16),
            ((r * HP, count), f32),
            ((IP, CS), f32),
            ((IP, 128), f32),
            ((n * rows, lanes), bf16),
        ],
        [products, pair, gate, logits, values, tri_out_weight, bias_rows, single, frame, out_weight, frame_weight],
        limit=limit,
    )
    received = exchange(sent)
    single_out, rotation, translation = call(
        functools.partial(last_kernel, w, n),
        "last",
        [((r, CS), f32), ((9, r), f32), ((3, r), f32)],
        [received, pair_half, bias, state, frame, chain_ids, key_weight, query_weight, columns, out_weight, frame_weight],
        small=(5,),
        scratch=[pltpu.VMEM((128, 128), f32)],
        limit=limit,
    )
    return (pair_out, single_out, rotation, translation)


def solution(mesh):
    rows = ("grp", "row")
    placed = (P(rows, None, None), P(rows, None), P(None, rows), P(None, rows), P(rows), P(rows)) + (P(),) * 8
    return jax.shard_map(
        local,
        mesh=mesh,
        in_specs=placed,
        out_specs=(P(rows, None, None), P(rows, None), P(None, rows), P(None, rows)),
        check_vma=False,
    )
```

```python
import functools
import math

import jax
import jax.numpy as jnp
from jax import lax
from jax.experimental import pallas as pl
from jax.experimental.pallas import tpu as pltpu
from jax.sharding import PartitionSpec as P

CH = 128
CS = 384
H = 12
HP = 16
CHEAD = 16
PQ = 4
PV = 8
SLOT = 512
IP = 8
MASK_AT = 12
CHAIN_AT = 13

f32 = jnp.float32
bf16 = jnp.bfloat16
highest = lax.Precision.HIGHEST
epsilon = 1e-05
mask_fill = 100000.0
third = math.sqrt(1.0 / 3.0)


def layer_norm(values, axis=-1):
    center = values - jnp.mean(values, axis=axis, keepdims=True)
    spread = jnp.mean(center * center, axis=axis, keepdims=True)
    return center * lax.rsqrt(spread + epsilon)


def quat_entries(one, two, three, real):
    return [
        1.0 - 2.0 * (two * two + three * three),
        2.0 * (one * two - real * three),
        2.0 * (one * three + real * two),
        2.0 * (one * two + real * three),
        1.0 - 2.0 * (one * one + three * three),
        2.0 * (two * three - real * one),
        2.0 * (one * three - real * two),
        2.0 * (two * three + real * one),
        1.0 - 2.0 * (one * one + two * two),
    ]


def dot(a, b, precision=None):
    return lax.dot_general(
        a, b, (((1,), (0,)), ((), ())), precision=precision, preferred_element_type=f32
    )


def dot_nt(a, b, precision=None):
    return lax.dot_general(
        a, b, (((1,), (1,)), ((), ())), precision=precision, preferred_element_type=f32
    )


def dot_tn(a, b):
    return lax.dot_general(a, b, (((0,), (0,)), ((), ())), preferred_element_type=f32)


def log2(number):
    assert number & (number - 1) == 0
    return number.bit_length() - 1


def grid_of(shape):
    return lax.broadcasted_iota(jnp.int32, shape, 0), lax.broadcasted_iota(jnp.int32, shape, 1)


def onehot(match):
    return jnp.where(match, 1.0, 0.0).astype(bf16)


def swap_rows(count, minor_count):
    row, column = grid_of((count, count))
    major_count = count // minor_count
    minor = row >> log2(major_count)
    major = row & (major_count - 1)
    return onehot(column == major * minor_count + minor)


def spread_rows(slots, w, r):
    rows = 2 * w
    lanes = r * SLOT // rows
    x, i = grid_of((16, 16))
    q = x & (rows - 1)
    if lanes <= SLOT:
        total = None
        for t in range(SLOT // lanes):
            one = dot(onehot((q == t * r + i) & (i < r)), slots[:, t * lanes : (t + 1) * lanes])
            total = one if total is None else total + one
        return total.astype(bf16)
    return jnp.concatenate(
        [dot(onehot(i == t * rows + q), slots) for t in range(lanes // SLOT)], axis=1
    ).astype(bf16)


def natural_rows(x_ref, first, w, r, n, start=0, stop=SLOT):
    rows = 2 * w
    lanes = r * SLOT // rows
    count = n * r
    j, x = grid_of((count, n * rows))
    s = x >> log2(rows)
    q = x & (rows - 1)
    if lanes <= SLOT:
        pieces = []
        for t in range(SLOT // lanes):
            low, high = max(start, t * lanes), min(stop, (t + 1) * lanes)
            if low < high:
                values = x_ref[:, first + low - t * lanes : first + high - t * lanes]
                pieces.append(dot(onehot((j == s * r + q - t * r) & ((q >> log2(r)) == t)), values))
        return (pieces[0] if len(pieces) == 1 else jnp.concatenate(pieces, axis=1)).astype(bf16)
    total = None
    for t in range(lanes // SLOT):
        values = x_ref[:, first + t * SLOT + start : first + t * SLOT + stop]
        one = dot(onehot(j == s * r + t * rows + q), values)
        total = one if total is None else total + one
    return total.astype(bf16)


def frame_pieces(frame):
    high = frame.astype(bf16).astype(f32)
    rest = frame - high
    middle = rest.astype(bf16).astype(f32)
    low = (rest - middle).astype(bf16).astype(f32)
    return high + pltpu.roll(middle, 32, 1) + pltpu.roll(low, 64, 1)


def slots_of(state, frame):
    both = jnp.concatenate([state, frame_pieces(frame)], axis=1)
    return jnp.concatenate([both, jnp.zeros_like(both)], axis=0).astype(bf16)


def fill_rows(out_ref, first, tile):
    lanes = tile.shape[1]
    for t in range(out_ref.shape[0] // 16):
        out_ref[t * 16 : (t + 1) * 16, first : first + lanes] = tile


def piece_select(row_count, transposed=False):
    if transposed:
        lane, entry = grid_of((128, row_count))
    else:
        entry, lane = grid_of((row_count, 128))
    return onehot(((lane & 31) == entry) & (lane < 96))


def copies(sems, *pairs):
    started = [pltpu.make_async_copy(src, dst, sems.at[at]) for at, (src, dst) in enumerate(pairs)]
    for copy in started:
        copy.start()
    return started


def gate_kernel(
    w, n, pair_any, tri_any, single_any, quats_any, translate_any, mask_any, chain_any, send_ref, frame_ref,
    pair_ref, tri_ref, single_ref, quats_ref, translate_ref, mask_ref, chain_ref, scr, sems,
):
    r, count, _ = pair_ref.shape
    big = copies(sems, (tri_any.at[:, 0 : 4 * CH], tri_ref), *((pair_any.at[i], pair_ref.at[i]) for i in range(r)))
    little = copies(
        sems.at[r + 1 :],
        (quats_any, quats_ref),
        (translate_any, translate_ref),
        (mask_any, mask_ref),
        (chain_any, chain_ref),
        (single_any, single_ref),
    )
    row, column = grid_of((2 * CH, 2 * CH))
    d = row >> log2(2 * w)
    side = (row >> log2(w)) & 1
    take = onehot(column == side * CH + d * w + (row & (w - 1)))
    big[0].wait()
    gate_weight = jnp.concatenate([tri_ref[:, 0:CH], tri_ref[:, 2 * CH : 3 * CH]], axis=1)
    value_weight = jnp.concatenate([tri_ref[:, CH : 2 * CH], tri_ref[:, 3 * CH : 4 * CH]], axis=1)
    gate_weight = dot_nt(take, gate_weight).astype(bf16)
    value_weight = dot_nt(take, value_weight).astype(bf16)
    for copy in little:
        copy.wait()
    for i in range(r):
        big[1 + i].wait()
        normed = layer_norm(pair_ref[i]).astype(bf16)
        gates = dot_nt(gate_weight, normed)
        values = dot_nt(value_weight, normed)
        side_values = jax.nn.sigmoid(gates) * values * mask_ref[i].astype(f32)
        send_ref[:, i * count : (i + 1) * count] = side_values.astype(bf16)

    scr[...] = jnp.zeros_like(scr)
    quats = quats_ref[...]
    real = lax.rsqrt(1.0 + jnp.sum(quats * quats, axis=0, keepdims=True))
    unit = quats * real
    entries = quat_entries(unit[0:1], unit[1:2], unit[2:3], real)
    for at, entry in enumerate(entries):
        scr[at : at + 1, 0:r] = entry
    scr[9:12, 0:r] = translate_ref[...]
    frame = scr[...].T[0:IP, :]
    row, lane = grid_of((IP, 128))
    for i in range(r):
        frame = jnp.where((row == i) & (lane == MASK_AT), mask_ref[i].astype(f32), frame)
        frame = jnp.where((row == i) & (lane == CHAIN_AT), chain_ref[i].astype(f32), frame)
    frame_ref[...] = frame
    fill_rows(send_ref, r * count, spread_rows(slots_of(pad_state(single_ref), frame), w, r))


def product_kernel(w, n, r, recv_ref, send_ref):
    count = n * r
    rows = 2 * w
    pieces = natural_rows(recv_ref, r * count, w, r, n, CS, SLOT)
    mask = dot_nt(piece_select(16), pieces)[MASK_AT : MASK_AT + 1, :]
    mask = jnp.concatenate([mask] * r, axis=1)
    order = swap_rows(n * rows, rows)
    sides = (dot(order, recv_ref[:, 0 : r * count]) * mask).astype(bf16)
    row, column = grid_of((count, count))
    to_natural = onehot(row == (column & (n - 1)) * r + (column >> log2(n)))

    def stacked(block):
        part = sides[block * n : (block + 1) * n]
        return jnp.concatenate([part[:, i * count : (i + 1) * count] for i in range(r)], axis=0)

    half = r // 2
    products = []
    for c in range(w):
        right = dot(to_natural, stacked(w + c)).astype(bf16)
        products.append(dot_nt(stacked(c), right).astype(bf16))
    blocks = []
    for high in range(2):
        for c in range(w):
            first = high * half
            blocks.append(
                jnp.concatenate(
                    [products[c][(first + low) * n : (first + low + 1) * n] for low in range(half)], axis=1
                )
            )
    send_ref[...] = dot(swap_rows(n * rows, n), jnp.concatenate(blocks, axis=0)).astype(bf16)


def head_masks():
    h, lane = grid_of((HP, 256))
    query_scalar = jnp.where(((lane >> log2(CHEAD)) == h) & (h < H), 1.0, 0.0)
    value_scalar = jnp.where((((lane - 64) >> log2(CHEAD)) == h) & (h < H), 1.0, 0.0)
    h, lane = grid_of((HP, 128))
    query = jnp.where(((lane >> log2(PQ)) == h) & (h < H), 1.0, 0.0)
    value = jnp.where(((lane >> log2(PV)) == h) & (h < H), 1.0, 0.0)
    return query_scalar, value_scalar, query, value


def own_side(r, state, frame, query_weight, columns):
    both = jnp.concatenate([state, jnp.zeros_like(state)], axis=0).astype(bf16)
    own = dot(both, query_weight)[0:IP]
    width = H * CHEAD
    points = H * PQ
    fill = jnp.zeros((IP, 128 - points), f32)
    own_local = [
        jnp.concatenate([own[:, width + a * points : width + (a + 1) * points], fill], axis=1) for a in range(3)
    ]
    own_points = []
    for a in range(3):
        own_points.append(
            frame[:, 3 * a : 3 * a + 1] * own_local[0]
            + frame[:, 3 * a + 1 : 3 * a + 2] * own_local[1]
            + frame[:, 3 * a + 2 : 3 * a + 3] * own_local[2]
            + frame[:, 9 + a : 10 + a]
        )
    query_scalar, _, query_mask, _ = head_masks()
    weight = columns[:, 0:1]
    query_rows = []
    lengths = []
    for i in range(r):
        scalar = own[i : i + 1, 0:256] * (third / math.sqrt(CHEAD)) * query_scalar
        points = [p[i : i + 1] * query_mask for p in own_points]
        query_rows.append(
            jnp.concatenate([scalar] + [2.0 * weight * p for p in points] + [-weight * query_mask], axis=1)
        )
        length = points[0] * points[0] + points[1] * points[1] + points[2] * points[2]
        lengths.append(-weight * jnp.sum(length, axis=1, keepdims=True))
    return jnp.concatenate(query_rows, axis=0), jnp.concatenate(lengths, axis=0)


def logits_and_values(r, slots, own, frame, key_weight, columns):
    query_rows, lengths = own
    pieces = slots[:, CS:SLOT]
    entry = dot(pieces, piece_select(128, True))
    rows = dot_nt(piece_select(16), pieces)
    keys = dot(slots[:, 0:CS], key_weight)
    local = [keys[:, 384 + 256 * a : 640 + 256 * a] for a in range(3)]
    placed = []
    for a in range(3):
        placed.append(
            entry[:, 3 * a : 3 * a + 1] * local[0]
            + entry[:, 3 * a + 1 : 3 * a + 2] * local[1]
            + entry[:, 3 * a + 2 : 3 * a + 3] * local[2]
            + entry[:, 9 + a : 10 + a]
        )
    values = jnp.concatenate([keys[:, 128:384]] + [p[:, 0:128] for p in placed], axis=1)
    key_points = [p[:, 128:256] for p in placed]
    length = key_points[0] * key_points[0] + key_points[1] * key_points[1] + key_points[2] * key_points[2]
    key_side = jnp.concatenate([keys[:, 0:256]] + key_points + [length], axis=1)
    far = mask_fill * (rows[MASK_AT : MASK_AT + 1, :] - 1.0)
    added = []
    for i in range(r):
        same = rows[CHAIN_AT : CHAIN_AT + 1, :] == frame[i : i + 1, CHAIN_AT : CHAIN_AT + 1]
        added.append(jnp.where(same, columns[:, 2:3], columns[:, 1:2]) + far + lengths[i * HP : (i + 1) * HP])
    logits = dot_nt(query_rows, key_side, highest)
    return logits + jnp.concatenate(added, axis=0), values


def attend(r, logits, values, pair_half, state, frame, weights):
    top = jnp.max(logits, axis=1, keepdims=True)
    raised = jnp.exp(logits - top)
    attention = raised / jnp.sum(raised, axis=1, keepdims=True)
    summed = dot(attention, values, highest)
    _, value_scalar, _, value_mask = head_masks()
    masks = jnp.concatenate([value_scalar, value_mask, value_mask, value_mask], axis=1)
    summed = summed * jnp.concatenate([masks] * r, axis=0)
    gathered = jnp.sum(summed.reshape(r, HP, 640), axis=1)
    gathered = jnp.concatenate([gathered, jnp.zeros((IP - r, 640), f32)], axis=0)
    relative = [
        gathered[:, 256 + 128 * a : 256 + 128 * a + H * PV] - frame[:, 9 + a : 10 + a] for a in range(3)
    ]
    out_local = [
        frame[:, a : a + 1] * relative[0]
        + frame[:, 3 + a : 4 + a] * relative[1]
        + frame[:, 6 + a : 7 + a] * relative[2]
        for a in range(3)
    ]
    out_norm = jnp.sqrt(
        out_local[0] * out_local[0] + out_local[1] * out_local[1] + out_local[2] * out_local[2] + 1e-08
    )
    half = attention.astype(bf16)
    out_pair = jnp.concatenate(
        [dot(half[i * HP : (i + 1) * HP], pair_half[i]) for i in range(r)], axis=0
    ).astype(bf16)
    row, column = grid_of((H * IP, r * HP))
    by_head = dot(onehot(column == (row & (IP - 1)) * HP + (row >> log2(IP))), out_pair)
    combined = jnp.concatenate(
        [gathered[:, 256 - H * CHEAD : 256]]
        + out_local
        + [out_norm]
        + [by_head[h * IP : (h + 1) * IP] for h in range(H)],
        axis=1,
    )
    combined = jnp.concatenate([combined, jnp.zeros_like(combined)], axis=0).astype(bf16)
    out_weight, frame_weight = weights()
    state = layer_norm(state + dot(combined, out_weight)[0:IP])
    update = dot_nt(state, frame_weight, highest)
    quat = [update[:, a : a + 1] for a in range(3)]
    real = lax.rsqrt(1.0 + (quat[0] * quat[0] + quat[1] * quat[1] + quat[2] * quat[2]))
    step = quat_entries(quat[0] * real, quat[1] * real, quat[2] * real, real)
    old = [frame[:, e : e + 1] for e in range(9)]
    columns = []
    for target in range(3):
        for column in range(3):
            columns.append(
                old[target * 3] * step[column]
                + old[target * 3 + 1] * step[3 + column]
                + old[target * 3 + 2] * step[6 + column]
            )
    for target in range(3):
        columns.append(
            frame[:, 9 + target : 10 + target]
            + old[target * 3] * update[:, 3:4]
            + old[target * 3 + 1] * update[:, 4:5]
            + old[target * 3 + 2] * update[:, 5:6]
        )
    _, lane = grid_of((IP, 128))
    for at, column in enumerate(columns):
        frame = jnp.where(lane == at, column, frame)
    return state, frame


def pad_state(single_ref):
    r = single_ref.shape[0]
    return jnp.concatenate([single_ref[...], jnp.zeros((IP - r, CS), f32)], axis=0)


def own_kernel(
    pair_any, tri_any, qkv_any, single_any, frame_any, columns_any,
    gate_ref, key_ref, query_ref, rows_ref, lengths_ref,
    pair_ref, gate_weight_ref, qkv_ref, single_ref, frame_ref, columns_ref, sems,
):
    r, count, _ = pair_ref.shape
    for copy in copies(
        sems,
        (pair_any, pair_ref),
        (tri_any.at[:, 4 * CH :], gate_weight_ref),
        (qkv_any, qkv_ref),
        (single_any, single_ref),
        (frame_any, frame_ref),
        (columns_any, columns_ref),
    ):
        copy.wait()
    width = H * CHEAD
    start = 3 * width
    points = H * PQ

    def padded(first, size, to):
        block = qkv_ref[:, first : first + size].astype(f32)
        return jnp.concatenate([block, jnp.zeros((CS, to - size), f32)], axis=1).astype(bf16)

    queries = [qkv_ref[:, 0:width], qkv_ref[:, start : start + 3 * points]]
    query_ref[...] = jnp.concatenate([q.astype(f32) for q in queries] + [jnp.zeros((CS, 48), f32)], axis=1).astype(bf16)
    key_ref[:, 0 : 2 * width] = qkv_ref[:, width:start]
    for a in range(3):
        key_ref[:, 512 + 256 * a : 640 + 256 * a] = padded(start + (3 + a) * points, points, 128)
        key_ref[:, 384 + 256 * a : 512 + 256 * a] = padded(start + 6 * points + a * H * PV, H * PV, 128)
    rows, lengths = own_side(r, pad_state(single_ref), frame_ref[...], query_ref[...], columns_ref[...])
    rows_ref[...] = rows
    lengths_ref[...] = jnp.broadcast_to(lengths, lengths_ref.shape)
    for i in range(r):
        normed = layer_norm(pair_ref[i]).astype(bf16)
        gate_ref[i] = jax.nn.sigmoid(dot(normed, gate_weight_ref[...]))


def prepare_kernel(
    w, n, r, recv_any, frame_any, rows_any, lengths_any, key_any, columns_any, logits_ref, values_ref,
    recv_ref, frame_ref, rows_ref, lengths_ref, key_ref, columns_ref, sems,
):
    lanes = recv_ref.shape[1]
    for copy in copies(
        sems,
        (recv_any.at[:, r * n * r : r * n * r + lanes], recv_ref),
        (frame_any, frame_ref),
        (rows_any, rows_ref),
        (lengths_any, lengths_ref),
        (key_any, key_ref),
        (columns_any, columns_ref),
    ):
        copy.wait()
    slots = natural_rows(recv_ref, 0, w, r, n)
    logits, values = logits_and_values(
        r, slots, (rows_ref[...], lengths_ref[:, 0:1]), frame_ref[...], key_ref[...], columns_ref[...]
    )
    logits_ref[...] = logits
    values_ref[...] = values


def update_kernel(
    w, n, recv_any, tri_out_any, pair_any, gate_any, bias_weight_any, logits_any, values_any, single_any, frame_any,
    out_weight_any, frame_weight_any, pair_out_any, half_ref, bias_ref, state_ref, new_frame_ref, send_ref,
    recv_ref, tri_out_ref, pair_ref, gate_ref, bias_weight_ref, logits_ref, values_ref, single_ref, frame_ref,
    out_weight_ref, frame_weight_ref, pair_out_ref, sems,
):
    r, count, _ = pair_ref.shape
    bias_weight_ref[...] = jnp.zeros_like(bias_weight_ref)
    loads = copies(
        sems,
        (recv_any, recv_ref),
        (tri_out_any, tri_out_ref),
        (pair_any, pair_ref),
        (gate_any, gate_ref),
        (bias_weight_any, bias_weight_ref.at[0:H]),
        (logits_any, logits_ref),
        (values_any, values_ref),
        (single_any, single_ref),
        (frame_any, frame_ref),
        (out_weight_any, out_weight_ref),
        (frame_weight_any, frame_weight_ref),
    )
    half = r // 2
    row, column = grid_of((2 * CH, 2 * CH))
    c = row & (CH - 1)
    take = onehot(column == (c >> log2(w)) * 2 * w + (row >> log2(CH)) * w + (c & (w - 1)))
    loads[0].wait()
    product = dot(take, recv_ref[...])
    biases = []
    halves = []
    stores = []
    for copy in loads[1:5]:
        copy.wait()
    for high in range(2):
        normed = layer_norm(product[high * CH : (high + 1) * CH], axis=0).astype(bf16)
        update = dot_tn(normed, tri_out_ref[...])
        for low in range(half):
            i = high * half + low
            pair_out = pair_ref[i] + gate_ref[i] * update[low * count : (low + 1) * count]
            pair_out_ref[i] = pair_out
            store = pltpu.make_async_copy(pair_out_ref.at[i], pair_out_any.at[i], sems.at[11 + i])
            store.start()
            stores.append(store)
            normed_pair = layer_norm(pair_out)
            biases.append(dot_nt(bias_weight_ref[...], normed_pair, highest) * third)
            halves.append(normed_pair.astype(bf16))
            half_ref[i] = halves[-1]
    bias = jnp.concatenate(biases, axis=0)
    bias_ref[...] = bias

    def weights():
        loads[9].wait()
        loads[10].wait()
        return out_weight_ref[...], frame_weight_ref[...]

    for copy in loads[5:9]:
        copy.wait()
    state, frame = attend(
        r, logits_ref[...] + bias, values_ref[...], halves, pad_state(single_ref), frame_ref[...], weights
    )
    state_ref[...] = state
    new_frame_ref[...] = frame
    fill_rows(send_ref, 0, spread_rows(slots_of(state, frame), w, r))
    for store in stores:
        store.wait()


def last_kernel(
    w, n, recv_ref, half_ref, bias_ref, state_ref, frame_ref, columns_any, query_any, key_any,
    out_weight_any, frame_weight_any, single_out_ref, rotation_ref, translation_ref,
    columns_ref, query_ref, key_ref, out_weight_ref, frame_weight_ref, scr, sems,
):
    r = half_ref.shape[0]
    loads = copies(
        sems,
        (query_any, query_ref),
        (columns_any, columns_ref),
        (key_any, key_ref),
        (out_weight_any, out_weight_ref),
        (frame_weight_any, frame_weight_ref),
    )
    slots = natural_rows(recv_ref, 0, w, r, n)
    state, frame = state_ref[...], frame_ref[...]
    loads[0].wait()
    loads[1].wait()
    own = own_side(r, state, frame, query_ref[...], columns_ref[...])
    loads[2].wait()
    logits, values = logits_and_values(r, slots, own, frame, key_ref[...], columns_ref[...])

    def weights():
        loads[3].wait()
        loads[4].wait()
        return out_weight_ref[...], frame_weight_ref[...]

    halves = [half_ref[i] for i in range(r)]
    state, frame = attend(r, logits + bias_ref[...], values, halves, state, frame, weights)
    single_out_ref[...] = state[0:r]
    rotation_ref[...] = frame[0:r, 0:9]
    scr[...] = jnp.concatenate([frame, jnp.zeros((128 - IP, 128), f32)], axis=0).T
    translation_ref[...] = scr[9:12, 0:r]


VMEM = pl.BlockSpec(memory_space=pltpu.VMEM)
HBM = pl.BlockSpec(memory_space=pltpu.HBM)
FREE = pl.BlockSpec(memory_space=pl.ANY)


def call(body, name, outs, args, outside=(), outside_outs=(), free=(), scratch=(), limit=32, flops=0, moved=0):
    return pl.pallas_call(
        body,
        name=name,
        out_shape=[jax.ShapeDtypeStruct(s, d) for s, d in outs],
        in_specs=[FREE if at in free else HBM if at in outside else VMEM for at in range(len(args))],
        out_specs=[HBM if at in outside_outs else VMEM for at in range(len(outs))],
        scratch_shapes=list(scratch),
        compiler_params=pltpu.CompilerParams(vmem_limit_bytes=limit * 2**20),
        cost_estimate=pl.CostEstimate(flops=flops, bytes_accessed=moved, transcendentals=0),
    )(*args)


def local(
    pair, single, quats, translate, res_mask, chain_ids, tri_weight, tri_out_weight, qkv_weight, bias_weight,
    head_gamma, chain_bias, out_weight, frame_weight,
):
    n = lax.axis_size("row")
    r, count, _ = pair.shape
    w = CH // n
    rows = 2 * w
    lanes = r * SLOT // rows
    limit = 24 if count == 128 else 56

    def exchange(sent):
        width = sent.shape[1]
        got = lax.all_to_all(sent.reshape(n, rows, width), "row", 0, 0, tiled=True)
        return got.reshape(n * rows, width)

    def like(array):
        return pltpu.VMEM(array.shape, array.dtype)

    dma = pltpu.SemaphoreType.DMA
    sent, frame = call(
        functools.partial(gate_kernel, w, n),
        "gate",
        [((n * rows, r * count + lanes), bf16), ((IP, 128), f32)],
        [pair, tri_weight, single, quats, translate, res_mask, chain_ids],
        outside=range(7),
        scratch=[
            like(pair),
            pltpu.VMEM((CH, 4 * CH), bf16),
            like(single),
            like(quats),
            like(translate),
            pltpu.SMEM((r,), jnp.int32),
            pltpu.SMEM((r,), jnp.int32),
            pltpu.VMEM((128, 128), f32),
            dma((r + 6,)),
        ],
        limit=60,
    )
    received = exchange(sent)

    point_weight = head_gamma * (math.sqrt(2.0 / (9.0 * PQ)) * 0.5 * third)
    columns = jnp.stack([point_weight, chain_bias[0], chain_bias[1]], axis=1)
    columns = jnp.pad(columns, ((0, HP - H), (0, 125)))
    gate, key_weight, query_weight, query_rows, lengths = call(
        own_kernel,
        "own",
        [
            ((r, count, CH), f32),
            ((CS, 1152), bf16),
            ((CS, 384), bf16),
            ((r * HP, 768), f32),
            ((r * HP, 128), f32),
        ],
        [pair, tri_weight, qkv_weight, single, frame, columns],
        outside=range(6),
        scratch=[
            like(pair), pltpu.VMEM((CH, CH), bf16), like(qkv_weight), like(single), like(frame), like(columns), dma((6,))
        ],
        limit=60,
        flops=2 * r * count * CH * CH,
        moved=16 * 2**20,
    )
    received, gate, key_weight, query_weight, query_rows, lengths = lax.optimization_barrier(
        (received, gate, key_weight, query_weight, query_rows, lengths)
    )
    (formed,) = call(
        functools.partial(product_kernel, w, n, r),
        "product",
        [((n * rows, (r // 2) * count), bf16)],
        [received],
        limit=limit,
    )
    products = exchange(formed)
    logits, values = call(
        functools.partial(prepare_kernel, w, n, r),
        "prepare",
        [((r * HP, count), f32), ((count, 640), f32)],
        [received, frame, query_rows, lengths, key_weight, columns],
        outside=range(6),
        free=(0,),
        scratch=[
            pltpu.VMEM((n * rows, lanes), bf16),
            like(frame),
            like(query_rows),
            like(lengths),
            like(key_weight),
            like(columns),
            dma((6,)),
        ],
        limit=limit,
        flops=2 * count * CS * 1280,
        moved=8 * 2**20,
    )
    frame_weight = frame_weight.T
    pair_out, pair_half, bias, state, frame, sent = call(
        functools.partial(update_kernel, w, n),
        "update",
        [
            ((r, count, CH), f32),
            ((r, count, CH), bf16),
            ((r * HP, count), f32),
            ((IP, CS), f32),
            ((IP, 128), f32),
            ((n * rows, lanes), bf16),
        ],
        [products, tri_out_weight, pair, gate, bias_weight.T, logits, values, single, frame, out_weight, frame_weight],
        outside=range(11),
        free=(0,),
        outside_outs=(0,),
        scratch=[
            like(products),
            like(tri_out_weight),
            like(pair),
            like(gate),
            pltpu.VMEM((HP, CH), f32),
            like(logits),
            like(values),
            like(single),
            like(frame),
            like(out_weight),
            like(frame_weight),
            like(pair),
            dma((r + 11,)),
        ],
        limit=limit,
    )
    received = exchange(sent)
    single_out, rotation, translation = call(
        functools.partial(last_kernel, w, n),
        "last",
        [((r, CS), f32), ((r, 9), f32), ((3, r), f32)],
        [received, pair_half, bias, state, frame, columns, query_weight, key_weight, out_weight, frame_weight],
        outside=range(5, 10),
        scratch=[
            like(columns),
            like(query_weight),
            like(key_weight),
            like(out_weight),
            like(frame_weight),
            pltpu.VMEM((128, 128), f32),
            dma((5,)),
        ],
        limit=limit,
    )
    return (pair_out, single_out, rotation.T, translation)


def solution(mesh):
    rows = ("grp", "row")
    placed = (P(rows, None, None), P(rows, None), P(None, rows), P(None, rows), P(rows), P(rows)) + (P(),) * 8
    return jax.shard_map(
        local,
        mesh=mesh,
        in_specs=placed,
        out_specs=(P(rows, None, None), P(rows, None), P(None, rows), P(None, rows)),
        check_vma=False,
    )
```

```python
import functools
import math

import jax
import jax.numpy as jnp
from jax import lax
from jax.experimental import pallas as pl
from jax.experimental.pallas import tpu as pltpu
from jax.sharding import PartitionSpec as P

CH = 128
CS = 384
H = 12
HP = 16
CHEAD = 16
PQ = 4
PV = 8
SLOT = 512
IP = 8
MASK_AT = 12
CHAIN_AT = 13

f32 = jnp.float32
bf16 = jnp.bfloat16
highest = lax.Precision.HIGHEST
epsilon = 1e-05
mask_fill = 100000.0
third = math.sqrt(1.0 / 3.0)


def layer_norm(values, axis=-1):
    center = values - jnp.mean(values, axis=axis, keepdims=True)
    spread = jnp.mean(center * center, axis=axis, keepdims=True)
    return center * lax.rsqrt(spread + epsilon)


def quat_entries(one, two, three, real):
    return [
        1.0 - 2.0 * (two * two + three * three),
        2.0 * (one * two - real * three),
        2.0 * (one * three + real * two),
        2.0 * (one * two + real * three),
        1.0 - 2.0 * (one * one + three * three),
        2.0 * (two * three - real * one),
        2.0 * (one * three - real * two),
        2.0 * (two * three + real * one),
        1.0 - 2.0 * (one * one + two * two),
    ]


def dot(a, b, precision=None):
    return lax.dot_general(
        a, b, (((1,), (0,)), ((), ())), precision=precision, preferred_element_type=f32
    )


def dot_nt(a, b, precision=None):
    return lax.dot_general(
        a, b, (((1,), (1,)), ((), ())), precision=precision, preferred_element_type=f32
    )


def dot_tn(a, b):
    return lax.dot_general(a, b, (((0,), (0,)), ((), ())), preferred_element_type=f32)


def log2(number):
    assert number & (number - 1) == 0
    return number.bit_length() - 1


def grid_of(shape):
    return lax.broadcasted_iota(jnp.int32, shape, 0), lax.broadcasted_iota(jnp.int32, shape, 1)


def onehot(match):
    return jnp.where(match, 1.0, 0.0).astype(bf16)


def swap_rows(count, minor_count):
    row, column = grid_of((count, count))
    major_count = count // minor_count
    minor = row >> log2(major_count)
    major = row & (major_count - 1)
    return onehot(column == major * minor_count + minor)


def spread_rows(slots, w, r):
    rows = 2 * w
    lanes = r * SLOT // rows
    x, i = grid_of((16, 16))
    q = x & (rows - 1)
    if lanes <= SLOT:
        total = None
        for t in range(SLOT // lanes):
            one = dot(onehot((q == t * r + i) & (i < r)), slots[:, t * lanes : (t + 1) * lanes])
            total = one if total is None else total + one
        return total.astype(bf16)
    return jnp.concatenate(
        [dot(onehot(i == t * rows + q), slots) for t in range(lanes // SLOT)], axis=1
    ).astype(bf16)


def natural_rows(x_ref, first, w, r, n, start=0, stop=SLOT):
    rows = 2 * w
    lanes = r * SLOT // rows
    count = n * r
    j, x = grid_of((count, n * rows))
    s = x >> log2(rows)
    q = x & (rows - 1)
    if lanes <= SLOT:
        pieces = []
        for t in range(SLOT // lanes):
            low, high = max(start, t * lanes), min(stop, (t + 1) * lanes)
            if low < high:
                values = x_ref[:, first + low - t * lanes : first + high - t * lanes]
                pieces.append(dot(onehot((j == s * r + q - t * r) & ((q >> log2(r)) == t)), values))
        return (pieces[0] if len(pieces) == 1 else jnp.concatenate(pieces, axis=1)).astype(bf16)
    total = None
    for t in range(lanes // SLOT):
        values = x_ref[:, first + t * SLOT + start : first + t * SLOT + stop]
        one = dot(onehot(j == s * r + t * rows + q), values)
        total = one if total is None else total + one
    return total.astype(bf16)


def frame_pieces(frame):
    high = frame.astype(bf16).astype(f32)
    rest = frame - high
    middle = rest.astype(bf16).astype(f32)
    low = (rest - middle).astype(bf16).astype(f32)
    return high + pltpu.roll(middle, 32, 1) + pltpu.roll(low, 64, 1)


def slots_of(state, frame):
    both = jnp.concatenate([state, frame_pieces(frame)], axis=1)
    return jnp.concatenate([both, jnp.zeros_like(both)], axis=0).astype(bf16)


def fill_rows(out_ref, first, tile):
    lanes = tile.shape[1]
    for t in range(out_ref.shape[0] // 16):
        out_ref[t * 16 : (t + 1) * 16, first : first + lanes] = tile


def piece_select(row_count, transposed=False):
    if transposed:
        lane, entry = grid_of((128, row_count))
    else:
        entry, lane = grid_of((row_count, 128))
    return onehot(((lane & 31) == entry) & (lane < 96))


def copies(sems, *pairs):
    started = [pltpu.make_async_copy(src, dst, sems.at[at]) for at, (src, dst) in enumerate(pairs)]
    for copy in started:
        copy.start()
    return started


def gate_kernel(
    w, n, pair_any, tri_any, single_any, quats_any, translate_any, mask_any, chain_any, send_ref, frame_ref,
    pair_ref, tri_ref, single_ref, quats_ref, translate_ref, mask_ref, chain_ref, scr, sems,
):
    r, count, _ = pair_ref.shape
    big = copies(sems, (tri_any.at[:, 0 : 4 * CH], tri_ref), *((pair_any.at[i], pair_ref.at[i]) for i in range(r)))
    little = copies(
        sems.at[r + 1 :],
        (quats_any, quats_ref),
        (translate_any, translate_ref),
        (mask_any, mask_ref),
        (chain_any, chain_ref),
        (single_any, single_ref),
    )
    row, column = grid_of((2 * CH, 2 * CH))
    d = row >> log2(2 * w)
    side = (row >> log2(w)) & 1
    take = onehot(column == side * CH + d * w + (row & (w - 1)))
    big[0].wait()
    gate_weight = jnp.concatenate([tri_ref[:, 0:CH], tri_ref[:, 2 * CH : 3 * CH]], axis=1)
    value_weight = jnp.concatenate([tri_ref[:, CH : 2 * CH], tri_ref[:, 3 * CH : 4 * CH]], axis=1)
    gate_weight = dot_nt(take, gate_weight).astype(bf16)
    value_weight = dot_nt(take, value_weight).astype(bf16)
    for copy in little:
        copy.wait()
    for i in range(r):
        big[1 + i].wait()
        normed = layer_norm(pair_ref[i]).astype(bf16)
        gates = dot_nt(gate_weight, normed)
        values = dot_nt(value_weight, normed)
        side_values = jax.nn.sigmoid(gates) * values * mask_ref[i].astype(f32)
        send_ref[:, i * count : (i + 1) * count] = side_values.astype(bf16)

    scr[...] = jnp.zeros_like(scr)
    quats = quats_ref[...]
    real = lax.rsqrt(1.0 + jnp.sum(quats * quats, axis=0, keepdims=True))
    unit = quats * real
    entries = quat_entries(unit[0:1], unit[1:2], unit[2:3], real)
    for at, entry in enumerate(entries):
        scr[at : at + 1, 0:r] = entry
    scr[9:12, 0:r] = translate_ref[...]
    frame = scr[...].T[0:IP, :]
    row, lane = grid_of((IP, 128))
    for i in range(r):
        frame = jnp.where((row == i) & (lane == MASK_AT), mask_ref[i].astype(f32), frame)
        frame = jnp.where((row == i) & (lane == CHAIN_AT), chain_ref[i].astype(f32), frame)
    frame_ref[...] = frame
    fill_rows(send_ref, r * count, spread_rows(slots_of(pad_state(single_ref), frame), w, r))


def product_kernel(w, n, r, recv_ref, send_ref):
    count = n * r
    rows = 2 * w
    pieces = natural_rows(recv_ref, r * count, w, r, n, CS, SLOT)
    mask = dot_nt(piece_select(16), pieces)[MASK_AT : MASK_AT + 1, :]
    mask = jnp.concatenate([mask] * r, axis=1)
    order = swap_rows(n * rows, rows)
    sides = (dot(order, recv_ref[:, 0 : r * count]) * mask).astype(bf16)
    row, column = grid_of((count, count))
    to_natural = onehot(row == (column & (n - 1)) * r + (column >> log2(n)))

    def stacked(block):
        part = sides[block * n : (block + 1) * n]
        return jnp.concatenate([part[:, i * count : (i + 1) * count] for i in range(r)], axis=0)

    half = r // 2
    products = []
    for c in range(w):
        right = dot(to_natural, stacked(w + c)).astype(bf16)
        products.append(dot_nt(stacked(c), right).astype(bf16))
    blocks = []
    for high in range(2):
        for c in range(w):
            first = high * half
            blocks.append(
                jnp.concatenate(
                    [products[c][(first + low) * n : (first + low + 1) * n] for low in range(half)], axis=1
                )
            )
    send_ref[...] = dot(swap_rows(n * rows, n), jnp.concatenate(blocks, axis=0)).astype(bf16)


def head_masks():
    h, lane = grid_of((HP, 256))
    query_scalar = jnp.where(((lane >> log2(CHEAD)) == h) & (h < H), 1.0, 0.0)
    value_scalar = jnp.where((((lane - 64) >> log2(CHEAD)) == h) & (h < H), 1.0, 0.0)
    h, lane = grid_of((HP, 128))
    query = jnp.where(((lane >> log2(PQ)) == h) & (h < H), 1.0, 0.0)
    value = jnp.where(((lane >> log2(PV)) == h) & (h < H), 1.0, 0.0)
    return query_scalar, value_scalar, query, value


def own_side(r, state, frame, query_weight, columns):
    both = jnp.concatenate([state, jnp.zeros_like(state)], axis=0).astype(bf16)
    own = dot(both, query_weight)[0:IP]
    width = H * CHEAD
    points = H * PQ
    fill = jnp.zeros((IP, 128 - points), f32)
    own_local = [
        jnp.concatenate([own[:, width + a * points : width + (a + 1) * points], fill], axis=1) for a in range(3)
    ]
    own_points = []
    for a in range(3):
        own_points.append(
            frame[:, 3 * a : 3 * a + 1] * own_local[0]
            + frame[:, 3 * a + 1 : 3 * a + 2] * own_local[1]
            + frame[:, 3 * a + 2 : 3 * a + 3] * own_local[2]
            + frame[:, 9 + a : 10 + a]
        )
    query_scalar, _, query_mask, _ = head_masks()
    weight = columns[:, 0:1]
    query_rows = []
    lengths = []
    for i in range(r):
        scalar = own[i : i + 1, 0:256] * (third / math.sqrt(CHEAD)) * query_scalar
        points = [p[i : i + 1] * query_mask for p in own_points]
        query_rows.append(
            jnp.concatenate([scalar] + [2.0 * weight * p for p in points] + [-weight * query_mask], axis=1)
        )
        length = points[0] * points[0] + points[1] * points[1] + points[2] * points[2]
        lengths.append(-weight * jnp.sum(length, axis=1, keepdims=True))
    return jnp.concatenate(query_rows, axis=0), jnp.concatenate(lengths, axis=0)


def logits_and_values(r, slots, own, frame, key_weight, columns):
    query_rows, lengths = own
    pieces = slots[:, CS:SLOT]
    entry = dot(pieces, piece_select(128, True))
    rows = dot_nt(piece_select(16), pieces)
    keys = dot(slots[:, 0:CS], key_weight)
    local = [keys[:, 384 + 256 * a : 640 + 256 * a] for a in range(3)]
    placed = []
    for a in range(3):
        placed.append(
            entry[:, 3 * a : 3 * a + 1] * local[0]
            + entry[:, 3 * a + 1 : 3 * a + 2] * local[1]
            + entry[:, 3 * a + 2 : 3 * a + 3] * local[2]
            + entry[:, 9 + a : 10 + a]
        )
    values = jnp.concatenate([keys[:, 128:384]] + [p[:, 0:128] for p in placed], axis=1)
    key_points = [p[:, 128:256] for p in placed]
    length = key_points[0] * key_points[0] + key_points[1] * key_points[1] + key_points[2] * key_points[2]
    key_side = jnp.concatenate([keys[:, 0:256]] + key_points + [length], axis=1)
    far = mask_fill * (rows[MASK_AT : MASK_AT + 1, :] - 1.0)
    added = []
    for i in range(r):
        same = rows[CHAIN_AT : CHAIN_AT + 1, :] == frame[i : i + 1, CHAIN_AT : CHAIN_AT + 1]
        added.append(jnp.where(same, columns[:, 2:3], columns[:, 1:2]) + far + lengths[i * HP : (i + 1) * HP])
    logits = dot_nt(query_rows, key_side, highest)
    return logits + jnp.concatenate(added, axis=0), values


def attend(r, logits, values, pair_half, state, frame, weights):
    top = jnp.max(logits, axis=1, keepdims=True)
    raised = jnp.exp(logits - top)
    attention = raised / jnp.sum(raised, axis=1, keepdims=True)
    summed = dot(attention, values, highest)
    _, value_scalar, _, value_mask = head_masks()
    masks = jnp.concatenate([value_scalar, value_mask, value_mask, value_mask], axis=1)
    summed = summed * jnp.concatenate([masks] * r, axis=0)
    gathered = jnp.sum(summed.reshape(r, HP, 640), axis=1)
    gathered = jnp.concatenate([gathered, jnp.zeros((IP - r, 640), f32)], axis=0)
    relative = [
        gathered[:, 256 + 128 * a : 256 + 128 * a + H * PV] - frame[:, 9 + a : 10 + a] for a in range(3)
    ]
    out_local = [
        frame[:, a : a + 1] * relative[0]
        + frame[:, 3 + a : 4 + a] * relative[1]
        + frame[:, 6 + a : 7 + a] * relative[2]
        for a in range(3)
    ]
    out_norm = jnp.sqrt(
        out_local[0] * out_local[0] + out_local[1] * out_local[1] + out_local[2] * out_local[2] + 1e-08
    )
    half = attention.astype(bf16)
    out_pair = jnp.concatenate(
        [dot(half[i * HP : (i + 1) * HP], pair_half[i]) for i in range(r)], axis=0
    ).astype(bf16)
    row, column = grid_of((H * IP, r * HP))
    by_head = dot(onehot(column == (row & (IP - 1)) * HP + (row >> log2(IP))), out_pair)
    combined = jnp.concatenate(
        [gathered[:, 256 - H * CHEAD : 256]]
        + out_local
        + [out_norm]
        + [by_head[h * IP : (h + 1) * IP] for h in range(H)],
        axis=1,
    )
    combined = jnp.concatenate([combined, jnp.zeros_like(combined)], axis=0).astype(bf16)
    out_weight, frame_weight = weights()
    state = layer_norm(state + dot(combined, out_weight)[0:IP])
    update = dot_nt(state, frame_weight, highest)
    quat = [update[:, a : a + 1] for a in range(3)]
    real = lax.rsqrt(1.0 + (quat[0] * quat[0] + quat[1] * quat[1] + quat[2] * quat[2]))
    step = quat_entries(quat[0] * real, quat[1] * real, quat[2] * real, real)
    old = [frame[:, e : e + 1] for e in range(9)]
    columns = []
    for target in range(3):
        for column in range(3):
            columns.append(
                old[target * 3] * step[column]
                + old[target * 3 + 1] * step[3 + column]
                + old[target * 3 + 2] * step[6 + column]
            )
    for target in range(3):
        columns.append(
            frame[:, 9 + target : 10 + target]
            + old[target * 3] * update[:, 3:4]
            + old[target * 3 + 1] * update[:, 4:5]
            + old[target * 3 + 2] * update[:, 5:6]
        )
    _, lane = grid_of((IP, 128))
    for at, column in enumerate(columns):
        frame = jnp.where(lane == at, column, frame)
    return state, frame


def pad_state(single_ref):
    r = single_ref.shape[0]
    return jnp.concatenate([single_ref[...], jnp.zeros((IP - r, CS), f32)], axis=0)


PACK_ROWS = 216
TRI_OUT, BIAS, COLUMNS, FRAME_WEIGHT, STATE, FRAME = 0, 128, 144, 160, 184, 208


def wide(pack_ref, first):
    return jnp.concatenate([pack_ref[first + IP * part : first + IP * (part + 1)] for part in range(3)], axis=1)


def own_kernel(
    pair_any, tri_any, qkv_any, single_any, frame_any, columns_any, tri_out_any, bias_weight_any, frame_weight_any,
    gate_ref, key_ref, query_ref, rows_ref, pack_ref, pair_copy_any,
    pair_ref, gate_weight_ref, qkv_ref, single_ref, tri_out_ref, bias_weight_ref, frame_weight_ref, sems,
):
    r, count, _ = pair_ref.shape
    frame_ref = pack_ref.at[FRAME : FRAME + IP]
    columns_ref = pack_ref.at[COLUMNS : COLUMNS + HP]
    for copy in copies(
        sems,
        (pair_any, pair_ref),
        (tri_any.at[:, 4 * CH :], gate_weight_ref),
        (qkv_any, qkv_ref),
        (single_any, single_ref),
        (frame_any, frame_ref),
        (columns_any, columns_ref),
        (tri_out_any, tri_out_ref),
        (bias_weight_any, bias_weight_ref),
        (frame_weight_any, frame_weight_ref),
    ):
        copy.wait()
    back = pltpu.make_async_copy(pair_ref, pair_copy_any, sems.at[9])
    back.start()
    pack_ref[TRI_OUT : TRI_OUT + CH, :] = tri_out_ref[...].astype(f32)
    bias_weight = bias_weight_ref[...]
    pack_ref[BIAS : BIAS + HP, :] = jnp.concatenate([bias_weight, jnp.zeros((HP - H, CH), f32)], axis=0)
    state = pad_state(single_ref)
    frame_weight = frame_weight_ref[...]
    frame_weight = jnp.concatenate([frame_weight, jnp.zeros((IP - 6, CS), f32)], axis=0)
    for part in range(3):
        lanes = slice(128 * part, 128 * (part + 1))
        pack_ref[FRAME_WEIGHT + IP * part : FRAME_WEIGHT + IP * (part + 1), :] = frame_weight[:, lanes]
        pack_ref[STATE + IP * part : STATE + IP * (part + 1), :] = state[:, lanes]
    width = H * CHEAD
    start = 3 * width
    points = H * PQ

    def padded(first, size, to):
        block = qkv_ref[:, first : first + size].astype(f32)
        return jnp.concatenate([block, jnp.zeros((CS, to - size), f32)], axis=1).astype(bf16)

    queries = [qkv_ref[:, 0:width], qkv_ref[:, start : start + 3 * points]]
    query_ref[...] = jnp.concatenate([q.astype(f32) for q in queries] + [jnp.zeros((CS, 48), f32)], axis=1).astype(bf16)
    key_ref[:, 0 : 2 * width] = qkv_ref[:, width:start]
    for a in range(3):
        key_ref[:, 512 + 256 * a : 640 + 256 * a] = padded(start + (3 + a) * points, points, 128)
        key_ref[:, 384 + 256 * a : 512 + 256 * a] = padded(start + 6 * points + a * H * PV, H * PV, 128)
    rows, lengths = own_side(r, state, frame_ref[...], query_ref[...], columns_ref[...])
    rows_ref[:, 0:768] = rows
    rows_ref[:, 768:896] = jnp.broadcast_to(lengths, (r * HP, 128))
    for i in range(r):
        normed = layer_norm(pair_ref[i]).astype(bf16)
        gate_ref[i] = jax.nn.sigmoid(dot(normed, gate_weight_ref[...])).astype(bf16)
    back.wait()


def prepare_kernel(w, n, r, recv_ref, rows_ref, key_ref, pack_ref, logits_ref, values_ref):
    slots = natural_rows(recv_ref, r * n * r, w, r, n)
    logits, values = logits_and_values(
        r, slots, (rows_ref[:, 0:768], rows_ref[:, 768:769]), pack_ref[FRAME : FRAME + IP], key_ref[...],
        pack_ref[COLUMNS : COLUMNS + HP],
    )
    logits_ref[...] = logits
    values_ref[...] = values


def update_kernel(
    w, n, recv_ref, pair_any, gate_ref, logits_ref, values_ref, pack_ref, out_weight_ref,
    pair_out_any, half_ref, bias_ref, state_ref, new_frame_ref, send_ref, pair_ref, sems,
):
    r, count, _ = pair_ref.shape
    load = pltpu.make_async_copy(pair_any, pair_ref, sems.at[r])
    load.start()
    half = r // 2
    row, column = grid_of((2 * CH, 2 * CH))
    c = row & (CH - 1)
    take = onehot(column == (c >> log2(w)) * 2 * w + (row >> log2(CH)) * w + (c & (w - 1)))
    product = dot(take, recv_ref[...])
    tri_out = pack_ref[TRI_OUT : TRI_OUT + CH, :].astype(bf16)
    updates = []
    for high in range(2):
        normed = layer_norm(product[high * CH : (high + 1) * CH], axis=0).astype(bf16)
        updates.append(dot_tn(normed, tri_out))
    load.wait()
    biases = []
    halves = []
    stores = []
    for i in range(r):
        low = i % half
        update = updates[i // half][low * count : (low + 1) * count]
        pair_out = pair_ref[i] + gate_ref[i].astype(f32) * update
        pair_ref[i] = pair_out
        store = pltpu.make_async_copy(pair_ref.at[i], pair_out_any.at[i], sems.at[i])
        store.start()
        stores.append(store)
        normed_pair = layer_norm(pair_out)
        biases.append(dot_nt(pack_ref[BIAS : BIAS + HP, :], normed_pair, highest) * third)
        halves.append(normed_pair.astype(bf16))
        half_ref[i] = halves[-1]
    bias = jnp.concatenate(biases, axis=0)
    bias_ref[...] = bias
    state, frame = attend(
        r, logits_ref[...] + bias, values_ref[...], halves, wide(pack_ref, STATE), pack_ref[FRAME : FRAME + IP],
        lambda: (out_weight_ref[...], wide(pack_ref, FRAME_WEIGHT)),
    )
    state_ref[...] = state
    new_frame_ref[...] = frame
    fill_rows(send_ref, 0, spread_rows(slots_of(state, frame), w, r))
    for store in stores:
        store.wait()


def last_kernel(
    w, n, recv_ref, half_ref, bias_ref, state_ref, frame_ref, pack_ref, query_ref, key_ref, out_weight_ref,
    single_out_ref, rotation_ref, translation_ref, scr,
):
    r = half_ref.shape[0]
    slots = natural_rows(recv_ref, 0, w, r, n)
    state, frame = state_ref[...], frame_ref[...]
    columns = pack_ref[COLUMNS : COLUMNS + HP]
    own = own_side(r, state, frame, query_ref[...], columns)
    logits, values = logits_and_values(r, slots, own, frame, key_ref[...], columns)
    halves = [half_ref[i] for i in range(r)]
    state, frame = attend(
        r, logits + bias_ref[...], values, halves, state, frame,
        lambda: (out_weight_ref[...], wide(pack_ref, FRAME_WEIGHT)),
    )
    single_out_ref[...] = state[0:r]
    rotation_ref[...] = frame[0:r, 0:9]
    scr[...] = jnp.concatenate([frame, jnp.zeros((128 - IP, 128), f32)], axis=0).T
    translation_ref[...] = scr[9:12, 0:r]


VMEM = pl.BlockSpec(memory_space=pltpu.VMEM)
HBM = pl.BlockSpec(memory_space=pltpu.HBM)


def call(body, name, outs, args, outside=(), outside_outs=(), scratch=(), limit=32, alias=None, flops=0, moved=0):
    return pl.pallas_call(
        body,
        name=name,
        out_shape=[jax.ShapeDtypeStruct(s, d) for s, d in outs],
        in_specs=[HBM if at in outside else VMEM for at in range(len(args))],
        out_specs=[HBM if at in outside_outs else VMEM for at in range(len(outs))],
        scratch_shapes=list(scratch),
        input_output_aliases=alias or {},
        compiler_params=pltpu.CompilerParams(vmem_limit_bytes=limit * 2**20),
        cost_estimate=pl.CostEstimate(flops=flops, bytes_accessed=moved, transcendentals=0),
    )(*args)


def local(
    pair, single, quats, translate, res_mask, chain_ids, tri_weight, tri_out_weight, qkv_weight, bias_weight,
    head_gamma, chain_bias, out_weight, frame_weight,
):
    n = lax.axis_size("row")
    r, count, _ = pair.shape
    w = CH // n
    rows = 2 * w
    lanes = r * SLOT // rows
    limit = 24 if count == 128 else 56

    def exchange(sent):
        width = sent.shape[1]
        got = lax.all_to_all(sent.reshape(n, rows, width), "row", 0, 0, tiled=True)
        return got.reshape(n * rows, width)

    def like(array):
        return pltpu.VMEM(array.shape, array.dtype)

    dma = pltpu.SemaphoreType.DMA
    sent, frame = call(
        functools.partial(gate_kernel, w, n),
        "gate",
        [((n * rows, r * count + lanes), bf16), ((IP, 128), f32)],
        [pair, tri_weight, single, quats, translate, res_mask, chain_ids],
        outside=range(7),
        scratch=[
            like(pair),
            pltpu.VMEM((CH, 4 * CH), bf16),
            like(single),
            like(quats),
            like(translate),
            pltpu.SMEM((r,), jnp.int32),
            pltpu.SMEM((r,), jnp.int32),
            pltpu.VMEM((128, 128), f32),
            dma((r + 6,)),
        ],
        limit=60,
    )
    received = exchange(sent)

    point_weight = head_gamma * (math.sqrt(2.0 / (9.0 * PQ)) * 0.5 * third)
    columns = jnp.stack([point_weight, chain_bias[0], chain_bias[1]], axis=1)
    columns = jnp.pad(columns, ((0, HP - H), (0, 125)))
    gate, key_weight, query_weight, query_rows, pack, pair_copy = call(
        own_kernel,
        "own",
        [
            ((r, count, CH), bf16),
            ((CS, 1152), bf16),
            ((CS, 384), bf16),
            ((r * HP, 896), f32),
            ((PACK_ROWS, 128), f32),
            (pair.shape, f32),
        ],
        [pair, tri_weight, qkv_weight, single, frame, columns, tri_out_weight, bias_weight.T, frame_weight.T],
        outside=range(9),
        outside_outs=(5,),
        scratch=[
            like(pair),
            pltpu.VMEM((CH, CH), bf16),
            like(qkv_weight),
            like(single),
            like(tri_out_weight),
            pltpu.VMEM((H, CH), f32),
            pltpu.VMEM((6, CS), f32),
            dma((10,)),
        ],
        limit=60,
        flops=2 * r * count * CH * CH,
        moved=16 * 2**20,
    )
    received, gate, key_weight, query_weight, query_rows, pack, pair_copy = lax.optimization_barrier(
        (received, gate, key_weight, query_weight, query_rows, pack, pair_copy)
    )
    (formed,) = call(
        functools.partial(product_kernel, w, n, r),
        "product",
        [((n * rows, (r // 2) * count), bf16)],
        [received],
        limit=limit,
    )
    products = exchange(formed)
    logits, values = call(
        functools.partial(prepare_kernel, w, n, r),
        "prepare",
        [((r * HP, count), f32), ((count, 640), f32)],
        [received, query_rows, key_weight, pack],
        limit=limit,
        flops=2 * count * CS * 1152,
        moved=8 * 2**20,
    )
    pair_out, pair_half, bias, state, frame, sent = call(
        functools.partial(update_kernel, w, n),
        "update",
        [
            ((r, count, CH), f32),
            ((r, count, CH), bf16),
            ((r * HP, count), f32),
            ((IP, CS), f32),
            ((IP, 128), f32),
            ((n * rows, lanes), bf16),
        ],
        [products, pair_copy, gate, logits, values, pack, out_weight],
        outside=(1,),
        outside_outs=(0,),
        alias={1: 0},
        scratch=[like(pair), dma((r + 1,))],
        limit=limit,
    )
    received = exchange(sent)
    single_out, rotation, translation = call(
        functools.partial(last_kernel, w, n),
        "last",
        [((r, CS), f32), ((r, 9), f32), ((3, r), f32)],
        [received, pair_half, bias, state, frame, pack, query_weight, key_weight, out_weight],
        scratch=[pltpu.VMEM((128, 128), f32)],
        limit=limit,
    )
    return (pair_out, single_out, rotation.T, translation)


def solution(mesh):
    rows = ("grp", "row")
    placed = (P(rows, None, None), P(rows, None), P(None, rows), P(None, rows), P(rows), P(rows)) + (P(),) * 8
    return jax.shard_map(
        local,
        mesh=mesh,
        in_specs=placed,
        out_specs=(P(rows, None, None), P(rows, None), P(None, rows), P(None, rows)),
        check_vma=False,
    )
```

```python
import functools
import math

import jax
import jax.numpy as jnp
from jax import lax
from jax.experimental import pallas as pl
from jax.experimental.pallas import tpu as pltpu
from jax.sharding import PartitionSpec as P

CH = 128
CS = 384
H = 12
CHEAD = 16
PQ = 4
PV = 8
SLOT = 512
IP = 8
ROWS = H * IP
MASK_AT = 12
CHAIN_AT = 13

f32 = jnp.float32
bf16 = jnp.bfloat16
highest = lax.Precision.HIGHEST
epsilon = 1e-05
mask_fill = 100000.0
third = math.sqrt(1.0 / 3.0)


def layer_norm(values, axis=-1):
    center = values - jnp.mean(values, axis=axis, keepdims=True)
    spread = jnp.mean(center * center, axis=axis, keepdims=True)
    return center * lax.rsqrt(spread + epsilon)


def quat_entries(one, two, three, real):
    return [
        1.0 - 2.0 * (two * two + three * three),
        2.0 * (one * two - real * three),
        2.0 * (one * three + real * two),
        2.0 * (one * two + real * three),
        1.0 - 2.0 * (one * one + three * three),
        2.0 * (two * three - real * one),
        2.0 * (one * three - real * two),
        2.0 * (two * three + real * one),
        1.0 - 2.0 * (one * one + two * two),
    ]


def dot(a, b, precision=None):
    return lax.dot_general(
        a, b, (((1,), (0,)), ((), ())), precision=precision, preferred_element_type=f32
    )


def dot_nt(a, b, precision=None):
    return lax.dot_general(
        a, b, (((1,), (1,)), ((), ())), precision=precision, preferred_element_type=f32
    )


def dot_tn(a, b):
    return lax.dot_general(a, b, (((0,), (0,)), ((), ())), preferred_element_type=f32)


def log2(number):
    assert number & (number - 1) == 0
    return number.bit_length() - 1


def grid_of(shape):
    return lax.broadcasted_iota(jnp.int32, shape, 0), lax.broadcasted_iota(jnp.int32, shape, 1)


def onehot(match):
    return jnp.where(match, 1.0, 0.0).astype(bf16)


def swap_rows(count, minor_count):
    row, column = grid_of((count, count))
    major_count = count // minor_count
    minor = row >> log2(major_count)
    major = row & (major_count - 1)
    return onehot(column == major * minor_count + minor)


def spread_rows(slots, w, r):
    rows = 2 * w
    lanes = r * SLOT // rows
    if rows == 8 and r == 4:
        low, high = slots[0:IP, 0:lanes].astype(f32), slots[0:IP, lanes:].astype(f32)
        row, _ = grid_of((IP, lanes))
        one = jnp.where(row < r, low, pltpu.roll(high, r, 0))
        return jnp.concatenate([one, one], axis=0).astype(bf16)
    x, i = grid_of((16, 16))
    q = x & (rows - 1)
    if lanes <= SLOT:
        total = None
        for t in range(SLOT // lanes):
            one = dot(onehot((q == t * r + i) & (i < r)), slots[:, t * lanes : (t + 1) * lanes])
            total = one if total is None else total + one
        return total.astype(bf16)
    return jnp.concatenate(
        [dot(onehot(i == t * rows + q), slots) for t in range(lanes // SLOT)], axis=1
    ).astype(bf16)


def natural_rows(x_ref, first, w, r, n, start=0, stop=SLOT):
    rows = 2 * w
    lanes = r * SLOT // rows
    count = n * r
    j, x = grid_of((count, n * rows))
    s = x >> log2(rows)
    q = x & (rows - 1)
    if lanes <= SLOT:
        pieces = []
        for t in range(SLOT // lanes):
            low, high = max(start, t * lanes), min(stop, (t + 1) * lanes)
            if low < high:
                values = x_ref[:, first + low - t * lanes : first + high - t * lanes]
                pieces.append(dot(onehot((j == s * r + q - t * r) & ((q >> log2(r)) == t)), values))
        return (pieces[0] if len(pieces) == 1 else jnp.concatenate(pieces, axis=1)).astype(bf16)
    total = None
    for t in range(lanes // SLOT):
        values = x_ref[:, first + t * SLOT + start : first + t * SLOT + stop]
        one = dot(onehot(j == s * r + t * rows + q), values)
        total = one if total is None else total + one
    return total.astype(bf16)


def frame_pieces(frame):
    high = frame.astype(bf16).astype(f32)
    rest = frame - high
    middle = rest.astype(bf16).astype(f32)
    low = (rest - middle).astype(bf16).astype(f32)
    return high + pltpu.roll(middle, 32, 1) + pltpu.roll(low, 64, 1)


def slots_of(state, frame):
    both = jnp.concatenate([state, frame_pieces(frame)], axis=1)
    return jnp.concatenate([both, jnp.zeros_like(both)], axis=0).astype(bf16)


def fill_rows(out_ref, first, tile):
    lanes = tile.shape[1]
    for t in range(out_ref.shape[0] // 16):
        out_ref[t * 16 : (t + 1) * 16, first : first + lanes] = tile


def piece_select(row_count, transposed=False):
    if transposed:
        lane, entry = grid_of((128, row_count))
    else:
        entry, lane = grid_of((row_count, 128))
    return onehot(((lane & 31) == entry) & (lane < 96))


def copies(sems, *pairs):
    started = [pltpu.make_async_copy(src, dst, sems.at[at]) for at, (src, dst) in enumerate(pairs)]
    for copy in started:
        copy.start()
    return started


def gate_kernel(
    w, n, pair_any, tri_any, single_any, quats_any, translate_any, mask_any, chain_any, send_ref, frame_ref,
    pair_ref, tri_ref, single_ref, quats_ref, translate_ref, mask_ref, chain_ref, scr, sems,
):
    r, count, _ = pair_ref.shape
    loads = copies(
        sems,
        (quats_any, quats_ref),
        (translate_any, translate_ref),
        (mask_any, mask_ref),
        (chain_any, chain_ref),
        (single_any, single_ref),
        (tri_any.at[:, 0 : 4 * CH], tri_ref),
        (pair_any, pair_ref),
    )
    row, column = grid_of((2 * CH, 2 * CH))
    d = row >> log2(2 * w)
    side = (row >> log2(w)) & 1
    take = onehot(column == side * CH + d * w + (row & (w - 1)))
    for load in loads:
        load.wait()
    gate_weight = jnp.concatenate([tri_ref[:, 0:CH], tri_ref[:, 2 * CH : 3 * CH]], axis=1)
    value_weight = jnp.concatenate([tri_ref[:, CH : 2 * CH], tri_ref[:, 3 * CH : 4 * CH]], axis=1)
    gate_weight = dot_nt(take, gate_weight).astype(bf16)
    value_weight = dot_nt(take, value_weight).astype(bf16)
    normed = layer_norm(pair_ref[...].reshape(r * count, CH)).astype(bf16)
    gates = dot_nt(gate_weight, normed)
    values = dot_nt(value_weight, normed)
    mask = jnp.concatenate([jnp.full((1, count), mask_ref[i].astype(f32)) for i in range(r)], axis=1)
    send_ref[:, 0 : r * count] = (jax.nn.sigmoid(gates) * values * mask).astype(bf16)

    scr[...] = jnp.zeros_like(scr)
    quats = quats_ref[...]
    real = lax.rsqrt(1.0 + jnp.sum(quats * quats, axis=0, keepdims=True))
    unit = quats * real
    entries = quat_entries(unit[0:1], unit[1:2], unit[2:3], real)
    for at, entry in enumerate(entries):
        scr[at : at + 1, 0:r] = entry
    scr[9:12, 0:r] = translate_ref[...]
    frame = scr[...].T[0:IP, :]
    row, lane = grid_of((IP, 128))
    for i in range(r):
        frame = jnp.where((row == i) & (lane == MASK_AT), mask_ref[i].astype(f32), frame)
        frame = jnp.where((row == i) & (lane == CHAIN_AT), chain_ref[i].astype(f32), frame)
    frame_ref[...] = frame
    fill_rows(send_ref, r * count, spread_rows(slots_of(pad_state(single_ref), frame), w, r))


def product_kernel(w, n, r, recv_ref, send_ref, slots_ref):
    count = n * r
    slots_ref[...] = recv_ref[:, r * count :]
    rows = 2 * w
    pieces = natural_rows(recv_ref, r * count, w, r, n, CS, SLOT)
    mask = dot_nt(piece_select(16), pieces)[MASK_AT : MASK_AT + 1, :]
    mask = jnp.concatenate([mask] * r, axis=1)
    order = swap_rows(n * rows, rows)
    sides = (dot(order, recv_ref[:, 0 : r * count]) * mask).astype(bf16)
    row, column = grid_of((count, count))
    to_natural = onehot(row == (column & (n - 1)) * r + (column >> log2(n)))

    def stacked(block):
        part = sides[block * n : (block + 1) * n]
        return jnp.concatenate([part[:, i * count : (i + 1) * count] for i in range(r)], axis=0)

    half = r // 2
    products = []
    for c in range(w):
        right = dot(to_natural, stacked(w + c)).astype(bf16)
        products.append(dot_nt(stacked(c), right).astype(bf16))
    blocks = []
    for high in range(2):
        for c in range(w):
            first = high * half
            blocks.append(
                jnp.concatenate(
                    [products[c][(first + low) * n : (first + low + 1) * n] for low in range(half)], axis=1
                )
            )
    send_ref[...] = dot(swap_rows(n * rows, n), jnp.concatenate(blocks, axis=0)).astype(bf16)


def tiles(x):
    return [x[h * IP : (h + 1) * IP] for h in range(H)]


def own_side(state, frame, qkv_ref, point_weight):
    both = jnp.concatenate([state, jnp.zeros_like(state)], axis=0).astype(bf16)
    own = dot(both, jnp.concatenate([qkv_ref[:, 0:256], qkv_ref[:, 512:768]], axis=1))[0:IP]
    width = H * CHEAD
    count = H * PQ
    start = 3 * width - 256
    fill = jnp.zeros((IP, 128 - count), f32)
    own_local = [jnp.concatenate([own[:, start + a * count : start + (a + 1) * count], fill], axis=1) for a in range(3)]
    scalars = jnp.concatenate([jnp.zeros((IP, 256 - width), f32), own[:, 0:width]], axis=1)
    points = []
    for a in range(3):
        points.append(
            frame[:, 3 * a : 3 * a + 1] * own_local[0]
            + frame[:, 3 * a + 1 : 3 * a + 2] * own_local[1]
            + frame[:, 3 * a + 2 : 3 * a + 3] * own_local[2]
            + frame[:, 9 + a : 10 + a]
        )
    weight = jnp.broadcast_to(point_weight, (IP, 128))
    length = weight * (points[0] * points[0] + points[1] * points[1] + points[2] * points[2])
    everything = jnp.concatenate(
        [scalars * (third / math.sqrt(CHEAD))] + [2.0 * weight * p for p in points] + [-weight], axis=1
    )
    _, lane = grid_of((IP, 768))
    head = jnp.where(lane < 256, (lane - (256 - width)) >> log2(CHEAD), (lane & 127) >> log2(PQ))
    _, lane = grid_of((IP, 128))
    rows = []
    lengths = []
    for h in range(H):
        rows.append(jnp.where(head == h, everything, 0.0))
        lengths.append(-jnp.sum(jnp.where((lane >> log2(PQ)) == h, length, 0.0), axis=1, keepdims=True))
    return jnp.concatenate(rows, axis=0), jnp.concatenate(lengths, axis=0)


def logits_and_values(slots, own, frame, qkv, columns):
    query_rows, lengths = own
    pieces = slots[:, CS:SLOT]
    entry = dot(pieces, piece_select(128, True))
    rows = dot_nt(piece_select(16), pieces)
    keys = dot(slots[:, 0:CS], qkv)
    points = H * PQ
    first = 3 * H * CHEAD + 3 * points
    _, lane = grid_of((keys.shape[0], 128))

    def block(start, size):
        at, offset = start // 128 * 128, start % 128
        one = keys[:, at : at + 128]
        if offset == 0:
            return one
        one = pltpu.roll(one, 128 - offset, 1)
        if offset + size <= 128:
            return one
        return jnp.where(lane < 128 - offset, one, pltpu.roll(keys[:, at + 128 : at + 256], 128 - offset, 1))

    local = []
    for a in range(3):
        value_points = block(first + 3 * points + a * H * PV, H * PV)
        local.append(jnp.concatenate([value_points, block(first + a * points, points)], axis=1))
    placed = []
    for a in range(3):
        placed.append(
            entry[:, 3 * a : 3 * a + 1] * local[0]
            + entry[:, 3 * a + 1 : 3 * a + 2] * local[1]
            + entry[:, 3 * a + 2 : 3 * a + 3] * local[2]
            + entry[:, 9 + a : 10 + a]
        )
    values = jnp.concatenate([keys[:, 384:640]] + [p[:, 0:128] for p in placed], axis=1)
    key_points = [p[:, 128:256] for p in placed]
    length = key_points[0] * key_points[0] + key_points[1] * key_points[1] + key_points[2] * key_points[2]
    key_side = jnp.concatenate([keys[:, 128:384]] + key_points + [length], axis=1)
    far = mask_fill * (rows[MASK_AT : MASK_AT + 1, :] - 1.0)
    chain = jnp.broadcast_to(rows[CHAIN_AT : CHAIN_AT + 1, :], (IP, rows.shape[1]))
    chain = jnp.concatenate([chain - frame[:, CHAIN_AT : CHAIN_AT + 1]] * H, axis=0)
    added = jnp.where(chain == 0.0, columns[:, ROWS + 1 : ROWS + 2], columns[:, ROWS : ROWS + 1]) + far + lengths
    return dot_nt(query_rows, key_side, highest) + added, values


def attend(r, logits, values, halves, state, frame, weights):
    top = jnp.max(logits, axis=1, keepdims=True)
    raised = jnp.exp(logits - top)
    attention = raised / jnp.sum(raised, axis=1, keepdims=True)
    row, _ = grid_of(attention.shape)
    parts = [jnp.where((row & (IP - 1)) == i, attention, 0.0).astype(bf16) for i in range(r)]
    out_pair = dot(jnp.concatenate(parts, axis=1), halves)
    summed = dot(attention, values, highest)
    _, lane = grid_of((IP, 640))
    head = jnp.where(lane < 256, lane >> log2(CHEAD), (lane & 127) >> log2(PV))
    gathered = None
    for h, tile in enumerate(tiles(summed)):
        one = jnp.where(head == h, tile, 0.0)
        gathered = one if gathered is None else gathered + one
    relative = [
        gathered[:, 256 + 128 * a : 256 + 128 * a + H * PV] - frame[:, 9 + a : 10 + a] for a in range(3)
    ]
    out_local = [
        frame[:, a : a + 1] * relative[0]
        + frame[:, 3 + a : 4 + a] * relative[1]
        + frame[:, 6 + a : 7 + a] * relative[2]
        for a in range(3)
    ]
    out_norm = jnp.sqrt(
        out_local[0] * out_local[0] + out_local[1] * out_local[1] + out_local[2] * out_local[2] + 1e-08
    )
    combined = jnp.concatenate(
        [gathered[:, 0 : H * CHEAD]] + out_local + [out_norm] + tiles(out_pair), axis=1
    )
    combined = jnp.concatenate([combined, jnp.zeros_like(combined)], axis=0).astype(bf16)
    out_weight, frame_weight = weights()
    state = layer_norm(state + dot(combined, out_weight)[0:IP])
    update = [jnp.sum(state * frame_weight[e : e + 1], axis=1, keepdims=True) for e in range(6)]
    quat = update[0:3]
    real = lax.rsqrt(1.0 + (quat[0] * quat[0] + quat[1] * quat[1] + quat[2] * quat[2]))
    step = quat_entries(quat[0] * real, quat[1] * real, quat[2] * real, real)
    old = [frame[:, e : e + 1] for e in range(9)]
    columns = []
    for target in range(3):
        for column in range(3):
            columns.append(
                old[target * 3] * step[column]
                + old[target * 3 + 1] * step[3 + column]
                + old[target * 3 + 2] * step[6 + column]
            )
    for target in range(3):
        columns.append(
            frame[:, 9 + target : 10 + target]
            + old[target * 3] * update[3]
            + old[target * 3 + 1] * update[4]
            + old[target * 3 + 2] * update[5]
        )
    _, lane = grid_of((IP, 128))
    for at, column in enumerate(columns):
        frame = jnp.where(lane == at, column, frame)
    return state, frame


def pad_state(single_ref):
    r = single_ref.shape[0]
    return jnp.concatenate([single_ref[...], jnp.zeros((IP - r, CS), f32)], axis=0)


PACK_ROWS = 192
BIAS, POINT_WEIGHT, FRAME_WEIGHT, STATE, FRAME = 0, 128, 136, 160, 184


def wide(pack_ref, first):
    return jnp.concatenate([pack_ref[first + IP * part : first + IP * (part + 1)] for part in range(3)], axis=1)


def own_kernel(
    pair_any, tri_any, qkv_any, single_any, frame_any, columns_any, tri_out_any, bias_weight_any, frame_weight_any,
    gate_ref, rows_ref, pack_ref, pair_copy_any,
    pair_ref, gate_weight_ref, qkv_ref, single_ref, columns_ref, tri_out_ref, bias_weight_ref, frame_weight_ref, sems,
):
    r, count, _ = pair_ref.shape
    frame_ref = pack_ref.at[FRAME : FRAME + IP]
    for copy in copies(
        sems,
        (pair_any, pair_ref),
        (tri_any.at[:, 4 * CH :], gate_weight_ref),
        (qkv_any, qkv_ref),
        (single_any, single_ref),
        (frame_any, frame_ref),
        (columns_any, columns_ref),
        (tri_out_any, tri_out_ref),
        (bias_weight_any, bias_weight_ref),
        (frame_weight_any, frame_weight_ref),
    ):
        copy.wait()
    back = pltpu.make_async_copy(pair_ref, pair_copy_any, sems.at[9])
    back.start()
    gate_ref[r * count :, :] = tri_out_ref[...]
    bias_weight = bias_weight_ref[...]
    spread = [jnp.broadcast_to(bias_weight[h : h + 1], (IP, CH)) for h in range(H)]
    bias_weight = jnp.concatenate(spread + [jnp.zeros((128 - ROWS, CH), f32)], axis=0).T
    _, lane = grid_of((CH, 128))
    pack_ref[BIAS : BIAS + CH, :] = jnp.where(lane < ROWS, bias_weight, columns_ref[0:CH, :])
    pack_ref[POINT_WEIGHT : POINT_WEIGHT + IP, :] = columns_ref[CH : CH + IP, :]
    state = pad_state(single_ref)
    frame_weight = frame_weight_ref[...]
    frame_weight = jnp.concatenate([frame_weight, jnp.zeros((IP - 6, CS), f32)], axis=0)
    for part in range(3):
        lanes = slice(128 * part, 128 * (part + 1))
        pack_ref[FRAME_WEIGHT + IP * part : FRAME_WEIGHT + IP * (part + 1), :] = frame_weight[:, lanes]
        pack_ref[STATE + IP * part : STATE + IP * (part + 1), :] = state[:, lanes]
    rows, lengths = own_side(state, frame_ref[...], qkv_ref, pack_ref[POINT_WEIGHT : POINT_WEIGHT + 1])
    rows_ref[:, 0:768] = rows
    rows_ref[:, 768:896] = jnp.broadcast_to(lengths, (ROWS, 128))
    for i in range(r):
        normed = layer_norm(pair_ref[i]).astype(bf16)
        gate_ref[i * count : (i + 1) * count] = jax.nn.sigmoid(dot(normed, gate_weight_ref[...])).astype(bf16)
    back.wait()


def prepare_kernel(w, n, r, recv_ref, rows_ref, qkv_ref, pack_ref, logits_ref, values_ref):
    slots = natural_rows(recv_ref, 0, w, r, n)
    logits, values = logits_and_values(
        slots, (rows_ref[:, 0:768], rows_ref[:, 768:769]), pack_ref[FRAME : FRAME + IP], qkv_ref[...],
        pack_ref[BIAS : BIAS + ROWS],
    )
    logits_ref[...] = logits
    values_ref[...] = values


def update_kernel(
    w, n, recv_ref, pair_any, gate_ref, logits_ref, values_ref, pack_ref, out_weight_ref,
    pair_out_any, half_ref, bias_ref, state_ref, new_frame_ref, send_ref, pair_ref, sems,
):
    r, count, _ = pair_ref.shape
    load = pltpu.make_async_copy(pair_any, pair_ref, sems.at[0])
    load.start()
    row, column = grid_of((2 * CH, 2 * CH))
    c = row & (CH - 1)
    take = onehot(column == (c >> log2(w)) * 2 * w + (row >> log2(CH)) * w + (c & (w - 1)))
    product = dot(take, recv_ref[...])
    tri_out = gate_ref[r * count :, :]
    updates = []
    for high in range(2):
        normed = layer_norm(product[high * CH : (high + 1) * CH], axis=0).astype(bf16)
        updates.append(dot_tn(normed, tri_out))
    update = jnp.concatenate(updates, axis=0)
    bias_weight = pack_ref[BIAS : BIAS + CH, :]
    _, lane = grid_of((CH, 128))
    bias_weight = jnp.concatenate(
        [jnp.where(((lane & (IP - 1)) == i) & (lane < ROWS), bias_weight, 0.0) for i in range(r)], axis=0
    )
    load.wait()
    pair = pair_ref[...].reshape(r * count, CH)
    pair_out = pair + gate_ref[0 : r * count, :].astype(f32) * update
    pair_ref[...] = pair_out.reshape(r, count, CH)
    store = pltpu.make_async_copy(pair_ref, pair_out_any, sems.at[1])
    store.start()
    normed_pair = layer_norm(pair_out)
    halves = normed_pair.astype(bf16)
    half_ref[...] = halves
    side_by_side = jnp.concatenate([normed_pair[i * count : (i + 1) * count] for i in range(r)], axis=1)
    bias = (dot(side_by_side, bias_weight, highest) * third).T[0:ROWS]
    bias_ref[...] = bias
    state, frame = attend(
        r, logits_ref[...] + bias, values_ref[...], halves, wide(pack_ref, STATE), pack_ref[FRAME : FRAME + IP],
        lambda: (out_weight_ref[...], wide(pack_ref, FRAME_WEIGHT)),
    )
    state_ref[...] = state
    new_frame_ref[...] = frame
    fill_rows(send_ref, 0, spread_rows(slots_of(state, frame), w, r))
    store.wait()


def last_kernel(
    w, n, r, recv_ref, half_ref, bias_ref, state_ref, frame_ref, pack_ref, qkv_ref, out_weight_ref,
    single_out_ref, rotation_ref, translation_ref, scr,
):
    slots = natural_rows(recv_ref, 0, w, r, n)
    state, frame = state_ref[...], frame_ref[...]
    own = own_side(state, frame, qkv_ref, pack_ref[POINT_WEIGHT : POINT_WEIGHT + 1])
    logits, values = logits_and_values(slots, own, frame, qkv_ref[...], pack_ref[BIAS : BIAS + ROWS])
    state, frame = attend(
        r, logits + bias_ref[...], values, half_ref[...], state, frame,
        lambda: (out_weight_ref[...], wide(pack_ref, FRAME_WEIGHT)),
    )
    single_out_ref[...] = state[0:r]
    rotation_ref[...] = frame[0:r, 0:9]
    scr[...] = jnp.concatenate([frame, jnp.zeros((128 - IP, 128), f32)], axis=0).T
    translation_ref[...] = scr[9:12, 0:r]


VMEM = pl.BlockSpec(memory_space=pltpu.VMEM)
HBM = pl.BlockSpec(memory_space=pltpu.HBM)


def call(body, name, outs, args, outside=(), outside_outs=(), scratch=(), limit=32, alias=None, flops=0, moved=0):
    return pl.pallas_call(
        body,
        name=name,
        out_shape=[jax.ShapeDtypeStruct(s, d) for s, d in outs],
        in_specs=[HBM if at in outside else VMEM for at in range(len(args))],
        out_specs=[HBM if at in outside_outs else VMEM for at in range(len(outs))],
        scratch_shapes=list(scratch),
        input_output_aliases=alias or {},
        compiler_params=pltpu.CompilerParams(vmem_limit_bytes=limit * 2**20),
        cost_estimate=pl.CostEstimate(flops=flops, bytes_accessed=moved, transcendentals=0),
    )(*args)


def local(
    pair, single, quats, translate, res_mask, chain_ids, tri_weight, tri_out_weight, qkv_weight, bias_weight,
    head_gamma, chain_bias, out_weight, frame_weight,
):
    n = lax.axis_size("row")
    r, count, _ = pair.shape
    w = CH // n
    rows = 2 * w
    lanes = r * SLOT // rows
    limit = 24 if count == 128 else 56

    def exchange(sent):
        width = sent.shape[1]
        got = lax.all_to_all(sent.reshape(n, rows, width), "row", 0, 0, tiled=True)
        return got.reshape(n * rows, width)

    def like(array):
        return pltpu.VMEM(array.shape, array.dtype)

    dma = pltpu.SemaphoreType.DMA
    sent, frame = call(
        functools.partial(gate_kernel, w, n),
        "gate",
        [((n * rows, r * count + lanes), bf16), ((IP, 128), f32)],
        [pair, tri_weight, single, quats, translate, res_mask, chain_ids],
        outside=range(7),
        scratch=[
            like(pair),
            pltpu.VMEM((CH, 4 * CH), bf16),
            like(single),
            like(quats),
            like(translate),
            pltpu.SMEM((r,), jnp.int32),
            pltpu.SMEM((r,), jnp.int32),
            pltpu.VMEM((128, 128), f32),
            dma((7,)),
        ],
        limit=60,
    )
    received = exchange(sent)

    point_weight = head_gamma * (math.sqrt(2.0 / (9.0 * PQ)) * 0.5 * third)
    columns = jnp.pad(jnp.repeat(chain_bias.T, IP, axis=0), ((0, CH - ROWS + IP), (ROWS, 126 - ROWS)))
    columns = columns.at[CH, 0 : H * PQ].set(jnp.repeat(point_weight, PQ))
    gate, query_rows, pack, pair_copy = call(
        own_kernel,
        "own",
        [
            ((r * count + CH, CH), bf16),
            ((ROWS, 896), f32),
            ((PACK_ROWS, 128), f32),
            (pair.shape, f32),
        ],
        [pair, tri_weight, qkv_weight, single, frame, columns, tri_out_weight, bias_weight.T, frame_weight.T],
        outside=range(9),
        outside_outs=(3,),
        scratch=[
            like(pair),
            pltpu.VMEM((CH, CH), bf16),
            like(qkv_weight),
            like(single),
            like(columns),
            like(tri_out_weight),
            pltpu.VMEM((H, CH), f32),
            pltpu.VMEM((6, CS), f32),
            dma((10,)),
        ],
        limit=60,
        flops=2 * r * count * CH * CH,
        moved=16 * 2**20,
    )
    received, gate, query_rows, pack, pair_copy = lax.optimization_barrier(
        (received, gate, query_rows, pack, pair_copy)
    )
    formed, slots = call(
        functools.partial(product_kernel, w, n, r),
        "product",
        [((n * rows, (r // 2) * count), bf16), ((n * rows, lanes), bf16)],
        [received],
        limit=limit,
    )
    products = exchange(formed)
    logits, values = call(
        functools.partial(prepare_kernel, w, n, r),
        "prepare",
        [((ROWS, count), f32), ((count, 640), f32)],
        [slots, query_rows, qkv_weight, pack],
        limit=limit,
        flops=2 * count * CS * 1152,
        moved=8 * 2**20,
    )
    pair_out, pair_half, bias, state, frame, sent = call(
        functools.partial(update_kernel, w, n),
        "update",
        [
            ((r, count, CH), f32),
            ((r * count, CH), bf16),
            ((ROWS, count), f32),
            ((IP, CS), f32),
            ((IP, 128), f32),
            ((n * rows, lanes), bf16),
        ],
        [products, pair_copy, gate, logits, values, pack, out_weight],
        outside=(1,),
        outside_outs=(0,),
        alias={1: 0},
        scratch=[like(pair), dma((2,))],
        limit=limit,
    )
    received = exchange(sent)
    single_out, rotation, translation = call(
        functools.partial(last_kernel, w, n, r),
        "last",
        [((r, CS), f32), ((r, 9), f32), ((3, r), f32)],
        [received, pair_half, bias, state, frame, pack, qkv_weight, out_weight],
        scratch=[pltpu.VMEM((128, 128), f32)],
        limit=limit,
    )
    return (pair_out, single_out, rotation.T, translation)


def solution(mesh):
    rows = ("grp", "row")
    placed = (P(rows, None, None), P(rows, None), P(None, rows), P(None, rows), P(rows), P(rows)) + (P(),) * 8
    return jax.shard_map(
        local,
        mesh=mesh,
        in_specs=placed,
        out_specs=(P(rows, None, None), P(rows, None), P(None, rows), P(None, rows)),
        check_vma=False,
    )
```

```python
import functools
import math

import jax
import jax.numpy as jnp
from jax import lax
from jax.experimental import pallas as pl
from jax.experimental.pallas import tpu as pltpu
from jax.sharding import PartitionSpec as P

CH = 128
CS = 384
H = 12
CHEAD = 16
PQ = 4
PV = 8
SLOT = 512
IP = 8
ROWS = H * IP
MASK_AT = 12
CHAIN_AT = 13

f32 = jnp.float32
bf16 = jnp.bfloat16
highest = lax.Precision.HIGHEST
epsilon = 1e-05
mask_fill = 100000.0
third = math.sqrt(1.0 / 3.0)


def layer_norm(values, axis=-1):
    center = values - jnp.mean(values, axis=axis, keepdims=True)
    spread = jnp.mean(center * center, axis=axis, keepdims=True)
    return center * lax.rsqrt(spread + epsilon)


def quat_entries(one, two, three, real):
    return [
        1.0 - 2.0 * (two * two + three * three),
        2.0 * (one * two - real * three),
        2.0 * (one * three + real * two),
        2.0 * (one * two + real * three),
        1.0 - 2.0 * (one * one + three * three),
        2.0 * (two * three - real * one),
        2.0 * (one * three - real * two),
        2.0 * (two * three + real * one),
        1.0 - 2.0 * (one * one + two * two),
    ]


def dot(a, b, precision=None):
    return lax.dot_general(
        a, b, (((1,), (0,)), ((), ())), precision=precision, preferred_element_type=f32
    )


def dot_nt(a, b, precision=None):
    return lax.dot_general(
        a, b, (((1,), (1,)), ((), ())), precision=precision, preferred_element_type=f32
    )


def dot_tn(a, b):
    return lax.dot_general(a, b, (((0,), (0,)), ((), ())), preferred_element_type=f32)


def halves_of(x):
    high = x.astype(bf16)
    return high, (x - high.astype(f32)).astype(bf16)


def dot_close(a, b):
    a_high, a_low = halves_of(a)
    b_high, b_low = halves_of(b)
    return dot(jnp.concatenate([a_high, a_low, a_high], axis=1), jnp.concatenate([b_high, b_high, b_low], axis=0))


def sigmoid(x):
    return 0.5 * jnp.tanh(0.5 * x) + 0.5


def log2(number):
    assert number & (number - 1) == 0
    return number.bit_length() - 1


def grid_of(shape):
    return lax.broadcasted_iota(jnp.int32, shape, 0), lax.broadcasted_iota(jnp.int32, shape, 1)


def onehot(match):
    return jnp.where(match, 1.0, 0.0).astype(bf16)


def swap_rows(count, minor_count):
    row, column = grid_of((count, count))
    major_count = count // minor_count
    minor = row >> log2(major_count)
    major = row & (major_count - 1)
    return onehot(column == major * minor_count + minor)


def spread_rows(slots, w, r):
    rows = 2 * w
    lanes = r * SLOT // rows
    if rows == 8 and r == 4:
        low, high = slots[0:IP, 0:lanes].astype(f32), slots[0:IP, lanes:].astype(f32)
        row, _ = grid_of((IP, lanes))
        one = jnp.where(row < r, low, pltpu.roll(high, r, 0))
        return jnp.concatenate([one, one], axis=0).astype(bf16)
    x, i = grid_of((16, 16))
    q = x & (rows - 1)
    if lanes <= SLOT:
        total = None
        for t in range(SLOT // lanes):
            one = dot(onehot((q == t * r + i) & (i < r)), slots[:, t * lanes : (t + 1) * lanes])
            total = one if total is None else total + one
        return total.astype(bf16)
    return jnp.concatenate(
        [dot(onehot(i == t * rows + q), slots) for t in range(lanes // SLOT)], axis=1
    ).astype(bf16)


def natural_rows(x_ref, first, w, r, n, start=0, stop=SLOT):
    rows = 2 * w
    lanes = r * SLOT // rows
    count = n * r
    j, x = grid_of((count, n * rows))
    s = x >> log2(rows)
    q = x & (rows - 1)
    if lanes <= SLOT:
        pieces = []
        for t in range(SLOT // lanes):
            low, high = max(start, t * lanes), min(stop, (t + 1) * lanes)
            if low < high:
                values = x_ref[:, first + low - t * lanes : first + high - t * lanes]
                pieces.append(dot(onehot((j == s * r + q - t * r) & ((q >> log2(r)) == t)), values))
        return (pieces[0] if len(pieces) == 1 else jnp.concatenate(pieces, axis=1)).astype(bf16)
    total = None
    for t in range(lanes // SLOT):
        values = x_ref[:, first + t * SLOT + start : first + t * SLOT + stop]
        one = dot(onehot(j == s * r + t * rows + q), values)
        total = one if total is None else total + one
    return total.astype(bf16)


def frame_pieces(frame):
    high = frame.astype(bf16).astype(f32)
    rest = frame - high
    middle = rest.astype(bf16).astype(f32)
    low = (rest - middle).astype(bf16).astype(f32)
    return high + pltpu.roll(middle, 32, 1) + pltpu.roll(low, 64, 1)


def slots_of(state, frame):
    both = jnp.concatenate([state, frame_pieces(frame)], axis=1)
    return jnp.concatenate([both, jnp.zeros_like(both)], axis=0).astype(bf16)


def fill_rows(out_ref, first, tile):
    lanes = tile.shape[1]
    for t in range(out_ref.shape[0] // 16):
        out_ref[t * 16 : (t + 1) * 16, first : first + lanes] = tile


def piece_select(row_count, transposed=False):
    if transposed:
        lane, entry = grid_of((128, row_count))
    else:
        entry, lane = grid_of((row_count, 128))
    return onehot(((lane & 31) == entry) & (lane < 96))


def copies(sems, *pairs):
    started = [pltpu.make_async_copy(src, dst, sems.at[at]) for at, (src, dst) in enumerate(pairs)]
    for copy in started:
        copy.start()
    return started


def gate_kernel(
    w, n, pair_any, tri_any, single_any, quats_any, translate_any, mask_any, chain_any, send_ref, frame_ref,
    pair_ref, tri_ref, single_ref, quats_ref, translate_ref, mask_ref, chain_ref, scr, sems,
):
    r, count, _ = pair_ref.shape
    loads = copies(
        sems,
        (quats_any, quats_ref),
        (translate_any, translate_ref),
        (mask_any, mask_ref),
        (chain_any, chain_ref),
        (single_any, single_ref),
        (tri_any.at[:, 0 : 4 * CH], tri_ref),
        (pair_any, pair_ref),
    )
    row, column = grid_of((2 * CH, 2 * CH))
    d = row >> log2(2 * w)
    side = (row >> log2(w)) & 1
    take = onehot(column == side * CH + d * w + (row & (w - 1)))
    for load in loads:
        load.wait()
    gate_weight = jnp.concatenate([tri_ref[:, 0:CH], tri_ref[:, 2 * CH : 3 * CH]], axis=1)
    value_weight = jnp.concatenate([tri_ref[:, CH : 2 * CH], tri_ref[:, 3 * CH : 4 * CH]], axis=1)
    gate_weight = dot_nt(take, gate_weight).astype(bf16)
    value_weight = dot_nt(take, value_weight).astype(bf16)
    normed = layer_norm(pair_ref[...].reshape(r * count, CH)).astype(bf16)
    gates = dot_nt(gate_weight, normed)
    values = dot_nt(value_weight, normed)
    mask = jnp.concatenate([jnp.full((1, count), mask_ref[i].astype(f32)) for i in range(r)], axis=1)
    send_ref[:, 0 : r * count] = (sigmoid(gates) * values * mask).astype(bf16)

    scr[...] = jnp.zeros_like(scr)
    quats = quats_ref[...]
    real = lax.rsqrt(1.0 + jnp.sum(quats * quats, axis=0, keepdims=True))
    unit = quats * real
    entries = quat_entries(unit[0:1], unit[1:2], unit[2:3], real)
    for at, entry in enumerate(entries):
        scr[at : at + 1, 0:r] = entry
    scr[9:12, 0:r] = translate_ref[...]
    frame = scr[...].T[0:IP, :]
    row, lane = grid_of((IP, 128))
    for i in range(r):
        frame = jnp.where((row == i) & (lane == MASK_AT), mask_ref[i].astype(f32), frame)
        frame = jnp.where((row == i) & (lane == CHAIN_AT), chain_ref[i].astype(f32), frame)
    frame_ref[...] = frame
    fill_rows(send_ref, r * count, spread_rows(slots_of(pad_state(single_ref), frame), w, r))


def product_kernel(w, n, r, recv_ref, send_ref, slots_ref):
    count = n * r
    slots_ref[...] = recv_ref[:, r * count :]
    rows = 2 * w
    pieces = natural_rows(recv_ref, r * count, w, r, n, CS, SLOT)
    mask = dot_nt(piece_select(16), pieces)[MASK_AT : MASK_AT + 1, :]
    mask = jnp.concatenate([mask] * r, axis=1)
    order = swap_rows(n * rows, rows)
    sides = (dot(order, recv_ref[:, 0 : r * count]) * mask).astype(bf16)
    row, column = grid_of((count, count))
    to_natural = onehot(row == (column & (n - 1)) * r + (column >> log2(n)))

    def stacked(block):
        part = sides[block * n : (block + 1) * n]
        return jnp.concatenate([part[:, i * count : (i + 1) * count] for i in range(r)], axis=0)

    half = r // 2
    products = []
    for c in range(w):
        right = dot(to_natural, stacked(w + c)).astype(bf16)
        products.append(dot_nt(stacked(c), right).astype(bf16))
    blocks = []
    for high in range(2):
        for c in range(w):
            first = high * half
            blocks.append(
                jnp.concatenate(
                    [products[c][(first + low) * n : (first + low + 1) * n] for low in range(half)], axis=1
                )
            )
    send_ref[...] = dot(swap_rows(n * rows, n), jnp.concatenate(blocks, axis=0)).astype(bf16)


def tiles(x):
    return [x[h * IP : (h + 1) * IP] for h in range(H)]


def own_side(state, frame, qkv_ref, point_weight):
    both = jnp.concatenate([state, jnp.zeros_like(state)], axis=0).astype(bf16)
    own = dot(both, jnp.concatenate([qkv_ref[:, 0:256], qkv_ref[:, 512:768]], axis=1))[0:IP]
    width = H * CHEAD
    count = H * PQ
    start = 3 * width - 256
    fill = jnp.zeros((IP, 128 - count), f32)
    own_local = [jnp.concatenate([own[:, start + a * count : start + (a + 1) * count], fill], axis=1) for a in range(3)]
    scalars = jnp.concatenate([jnp.zeros((IP, 256 - width), f32), own[:, 0:width]], axis=1)
    points = []
    for a in range(3):
        points.append(
            frame[:, 3 * a : 3 * a + 1] * own_local[0]
            + frame[:, 3 * a + 1 : 3 * a + 2] * own_local[1]
            + frame[:, 3 * a + 2 : 3 * a + 3] * own_local[2]
            + frame[:, 9 + a : 10 + a]
        )
    weight = jnp.broadcast_to(point_weight, (IP, 128))
    length = weight * (points[0] * points[0] + points[1] * points[1] + points[2] * points[2])
    everything = jnp.concatenate(
        [scalars * (third / math.sqrt(CHEAD))] + [2.0 * weight * p for p in points] + [-weight], axis=1
    )
    _, lane = grid_of((IP, 768))
    head = jnp.where(lane < 256, (lane - (256 - width)) >> log2(CHEAD), (lane & 127) >> log2(PQ))
    _, lane = grid_of((IP, 128))
    rows = []
    lengths = []
    for h in range(H):
        rows.append(jnp.where(head == h, everything, 0.0))
        lengths.append(-jnp.sum(jnp.where((lane >> log2(PQ)) == h, length, 0.0), axis=1, keepdims=True))
    return jnp.concatenate(rows, axis=0), jnp.concatenate(lengths, axis=0)


def logits_and_values(slots, own, frame, qkv, columns):
    query_rows, lengths = own
    pieces = slots[:, CS:SLOT]
    entry = dot(pieces, piece_select(128, True))
    rows = dot_nt(piece_select(16), pieces)
    keys = dot(slots[:, 0:CS], qkv)
    points = H * PQ
    first = 3 * H * CHEAD + 3 * points
    _, lane = grid_of((keys.shape[0], 128))

    def block(start, size):
        at, offset = start // 128 * 128, start % 128
        one = keys[:, at : at + 128]
        if offset == 0:
            return one
        one = pltpu.roll(one, 128 - offset, 1)
        if offset + size <= 128:
            return one
        return jnp.where(lane < 128 - offset, one, pltpu.roll(keys[:, at + 128 : at + 256], 128 - offset, 1))

    local = []
    for a in range(3):
        value_points = block(first + 3 * points + a * H * PV, H * PV)
        local.append(jnp.concatenate([value_points, block(first + a * points, points)], axis=1))
    placed = []
    for a in range(3):
        placed.append(
            entry[:, 3 * a : 3 * a + 1] * local[0]
            + entry[:, 3 * a + 1 : 3 * a + 2] * local[1]
            + entry[:, 3 * a + 2 : 3 * a + 3] * local[2]
            + entry[:, 9 + a : 10 + a]
        )
    values = jnp.concatenate([keys[:, 384:640]] + [p[:, 0:128] for p in placed], axis=1)
    key_points = [p[:, 128:256] for p in placed]
    length = key_points[0] * key_points[0] + key_points[1] * key_points[1] + key_points[2] * key_points[2]
    key_side = jnp.concatenate([keys[:, 128:384]] + key_points + [length], axis=1)
    far = mask_fill * (rows[MASK_AT : MASK_AT + 1, :] - 1.0)
    chain = jnp.broadcast_to(rows[CHAIN_AT : CHAIN_AT + 1, :], (IP, rows.shape[1]))
    chain = jnp.concatenate([chain - frame[:, CHAIN_AT : CHAIN_AT + 1]] * H, axis=0)
    added = jnp.where(chain == 0.0, columns[:, ROWS + 1 : ROWS + 2], columns[:, ROWS : ROWS + 1]) + far + lengths
    return dot_nt(query_rows, key_side, highest) + added, values


def attend(r, logits, values, halves, state, frame, weights):
    top = jnp.max(logits, axis=1, keepdims=True)
    raised = jnp.exp(logits - top)
    attention = raised / jnp.sum(raised, axis=1, keepdims=True)
    row, _ = grid_of(attention.shape)
    parts = [jnp.where((row & (IP - 1)) == i, attention, 0.0).astype(bf16) for i in range(r)]
    out_pair = dot(jnp.concatenate(parts, axis=1), halves)
    summed = dot_close(attention, values)
    _, lane = grid_of((IP, 640))
    head = jnp.where(lane < 256, lane >> log2(CHEAD), (lane & 127) >> log2(PV))
    gathered = None
    for h, tile in enumerate(tiles(summed)):
        one = jnp.where(head == h, tile, 0.0)
        gathered = one if gathered is None else gathered + one
    relative = [
        gathered[:, 256 + 128 * a : 256 + 128 * a + H * PV] - frame[:, 9 + a : 10 + a] for a in range(3)
    ]
    out_local = [
        frame[:, a : a + 1] * relative[0]
        + frame[:, 3 + a : 4 + a] * relative[1]
        + frame[:, 6 + a : 7 + a] * relative[2]
        for a in range(3)
    ]
    out_norm = jnp.sqrt(
        out_local[0] * out_local[0] + out_local[1] * out_local[1] + out_local[2] * out_local[2] + 1e-08
    )
    out_ref, frame_weight = weights()

    def projected(blocks, first):
        rows = jnp.concatenate(blocks, axis=1)
        rows = jnp.concatenate([rows, jnp.zeros_like(rows)], axis=0).astype(bf16)
        return dot(rows, out_ref[first : first + rows.shape[1], :])[0:IP]

    from_pair = projected(tiles(out_pair), H * (CHEAD + 4 * PV))
    from_points = projected([gathered[:, 0 : H * CHEAD]] + out_local + [out_norm], 0)
    state = layer_norm(state + (from_points + from_pair))
    update = [jnp.sum(state * frame_weight[e : e + 1], axis=1, keepdims=True) for e in range(6)]
    quat = update[0:3]
    real = lax.rsqrt(1.0 + (quat[0] * quat[0] + quat[1] * quat[1] + quat[2] * quat[2]))
    step = quat_entries(quat[0] * real, quat[1] * real, quat[2] * real, real)
    old = [frame[:, e : e + 1] for e in range(9)]
    columns = []
    for target in range(3):
        for column in range(3):
            columns.append(
                old[target * 3] * step[column]
                + old[target * 3 + 1] * step[3 + column]
                + old[target * 3 + 2] * step[6 + column]
            )
    for target in range(3):
        columns.append(
            frame[:, 9 + target : 10 + target]
            + old[target * 3] * update[3]
            + old[target * 3 + 1] * update[4]
            + old[target * 3 + 2] * update[5]
        )
    _, lane = grid_of((IP, 128))
    for at, column in enumerate(columns):
        frame = jnp.where(lane == at, column, frame)
    return state, frame


def pad_state(single_ref):
    r = single_ref.shape[0]
    return jnp.concatenate([single_ref[...], jnp.zeros((IP - r, CS), f32)], axis=0)


PACK_ROWS = 192
BIAS, POINT_WEIGHT, FRAME_WEIGHT, STATE, FRAME = 0, 128, 136, 160, 184


def wide(pack_ref, first):
    return jnp.concatenate([pack_ref[first + IP * part : first + IP * (part + 1)] for part in range(3)], axis=1)


def own_kernel(
    pair_any, tri_any, qkv_any, single_any, frame_any, columns_any, tri_out_any, bias_weight_any, frame_weight_any,
    gate_ref, rows_ref, pack_ref, pair_copy_any,
    pair_ref, gate_weight_ref, qkv_ref, single_ref, columns_ref, tri_out_ref, bias_weight_ref, frame_weight_ref, sems,
):
    r, count, _ = pair_ref.shape
    frame_ref = pack_ref.at[FRAME : FRAME + IP]
    for copy in copies(
        sems,
        (pair_any, pair_ref),
        (tri_any.at[:, 4 * CH :], gate_weight_ref),
        (qkv_any, qkv_ref),
        (single_any, single_ref),
        (frame_any, frame_ref),
        (columns_any, columns_ref),
        (tri_out_any, tri_out_ref),
        (bias_weight_any, bias_weight_ref),
        (frame_weight_any, frame_weight_ref),
    ):
        copy.wait()
    back = pltpu.make_async_copy(pair_ref, pair_copy_any, sems.at[9])
    back.start()
    gate_ref[r * count :, :] = tri_out_ref[...]
    bias_weight = bias_weight_ref[...]
    spread = [jnp.broadcast_to(bias_weight[h : h + 1], (IP, CH)) for h in range(H)]
    bias_weight = jnp.concatenate(spread + [jnp.zeros((128 - ROWS, CH), f32)], axis=0).T
    _, lane = grid_of((CH, 128))
    pack_ref[BIAS : BIAS + CH, :] = jnp.where(lane < ROWS, bias_weight, columns_ref[0:CH, :])
    pack_ref[POINT_WEIGHT : POINT_WEIGHT + IP, :] = columns_ref[CH : CH + IP, :]
    state = pad_state(single_ref)
    frame_weight = frame_weight_ref[...]
    frame_weight = jnp.concatenate([frame_weight, jnp.zeros((IP - 6, CS), f32)], axis=0)
    for part in range(3):
        lanes = slice(128 * part, 128 * (part + 1))
        pack_ref[FRAME_WEIGHT + IP * part : FRAME_WEIGHT + IP * (part + 1), :] = frame_weight[:, lanes]
        pack_ref[STATE + IP * part : STATE + IP * (part + 1), :] = state[:, lanes]
    rows, lengths = own_side(state, frame_ref[...], qkv_ref, pack_ref[POINT_WEIGHT : POINT_WEIGHT + 1])
    rows_ref[:, 0:768] = rows
    rows_ref[:, 768:896] = jnp.broadcast_to(lengths, (ROWS, 128))
    for i in range(r):
        normed = layer_norm(pair_ref[i]).astype(bf16)
        gate_ref[i * count : (i + 1) * count] = jax.nn.sigmoid(dot(normed, gate_weight_ref[...])).astype(bf16)
    back.wait()


def prepare_kernel(w, n, r, recv_ref, rows_ref, qkv_ref, pack_ref, logits_ref, values_ref):
    slots = natural_rows(recv_ref, 0, w, r, n)
    logits, values = logits_and_values(
        slots, (rows_ref[:, 0:768], rows_ref[:, 768:769]), pack_ref[FRAME : FRAME + IP], qkv_ref[...],
        pack_ref[BIAS : BIAS + ROWS],
    )
    logits_ref[...] = logits
    values_ref[...] = values


def update_kernel(
    w, n, recv_ref, pair_any, gate_ref, logits_ref, values_ref, pack_ref, out_weight_ref,
    pair_out_any, half_ref, bias_ref, state_ref, new_frame_ref, send_ref, pair_ref, sems,
):
    r, count, _ = pair_ref.shape
    load = pltpu.make_async_copy(pair_any, pair_ref, sems.at[0])
    load.start()
    row, column = grid_of((2 * CH, 2 * CH))
    c = row & (CH - 1)
    take = onehot(column == (c >> log2(w)) * 2 * w + (row >> log2(CH)) * w + (c & (w - 1)))
    product = dot(take, recv_ref[...])
    tri_out = gate_ref[r * count :, :]
    updates = []
    for high in range(2):
        normed = layer_norm(product[high * CH : (high + 1) * CH], axis=0).astype(bf16)
        updates.append(dot_tn(normed, tri_out))
    update = jnp.concatenate(updates, axis=0)
    bias_weight = pack_ref[BIAS : BIAS + CH, :]
    _, lane = grid_of((CH, 128))
    bias_weight = jnp.concatenate(
        [jnp.where(((lane & (IP - 1)) == i) & (lane < ROWS), bias_weight, 0.0) for i in range(r)], axis=0
    )
    load.wait()
    pair = pair_ref[...].reshape(r * count, CH)
    pair_out = pair + gate_ref[0 : r * count, :].astype(f32) * update
    pair_ref[...] = pair_out.reshape(r, count, CH)
    store = pltpu.make_async_copy(pair_ref, pair_out_any, sems.at[1])
    store.start()
    normed_pair = layer_norm(pair_out)
    halves = normed_pair.astype(bf16)
    half_ref[...] = halves
    side_by_side = jnp.concatenate([normed_pair[i * count : (i + 1) * count] for i in range(r)], axis=1)
    bias = (dot_close(side_by_side, bias_weight) * third).T[0:ROWS]
    bias_ref[...] = bias
    state, frame = attend(
        r, logits_ref[...] + bias, values_ref[...], halves, wide(pack_ref, STATE), pack_ref[FRAME : FRAME + IP],
        lambda: (out_weight_ref, wide(pack_ref, FRAME_WEIGHT)),
    )
    state_ref[...] = state
    new_frame_ref[...] = frame
    fill_rows(send_ref, 0, spread_rows(slots_of(state, frame), w, r))
    store.wait()


def last_kernel(
    w, n, r, recv_ref, half_ref, bias_ref, state_ref, frame_ref, pack_ref, qkv_ref, out_weight_ref,
    single_out_ref, rotation_ref, translation_ref, scr,
):
    slots = natural_rows(recv_ref, 0, w, r, n)
    state, frame = state_ref[...], frame_ref[...]
    own = own_side(state, frame, qkv_ref, pack_ref[POINT_WEIGHT : POINT_WEIGHT + 1])
    logits, values = logits_and_values(slots, own, frame, qkv_ref[...], pack_ref[BIAS : BIAS + ROWS])
    state, frame = attend(
        r, logits + bias_ref[...], values, half_ref[...], state, frame,
        lambda: (out_weight_ref, wide(pack_ref, FRAME_WEIGHT)),
    )
    single_out_ref[...] = state[0:r]
    rotation_ref[...] = frame[0:r, 0:9]
    scr[...] = jnp.concatenate([frame, jnp.zeros((128 - IP, 128), f32)], axis=0).T
    translation_ref[...] = scr[9:12, 0:r]


VMEM = pl.BlockSpec(memory_space=pltpu.VMEM)
HBM = pl.BlockSpec(memory_space=pltpu.HBM)


def call(body, name, outs, args, outside=(), outside_outs=(), scratch=(), limit=32, alias=None, flops=0, moved=0):
    return pl.pallas_call(
        body,
        name=name,
        out_shape=[jax.ShapeDtypeStruct(s, d) for s, d in outs],
        in_specs=[HBM if at in outside else VMEM for at in range(len(args))],
        out_specs=[HBM if at in outside_outs else VMEM for at in range(len(outs))],
        scratch_shapes=list(scratch),
        input_output_aliases=alias or {},
        compiler_params=pltpu.CompilerParams(vmem_limit_bytes=limit * 2**20),
        cost_estimate=pl.CostEstimate(flops=flops, bytes_accessed=moved, transcendentals=0),
    )(*args)


def local(
    pair, single, quats, translate, res_mask, chain_ids, tri_weight, tri_out_weight, qkv_weight, bias_weight,
    head_gamma, chain_bias, out_weight, frame_weight,
):
    n = lax.axis_size("row")
    r, count, _ = pair.shape
    w = CH // n
    rows = 2 * w
    lanes = r * SLOT // rows
    limit = 24 if count == 128 else 56

    def exchange(sent):
        width = sent.shape[1]
        got = lax.all_to_all(sent.reshape(n, rows, width), "row", 0, 0, tiled=True)
        return got.reshape(n * rows, width)

    def like(array):
        return pltpu.VMEM(array.shape, array.dtype)

    dma = pltpu.SemaphoreType.DMA
    sent, frame = call(
        functools.partial(gate_kernel, w, n),
        "gate",
        [((n * rows, r * count + lanes), bf16), ((IP, 128), f32)],
        [pair, tri_weight, single, quats, translate, res_mask, chain_ids],
        outside=range(7),
        scratch=[
            like(pair),
            pltpu.VMEM((CH, 4 * CH), bf16),
            like(single),
            like(quats),
            like(translate),
            pltpu.SMEM((r,), jnp.int32),
            pltpu.SMEM((r,), jnp.int32),
            pltpu.VMEM((128, 128), f32),
            dma((7,)),
        ],
        limit=60,
    )
    received = exchange(sent)

    point_weight = head_gamma * (math.sqrt(2.0 / (9.0 * PQ)) * 0.5 * third)
    columns = jnp.pad(jnp.repeat(chain_bias.T, IP, axis=0), ((0, CH - ROWS + IP), (ROWS, 126 - ROWS)))
    columns = columns.at[CH, 0 : H * PQ].set(jnp.repeat(point_weight, PQ))
    gate, query_rows, pack, pair_copy = call(
        own_kernel,
        "own",
        [
            ((r * count + CH, CH), bf16),
            ((ROWS, 896), f32),
            ((PACK_ROWS, 128), f32),
            (pair.shape, f32),
        ],
        [pair, tri_weight, qkv_weight, single, frame, columns, tri_out_weight, bias_weight.T, frame_weight.T],
        outside=range(9),
        outside_outs=(3,),
        scratch=[
            like(pair),
            pltpu.VMEM((CH, CH), bf16),
            like(qkv_weight),
            like(single),
            like(columns),
            like(tri_out_weight),
            pltpu.VMEM((H, CH), f32),
            pltpu.VMEM((6, CS), f32),
            dma((10,)),
        ],
        limit=60,
        flops=2 * r * count * CH * CH,
        moved=16 * 2**20,
    )
    received, gate, query_rows, pack, pair_copy = lax.optimization_barrier(
        (received, gate, query_rows, pack, pair_copy)
    )
    formed, slots = call(
        functools.partial(product_kernel, w, n, r),
        "product",
        [((n * rows, (r // 2) * count), bf16), ((n * rows, lanes), bf16)],
        [received],
        limit=limit,
    )
    products = exchange(formed)
    logits, values = call(
        functools.partial(prepare_kernel, w, n, r),
        "prepare",
        [((ROWS, count), f32), ((count, 640), f32)],
        [slots, query_rows, qkv_weight, pack],
        limit=limit,
        flops=2 * count * CS * 1152,
        moved=8 * 2**20,
    )
    pair_out, pair_half, bias, state, frame, sent = call(
        functools.partial(update_kernel, w, n),
        "update",
        [
            ((r, count, CH), f32),
            ((r * count, CH), bf16),
            ((ROWS, count), f32),
            ((IP, CS), f32),
            ((IP, 128), f32),
            ((n * rows, lanes), bf16),
        ],
        [products, pair_copy, gate, logits, values, pack, out_weight],
        outside=(1,),
        outside_outs=(0,),
        alias={1: 0},
        scratch=[like(pair), dma((2,))],
        limit=limit,
    )
    received = exchange(sent)
    single_out, rotation, translation = call(
        functools.partial(last_kernel, w, n, r),
        "last",
        [((r, CS), f32), ((r, 9), f32), ((3, r), f32)],
        [received, pair_half, bias, state, frame, pack, qkv_weight, out_weight],
        scratch=[pltpu.VMEM((128, 128), f32)],
        limit=limit,
    )
    return (pair_out, single_out, rotation.T, translation)


def solution(mesh):
    rows = ("grp", "row")
    placed = (P(rows, None, None), P(rows, None), P(None, rows), P(None, rows), P(rows), P(rows)) + (P(),) * 8
    return jax.shard_map(
        local,
        mesh=mesh,
        in_specs=placed,
        out_specs=(P(rows, None, None), P(rows, None), P(None, rows), P(None, rows)),
        check_vma=False,
    )
```

```python
import functools
import math

import jax
import jax.numpy as jnp
from jax import lax
from jax.experimental import pallas as pl
from jax.experimental.pallas import tpu as pltpu
from jax.sharding import PartitionSpec as P

CH = 128
CS = 384
H = 12
CHEAD = 16
PQ = 4
PV = 8
SLOT = 512
IP = 8
ROWS = H * IP
MASK_AT = 12
CHAIN_AT = 13

f32 = jnp.float32
bf16 = jnp.bfloat16
highest = lax.Precision.HIGHEST
epsilon = 1e-05
mask_fill = 100000.0
third = math.sqrt(1.0 / 3.0)


def layer_norm(values, axis=-1):
    center = values - jnp.mean(values, axis=axis, keepdims=True)
    spread = jnp.mean(center * center, axis=axis, keepdims=True)
    return center * lax.rsqrt(spread + epsilon)


def quat_entries(one, two, three, real):
    return [
        1.0 - 2.0 * (two * two + three * three),
        2.0 * (one * two - real * three),
        2.0 * (one * three + real * two),
        2.0 * (one * two + real * three),
        1.0 - 2.0 * (one * one + three * three),
        2.0 * (two * three - real * one),
        2.0 * (one * three - real * two),
        2.0 * (two * three + real * one),
        1.0 - 2.0 * (one * one + two * two),
    ]


def dot(a, b, precision=None):
    return lax.dot_general(
        a, b, (((1,), (0,)), ((), ())), precision=precision, preferred_element_type=f32
    )


def dot_nt(a, b, precision=None):
    return lax.dot_general(
        a, b, (((1,), (1,)), ((), ())), precision=precision, preferred_element_type=f32
    )


def dot_tn(a, b):
    return lax.dot_general(a, b, (((0,), (0,)), ((), ())), preferred_element_type=f32)


def halves_of(x):
    high = x.astype(bf16)
    return high, (x - high.astype(f32)).astype(bf16)


def dot_close(a, b):
    a_high, a_low = halves_of(a)
    b_high, b_low = halves_of(b)
    return dot(jnp.concatenate([a_high, a_low, a_high], axis=1), jnp.concatenate([b_high, b_high, b_low], axis=0))


def sigmoid(x):
    return 0.5 * jnp.tanh(0.5 * x) + 0.5


def log2(number):
    assert number & (number - 1) == 0
    return number.bit_length() - 1


def grid_of(shape):
    return lax.broadcasted_iota(jnp.int32, shape, 0), lax.broadcasted_iota(jnp.int32, shape, 1)


def onehot(match):
    return jnp.where(match, 1.0, 0.0).astype(bf16)


def swap_rows(count, minor_count):
    row, column = grid_of((count, count))
    major_count = count // minor_count
    minor = row >> log2(major_count)
    major = row & (major_count - 1)
    return onehot(column == major * minor_count + minor)


def spread_rows(slots, w, r):
    rows = 2 * w
    lanes = r * SLOT // rows
    if rows == 8 and r == 4:
        low, high = slots[0:IP, 0:lanes].astype(f32), slots[0:IP, lanes:].astype(f32)
        row, _ = grid_of((IP, lanes))
        one = jnp.where(row < r, low, pltpu.roll(high, r, 0))
        return jnp.concatenate([one, one], axis=0).astype(bf16)
    x, i = grid_of((16, 16))
    q = x & (rows - 1)
    if lanes <= SLOT:
        total = None
        for t in range(SLOT // lanes):
            one = dot(onehot((q == t * r + i) & (i < r)), slots[:, t * lanes : (t + 1) * lanes])
            total = one if total is None else total + one
        return total.astype(bf16)
    return jnp.concatenate(
        [dot(onehot(i == t * rows + q), slots) for t in range(lanes // SLOT)], axis=1
    ).astype(bf16)


def natural_rows(x_ref, first, w, r, n, start=0, stop=SLOT):
    rows = 2 * w
    lanes = r * SLOT // rows
    count = n * r
    j, x = grid_of((count, n * rows))
    s = x >> log2(rows)
    q = x & (rows - 1)
    if lanes <= SLOT:
        pieces = []
        for t in range(SLOT // lanes):
            low, high = max(start, t * lanes), min(stop, (t + 1) * lanes)
            if low < high:
                values = x_ref[:, first + low - t * lanes : first + high - t * lanes]
                pieces.append(dot(onehot((j == s * r + q - t * r) & ((q >> log2(r)) == t)), values))
        return pieces[0] if len(pieces) == 1 else jnp.concatenate(pieces, axis=1)
    total = None
    for t in range(lanes // SLOT):
        values = x_ref[:, first + t * SLOT + start : first + t * SLOT + stop]
        one = dot(onehot(j == s * r + t * rows + q), values)
        total = one if total is None else total + one
    return total


def frame_pieces(frame):
    high = frame.astype(bf16).astype(f32)
    rest = frame - high
    middle = rest.astype(bf16).astype(f32)
    low = (rest - middle).astype(bf16).astype(f32)
    return high + pltpu.roll(middle, 32, 1) + pltpu.roll(low, 64, 1)


def slots_of(state, frame):
    _, lane = grid_of((IP, 128))
    tail = state[:, 256:CS]
    mask = jnp.where(lane == 127, frame[:, MASK_AT : MASK_AT + 1], 0.0)
    moved = jnp.where((lane >= 112) & (lane < 120), pltpu.roll(tail, 120, 1), mask)
    last = jnp.where(lane < 96, frame_pieces(frame), moved)
    both = jnp.concatenate([state[:, 0:256], jnp.where(lane < 120, tail, mask), last], axis=1)
    return jnp.concatenate([both, jnp.zeros_like(both)], axis=0).astype(bf16)


def state_of(slots):
    _, lane = grid_of((slots.shape[0], 128))
    tail = jnp.where(lane < 120, slots[:, 256:384], pltpu.roll(slots[:, 384:512], 8, 1))
    return jnp.concatenate([slots[:, 0:256], tail], axis=1).astype(bf16)


def half_rows(slots, w, r):
    rows = 2 * w
    x, i = grid_of((16, 16))
    parity = (x >> log2(rows)) & 1
    blocks = []
    for at in range(2 * r // rows):
        b = (x & (rows - 1)) * (2 * r // rows) + at
        total = None
        for quarter in range(4):
            take = onehot((i == (b & (r - 1))) & (parity + 2 * (b >> log2(r)) == quarter))
            one = dot(take, slots[:, quarter * 128 : (quarter + 1) * 128])
            total = one if total is None else total + one
        blocks.append(total)
    return (blocks[0] if len(blocks) == 1 else jnp.concatenate(blocks, axis=1)).astype(bf16)


def quarter_of(x, first, second, w, r, n):
    rows = 2 * w
    j, row = grid_of((n * r, n * rows))
    total = None
    for at in range(2 * r // rows):
        b = (row & (rows - 1)) * (2 * r // rows) + at
        take = onehot((j == (row >> log2(rows)) * r + (b & (r - 1))) & ((b >> log2(r)) == second))
        one = dot(take, x[:, first + at * 128 : first + (at + 1) * 128])
        total = one if total is None else total + one
    return total


def fill_rows(out_ref, first, tile):
    lanes = tile.shape[1]
    for t in range(out_ref.shape[0] // 16):
        out_ref[t * 16 : (t + 1) * 16, first : first + lanes] = tile


def piece_select(row_count, transposed=False):
    if transposed:
        lane, entry = grid_of((128, row_count))
    else:
        entry, lane = grid_of((row_count, 128))
    return onehot(((lane & 31) == entry) & (lane < 96))


def copies(sems, *pairs):
    started = [pltpu.make_async_copy(src, dst, sems.at[at]) for at, (src, dst) in enumerate(pairs)]
    for copy in started:
        copy.start()
    return started


def gate_kernel(
    w, n, pair_any, tri_any, single_any, quats_any, translate_any, mask_any, chain_any, send_ref, frame_ref,
    pair_ref, tri_ref, single_ref, quats_ref, translate_ref, mask_ref, chain_ref, scr, sems,
):
    r, count, _ = pair_ref.shape
    loads = copies(
        sems,
        (quats_any, quats_ref),
        (translate_any, translate_ref),
        (mask_any, mask_ref),
        (chain_any, chain_ref),
        (single_any, single_ref),
        (tri_any.at[:, 0 : 4 * CH], tri_ref),
        (pair_any, pair_ref),
    )
    row, column = grid_of((2 * CH, 2 * CH))
    d = row >> log2(2 * w)
    side = (row >> log2(w)) & 1
    take = onehot(column == side * CH + d * w + (row & (w - 1)))
    for load in loads:
        load.wait()
    gate_weight = jnp.concatenate([tri_ref[:, 0:CH], tri_ref[:, 2 * CH : 3 * CH]], axis=1)
    value_weight = jnp.concatenate([tri_ref[:, CH : 2 * CH], tri_ref[:, 3 * CH : 4 * CH]], axis=1)
    gate_weight = dot_nt(take, gate_weight).astype(bf16)
    value_weight = dot_nt(take, value_weight).astype(bf16)
    normed = layer_norm(pair_ref[...].reshape(r * count, CH)).astype(bf16)
    gates = dot_nt(gate_weight, normed)
    values = dot_nt(value_weight, normed)
    mask = jnp.concatenate([jnp.full((1, count), mask_ref[i].astype(f32)) for i in range(r)], axis=1)
    send_ref[:, 0 : r * count] = (sigmoid(gates) * values * mask).astype(bf16)

    scr[...] = jnp.zeros_like(scr)
    quats = quats_ref[...]
    real = lax.rsqrt(1.0 + jnp.sum(quats * quats, axis=0, keepdims=True))
    unit = quats * real
    entries = quat_entries(unit[0:1], unit[1:2], unit[2:3], real)
    for at, entry in enumerate(entries):
        scr[at : at + 1, 0:r] = entry
    scr[9:12, 0:r] = translate_ref[...]
    frame = scr[...].T[0:IP, :]
    row, lane = grid_of((IP, 128))
    for i in range(r):
        frame = jnp.where((row == i) & (lane == MASK_AT), mask_ref[i].astype(f32), frame)
        frame = jnp.where((row == i) & (lane == CHAIN_AT), chain_ref[i].astype(f32), frame)
    frame_ref[...] = frame
    fill_rows(send_ref, r * count, half_rows(slots_of(pad_state(single_ref), frame), w, r))


def product_kernel(w, n, r, recv_ref, send_ref, slots_ref):
    count = n * r
    slots_ref[...] = recv_ref[:, r * count :]
    rows = 2 * w
    pieces = quarter_of(recv_ref, r * count, 1, w, r, n).astype(bf16)
    _, lane = grid_of((16, 128))
    mask = dot_nt(onehot(lane == 127), pieces)[0:1, :]
    mask = jnp.concatenate([mask] * r, axis=1)
    order = swap_rows(n * rows, rows)
    sides = (dot(order, recv_ref[:, 0 : r * count]) * mask).astype(bf16)
    row, column = grid_of((count, count))
    to_natural = onehot(row == (column & (n - 1)) * r + (column >> log2(n)))

    def stacked(block):
        part = sides[block * n : (block + 1) * n]
        return jnp.concatenate([part[:, i * count : (i + 1) * count] for i in range(r)], axis=0)

    half = r // 2
    products = []
    for c in range(w):
        right = dot(to_natural, stacked(w + c)).astype(bf16)
        products.append(dot_nt(stacked(c), right).astype(bf16))
    blocks = []
    for high in range(2):
        for c in range(w):
            first = high * half
            blocks.append(
                jnp.concatenate(
                    [products[c][(first + low) * n : (first + low + 1) * n] for low in range(half)], axis=1
                )
            )
    send_ref[...] = dot(swap_rows(n * rows, n), jnp.concatenate(blocks, axis=0)).astype(bf16)


def tiles(x):
    return [x[h * IP : (h + 1) * IP] for h in range(H)]


def own_side(state, frame, qkv_ref, point_weight):
    both = jnp.concatenate([state, jnp.zeros_like(state)], axis=0).astype(bf16)
    own = dot(both, jnp.concatenate([qkv_ref[:, 0:256], qkv_ref[:, 512:768]], axis=1))[0:IP]
    width = H * CHEAD
    count = H * PQ
    start = 3 * width - 256
    fill = jnp.zeros((IP, 128 - count), f32)
    own_local = [jnp.concatenate([own[:, start + a * count : start + (a + 1) * count], fill], axis=1) for a in range(3)]
    scalars = jnp.concatenate([jnp.zeros((IP, 256 - width), f32), own[:, 0:width]], axis=1)
    points = []
    for a in range(3):
        points.append(
            frame[:, 3 * a : 3 * a + 1] * own_local[0]
            + frame[:, 3 * a + 1 : 3 * a + 2] * own_local[1]
            + frame[:, 3 * a + 2 : 3 * a + 3] * own_local[2]
            + frame[:, 9 + a : 10 + a]
        )
    weight = jnp.broadcast_to(point_weight, (IP, 128))
    length = weight * (points[0] * points[0] + points[1] * points[1] + points[2] * points[2])
    everything = jnp.concatenate(
        [scalars * (third / math.sqrt(CHEAD))] + [2.0 * weight * p for p in points] + [-weight], axis=1
    )
    _, lane = grid_of((IP, 768))
    head = jnp.where(lane < 256, (lane - (256 - width)) >> log2(CHEAD), (lane & 127) >> log2(PQ))
    _, lane = grid_of((IP, 128))
    rows = []
    lengths = []
    for h in range(H):
        rows.append(jnp.where(head == h, everything, 0.0))
        lengths.append(-jnp.sum(jnp.where((lane >> log2(PQ)) == h, length, 0.0), axis=1, keepdims=True))
    return jnp.concatenate(rows, axis=0), jnp.concatenate(lengths, axis=0)


def logits_and_values(slots, own, frame, qkv, columns):
    query_rows, lengths = own
    pieces = slots[:, CS:SLOT].astype(bf16)
    entry = dot(pieces, piece_select(128, True))
    rows = dot_nt(piece_select(16), pieces)
    keys = dot(state_of(slots), qkv)
    points = H * PQ
    first = 3 * H * CHEAD + 3 * points
    _, lane = grid_of((keys.shape[0], 128))

    def block(start, size):
        at, offset = start // 128 * 128, start % 128
        one = keys[:, at : at + 128]
        if offset == 0:
            return one
        one = pltpu.roll(one, 128 - offset, 1)
        if offset + size <= 128:
            return one
        return jnp.where(lane < 128 - offset, one, pltpu.roll(keys[:, at + 128 : at + 256], 128 - offset, 1))

    local = []
    for a in range(3):
        value_points = block(first + 3 * points + a * H * PV, H * PV)
        local.append(jnp.concatenate([value_points, block(first + a * points, points)], axis=1))
    placed = []
    for a in range(3):
        placed.append(
            entry[:, 3 * a : 3 * a + 1] * local[0]
            + entry[:, 3 * a + 1 : 3 * a + 2] * local[1]
            + entry[:, 3 * a + 2 : 3 * a + 3] * local[2]
            + entry[:, 9 + a : 10 + a]
        )
    values = jnp.concatenate([keys[:, 384:640]] + [p[:, 0:128] for p in placed], axis=1)
    key_points = [p[:, 128:256] for p in placed]
    length = key_points[0] * key_points[0] + key_points[1] * key_points[1] + key_points[2] * key_points[2]
    key_side = jnp.concatenate([keys[:, 128:384]] + key_points + [length], axis=1)
    far = mask_fill * (rows[MASK_AT : MASK_AT + 1, :] - 1.0)
    chain = jnp.broadcast_to(rows[CHAIN_AT : CHAIN_AT + 1, :], (IP, rows.shape[1]))
    chain = jnp.concatenate([chain - frame[:, CHAIN_AT : CHAIN_AT + 1]] * H, axis=0)
    added = jnp.where(chain == 0.0, columns[:, ROWS + 1 : ROWS + 2], columns[:, ROWS : ROWS + 1]) + far + lengths
    return dot_nt(query_rows, key_side, highest) + added, values


def attend(r, logits, values, halves, state, frame, weights):
    top = jnp.max(logits, axis=1, keepdims=True)
    raised = jnp.exp(logits - top)
    attention = raised / jnp.sum(raised, axis=1, keepdims=True)
    row, _ = grid_of(attention.shape)
    parts = [jnp.where((row & (IP - 1)) == i, attention, 0.0).astype(bf16) for i in range(r)]
    out_pair = dot(jnp.concatenate(parts, axis=1), halves)
    summed = dot_close(attention, values)
    _, lane = grid_of((IP, 640))
    head = jnp.where(lane < 256, lane >> log2(CHEAD), (lane & 127) >> log2(PV))
    gathered = None
    for h, tile in enumerate(tiles(summed)):
        one = jnp.where(head == h, tile, 0.0)
        gathered = one if gathered is None else gathered + one
    relative = [
        gathered[:, 256 + 128 * a : 256 + 128 * a + H * PV] - frame[:, 9 + a : 10 + a] for a in range(3)
    ]
    out_local = [
        frame[:, a : a + 1] * relative[0]
        + frame[:, 3 + a : 4 + a] * relative[1]
        + frame[:, 6 + a : 7 + a] * relative[2]
        for a in range(3)
    ]
    out_norm = jnp.sqrt(
        out_local[0] * out_local[0] + out_local[1] * out_local[1] + out_local[2] * out_local[2] + 1e-08
    )
    out_ref, frame_weight = weights()

    def projected(blocks, first):
        rows = jnp.concatenate(blocks, axis=1)
        rows = jnp.concatenate([rows, jnp.zeros_like(rows)], axis=0).astype(bf16)
        return dot(rows, out_ref[first : first + rows.shape[1], :])[0:IP]

    from_pair = projected(tiles(out_pair), H * (CHEAD + 4 * PV))
    from_points = projected([gathered[:, 0 : H * CHEAD]] + out_local + [out_norm], 0)
    state = layer_norm(state + (from_points + from_pair))
    update = [jnp.sum(state * frame_weight[e : e + 1], axis=1, keepdims=True) for e in range(6)]
    quat = update[0:3]
    real = lax.rsqrt(1.0 + (quat[0] * quat[0] + quat[1] * quat[1] + quat[2] * quat[2]))
    step = quat_entries(quat[0] * real, quat[1] * real, quat[2] * real, real)
    old = [frame[:, e : e + 1] for e in range(9)]
    columns = []
    for target in range(3):
        for column in range(3):
            columns.append(
                old[target * 3] * step[column]
                + old[target * 3 + 1] * step[3 + column]
                + old[target * 3 + 2] * step[6 + column]
            )
    for target in range(3):
        columns.append(
            frame[:, 9 + target : 10 + target]
            + old[target * 3] * update[3]
            + old[target * 3 + 1] * update[4]
            + old[target * 3 + 2] * update[5]
        )
    _, lane = grid_of((IP, 128))
    for at, column in enumerate(columns):
        frame = jnp.where(lane == at, column, frame)
    return state, frame


def pad_state(single_ref):
    r = single_ref.shape[0]
    return jnp.concatenate([single_ref[...], jnp.zeros((IP - r, CS), f32)], axis=0)


PACK_ROWS = 192
BIAS, POINT_WEIGHT, FRAME_WEIGHT, STATE, FRAME = 0, 128, 136, 160, 184


def wide(pack_ref, first):
    return jnp.concatenate([pack_ref[first + IP * part : first + IP * (part + 1)] for part in range(3)], axis=1)


def own_kernel(
    pair_any, tri_any, qkv_any, single_any, frame_any, columns_any, tri_out_any, bias_weight_any, frame_weight_any,
    gate_ref, rows_ref, pack_ref, pair_copy_any,
    pair_ref, gate_weight_ref, qkv_ref, single_ref, columns_ref, tri_out_ref, bias_weight_ref, frame_weight_ref, sems,
):
    r, count, _ = pair_ref.shape
    frame_ref = pack_ref.at[FRAME : FRAME + IP]
    for copy in copies(
        sems,
        (pair_any, pair_ref),
        (tri_any.at[:, 4 * CH :], gate_weight_ref),
        (qkv_any, qkv_ref),
        (single_any, single_ref),
        (frame_any, frame_ref),
        (columns_any, columns_ref),
        (tri_out_any, tri_out_ref),
        (bias_weight_any, bias_weight_ref),
        (frame_weight_any, frame_weight_ref),
    ):
        copy.wait()
    back = pltpu.make_async_copy(pair_ref, pair_copy_any, sems.at[9])
    back.start()
    gate_ref[r * count :, :] = tri_out_ref[...]
    bias_weight = bias_weight_ref[...]
    spread = [jnp.broadcast_to(bias_weight[h : h + 1], (IP, CH)) for h in range(H)]
    bias_weight = jnp.concatenate(spread + [jnp.zeros((128 - ROWS, CH), f32)], axis=0).T
    _, lane = grid_of((CH, 128))
    pack_ref[BIAS : BIAS + CH, :] = jnp.where(lane < ROWS, bias_weight, columns_ref[0:CH, :])
    pack_ref[POINT_WEIGHT : POINT_WEIGHT + IP, :] = columns_ref[CH : CH + IP, :]
    state = pad_state(single_ref)
    frame_weight = frame_weight_ref[...]
    frame_weight = jnp.concatenate([frame_weight, jnp.zeros((IP - 6, CS), f32)], axis=0)
    for part in range(3):
        lanes = slice(128 * part, 128 * (part + 1))
        pack_ref[FRAME_WEIGHT + IP * part : FRAME_WEIGHT + IP * (part + 1), :] = frame_weight[:, lanes]
        pack_ref[STATE + IP * part : STATE + IP * (part + 1), :] = state[:, lanes]
    rows, lengths = own_side(state, frame_ref[...], qkv_ref, pack_ref[POINT_WEIGHT : POINT_WEIGHT + 1])
    rows_ref[:, 0:768] = rows
    rows_ref[:, 768:896] = jnp.broadcast_to(lengths, (ROWS, 128))
    for i in range(r):
        normed = layer_norm(pair_ref[i]).astype(bf16)
        gate_ref[i * count : (i + 1) * count] = jax.nn.sigmoid(dot(normed, gate_weight_ref[...])).astype(bf16)
    back.wait()


def prepare_kernel(w, n, r, mine_ref, other_ref, rows_ref, qkv_ref, pack_ref, logits_ref, values_ref):
    odd = pack_ref[POINT_WEIGHT + 1 : POINT_WEIGHT + 2, 0:1] > 0.5
    mine, other = mine_ref[...].astype(f32), other_ref[...].astype(f32)
    halves = [jnp.where(odd, other, mine).astype(bf16), jnp.where(odd, mine, other).astype(bf16)]
    slots = jnp.concatenate([quarter_of(halves[q & 1], 0, q >> 1, w, r, n) for q in range(4)], axis=1)
    logits, values = logits_and_values(
        slots, (rows_ref[:, 0:768], rows_ref[:, 768:769]), pack_ref[FRAME : FRAME + IP], qkv_ref[...],
        pack_ref[BIAS : BIAS + ROWS],
    )
    logits_ref[...] = logits
    values_ref[...] = values


def update_kernel(
    w, n, recv_ref, pair_any, gate_ref, logits_ref, values_ref, pack_ref, out_weight_ref,
    pair_out_any, half_ref, bias_ref, state_ref, new_frame_ref, send_ref, pair_ref, sems,
):
    r, count, _ = pair_ref.shape
    load = pltpu.make_async_copy(pair_any, pair_ref, sems.at[0])
    load.start()
    row, column = grid_of((2 * CH, 2 * CH))
    c = row & (CH - 1)
    take = onehot(column == (c >> log2(w)) * 2 * w + (row >> log2(CH)) * w + (c & (w - 1)))
    product = dot(take, recv_ref[...])
    tri_out = gate_ref[r * count :, :]
    updates = []
    for high in range(2):
        normed = layer_norm(product[high * CH : (high + 1) * CH], axis=0).astype(bf16)
        updates.append(dot_tn(normed, tri_out))
    update = jnp.concatenate(updates, axis=0)
    bias_weight = pack_ref[BIAS : BIAS + CH, :]
    _, lane = grid_of((CH, 128))
    bias_weight = jnp.concatenate(
        [jnp.where(((lane & (IP - 1)) == i) & (lane < ROWS), bias_weight, 0.0) for i in range(r)], axis=0
    )
    load.wait()
    pair = pair_ref[...].reshape(r * count, CH)
    pair_out = pair + gate_ref[0 : r * count, :].astype(f32) * update
    pair_ref[...] = pair_out.reshape(r, count, CH)
    store = pltpu.make_async_copy(pair_ref, pair_out_any, sems.at[1])
    store.start()
    normed_pair = layer_norm(pair_out)
    halves = normed_pair.astype(bf16)
    half_ref[...] = halves
    side_by_side = jnp.concatenate([normed_pair[i * count : (i + 1) * count] for i in range(r)], axis=1)
    bias = (dot_close(side_by_side, bias_weight) * third).T[0:ROWS]
    bias_ref[...] = bias
    state, frame = attend(
        r, logits_ref[...] + bias, values_ref[...], halves, wide(pack_ref, STATE), pack_ref[FRAME : FRAME + IP],
        lambda: (out_weight_ref, wide(pack_ref, FRAME_WEIGHT)),
    )
    state_ref[...] = state
    new_frame_ref[...] = frame
    fill_rows(send_ref, 0, spread_rows(slots_of(state, frame), w, r))
    store.wait()


def last_kernel(
    w, n, r, recv_ref, half_ref, bias_ref, state_ref, frame_ref, pack_ref, qkv_ref, out_weight_ref,
    single_out_ref, rotation_ref, translation_ref, scr,
):
    slots = natural_rows(recv_ref, 0, w, r, n)
    state, frame = state_ref[...], frame_ref[...]
    own = own_side(state, frame, qkv_ref, pack_ref[POINT_WEIGHT : POINT_WEIGHT + 1])
    logits, values = logits_and_values(slots, own, frame, qkv_ref[...], pack_ref[BIAS : BIAS + ROWS])
    state, frame = attend(
        r, logits + bias_ref[...], values, half_ref[...], state, frame,
        lambda: (out_weight_ref, wide(pack_ref, FRAME_WEIGHT)),
    )
    single_out_ref[...] = state[0:r]
    rotation_ref[...] = frame[0:r, 0:9]
    scr[...] = jnp.concatenate([frame, jnp.zeros((128 - IP, 128), f32)], axis=0).T
    translation_ref[...] = scr[9:12, 0:r]


VMEM = pl.BlockSpec(memory_space=pltpu.VMEM)
HBM = pl.BlockSpec(memory_space=pltpu.HBM)


def call(body, name, outs, args, outside=(), outside_outs=(), scratch=(), limit=32, alias=None, flops=0, moved=0):
    return pl.pallas_call(
        body,
        name=name,
        out_shape=[jax.ShapeDtypeStruct(s, d) for s, d in outs],
        in_specs=[HBM if at in outside else VMEM for at in range(len(args))],
        out_specs=[HBM if at in outside_outs else VMEM for at in range(len(outs))],
        scratch_shapes=list(scratch),
        input_output_aliases=alias or {},
        compiler_params=pltpu.CompilerParams(vmem_limit_bytes=limit * 2**20),
        cost_estimate=pl.CostEstimate(flops=flops, bytes_accessed=moved, transcendentals=0),
    )(*args)


def local(
    pair, single, quats, translate, res_mask, chain_ids, tri_weight, tri_out_weight, qkv_weight, bias_weight,
    head_gamma, chain_bias, out_weight, frame_weight,
):
    n = lax.axis_size("row")
    r, count, _ = pair.shape
    w = CH // n
    rows = 2 * w
    lanes = r * SLOT // rows
    limit = 24 if count == 128 else 56

    def exchange(sent):
        width = sent.shape[1]
        got = lax.all_to_all(sent.reshape(n, rows, width), "row", 0, 0, tiled=True)
        return got.reshape(n * rows, width)

    def like(array):
        return pltpu.VMEM(array.shape, array.dtype)

    dma = pltpu.SemaphoreType.DMA
    sent, frame = call(
        functools.partial(gate_kernel, w, n),
        "gate",
        [((n * rows, r * count + lanes // 2), bf16), ((IP, 128), f32)],
        [pair, tri_weight, single, quats, translate, res_mask, chain_ids],
        outside=range(7),
        scratch=[
            like(pair),
            pltpu.VMEM((CH, 4 * CH), bf16),
            like(single),
            like(quats),
            like(translate),
            pltpu.SMEM((r,), jnp.int32),
            pltpu.SMEM((r,), jnp.int32),
            pltpu.VMEM((128, 128), f32),
            dma((7,)),
        ],
        limit=60,
    )
    received = exchange(sent)

    point_weight = head_gamma * (math.sqrt(2.0 / (9.0 * PQ)) * 0.5 * third)
    columns = jnp.pad(jnp.repeat(chain_bias.T, IP, axis=0), ((0, CH - ROWS + IP), (ROWS, 126 - ROWS)))
    columns = columns.at[CH, 0 : H * PQ].set(jnp.repeat(point_weight, PQ))
    columns = columns.at[CH + 1, 0].set((lax.axis_index("row") & 1).astype(f32))
    gate, query_rows, pack, pair_copy = call(
        own_kernel,
        "own",
        [
            ((r * count + CH, CH), bf16),
            ((ROWS, 896), f32),
            ((PACK_ROWS, 128), f32),
            (pair.shape, f32),
        ],
        [pair, tri_weight, qkv_weight, single, frame, columns, tri_out_weight, bias_weight.T, frame_weight.T],
        outside=range(9),
        outside_outs=(3,),
        scratch=[
            like(pair),
            pltpu.VMEM((CH, CH), bf16),
            like(qkv_weight),
            like(single),
            like(columns),
            like(tri_out_weight),
            pltpu.VMEM((H, CH), f32),
            pltpu.VMEM((6, CS), f32),
            dma((10,)),
        ],
        limit=60,
        flops=2 * r * count * CH * CH,
        moved=16 * 2**20,
    )
    received, gate, query_rows, pack, pair_copy = lax.optimization_barrier(
        (received, gate, query_rows, pack, pair_copy)
    )
    formed, slots = call(
        functools.partial(product_kernel, w, n, r),
        "product",
        [((n * rows, (r // 2) * count), bf16), ((n * rows, lanes // 2), bf16)],
        [received],
        limit=limit,
    )
    products = exchange(formed)
    other = lax.ppermute(slots, "row", [(i, i ^ 1) for i in range(n)])
    logits, values = call(
        functools.partial(prepare_kernel, w, n, r),
        "prepare",
        [((ROWS, count), f32), ((count, 640), f32)],
        [slots, other, query_rows, qkv_weight, pack],
        limit=limit,
        flops=2 * count * CS * 1152,
        moved=8 * 2**20,
    )
    pair_out, pair_half, bias, state, frame, sent = call(
        functools.partial(update_kernel, w, n),
        "update",
        [
            ((r, count, CH), f32),
            ((r * count, CH), bf16),
            ((ROWS, count), f32),
            ((IP, CS), f32),
            ((IP, 128), f32),
            ((n * rows, lanes), bf16),
        ],
        [products, pair_copy, gate, logits, values, pack, out_weight],
        outside=(1,),
        outside_outs=(0,),
        alias={1: 0},
        scratch=[like(pair), dma((2,))],
        limit=limit,
    )
    received = exchange(sent)
    single_out, rotation, translation = call(
        functools.partial(last_kernel, w, n, r),
        "last",
        [((r, CS), f32), ((r, 9), f32), ((3, r), f32)],
        [received, pair_half, bias, state, frame, pack, qkv_weight, out_weight],
        scratch=[pltpu.VMEM((128, 128), f32)],
        limit=limit,
    )
    return (pair_out, single_out, rotation.T, translation)


def solution(mesh):
    rows = ("grp", "row")
    placed = (P(rows, None, None), P(rows, None), P(None, rows), P(None, rows), P(rows), P(rows)) + (P(),) * 8
    return jax.shard_map(
        local,
        mesh=mesh,
        in_specs=placed,
        out_specs=(P(rows, None, None), P(rows, None), P(None, rows), P(None, rows)),
        check_vma=False,
    )
```

```python
import functools
import math

import jax
import jax.numpy as jnp
from jax import lax
from jax.experimental import pallas as pl
from jax.experimental.pallas import tpu as pltpu
from jax.sharding import PartitionSpec as P

CH = 128
CS = 384
H = 12
CHEAD = 16
PQ = 4
PV = 8
SLOT = 512
IP = 8
ROWS = H * IP
MASK_AT = 12
CHAIN_AT = 13

f32 = jnp.float32
bf16 = jnp.bfloat16
highest = lax.Precision.HIGHEST
epsilon = 1e-05
mask_fill = 100000.0
third = math.sqrt(1.0 / 3.0)


def layer_norm(values, axis=-1):
    center = values - jnp.mean(values, axis=axis, keepdims=True)
    spread = jnp.mean(center * center, axis=axis, keepdims=True)
    return center * lax.rsqrt(spread + epsilon)


def quat_entries(one, two, three, real):
    return [
        1.0 - 2.0 * (two * two + three * three),
        2.0 * (one * two - real * three),
        2.0 * (one * three + real * two),
        2.0 * (one * two + real * three),
        1.0 - 2.0 * (one * one + three * three),
        2.0 * (two * three - real * one),
        2.0 * (one * three - real * two),
        2.0 * (two * three + real * one),
        1.0 - 2.0 * (one * one + two * two),
    ]


def dot(a, b, precision=None):
    return lax.dot_general(
        a, b, (((1,), (0,)), ((), ())), precision=precision, preferred_element_type=f32
    )


def dot_nt(a, b, precision=None):
    return lax.dot_general(
        a, b, (((1,), (1,)), ((), ())), precision=precision, preferred_element_type=f32
    )


def dot_tn(a, b):
    return lax.dot_general(a, b, (((0,), (0,)), ((), ())), preferred_element_type=f32)


def halves_of(x):
    high = x.astype(bf16)
    return high, (x - high.astype(f32)).astype(bf16)


def dot_close(a, b):
    a_high, a_low = halves_of(a)
    b_high, b_low = halves_of(b)
    return dot(jnp.concatenate([a_high, a_low, a_high], axis=1), jnp.concatenate([b_high, b_high, b_low], axis=0))


def sigmoid(x):
    return 0.5 * jnp.tanh(0.5 * x) + 0.5


def log2(number):
    assert number & (number - 1) == 0
    return number.bit_length() - 1


def grid_of(shape):
    return lax.broadcasted_iota(jnp.int32, shape, 0), lax.broadcasted_iota(jnp.int32, shape, 1)


def onehot(match):
    return jnp.where(match, 1.0, 0.0).astype(bf16)


def swap_rows(count, minor_count):
    row, column = grid_of((count, count))
    major_count = count // minor_count
    minor = row >> log2(major_count)
    major = row & (major_count - 1)
    return onehot(column == major * minor_count + minor)


def spread_rows(slots, w, r):
    rows = 2 * w
    lanes = r * SLOT // rows
    if rows == 8 and r == 4:
        low, high = slots[0:IP, 0:lanes].astype(f32), slots[0:IP, lanes:].astype(f32)
        row, _ = grid_of((IP, lanes))
        one = jnp.where(row < r, low, pltpu.roll(high, r, 0))
        return jnp.concatenate([one, one], axis=0).astype(bf16)
    x, i = grid_of((16, 16))
    q = x & (rows - 1)
    if lanes <= SLOT:
        total = None
        for t in range(SLOT // lanes):
            one = dot(onehot((q == t * r + i) & (i < r)), slots[:, t * lanes : (t + 1) * lanes])
            total = one if total is None else total + one
        return total.astype(bf16)
    return jnp.concatenate(
        [dot(onehot(i == t * rows + q), slots) for t in range(lanes // SLOT)], axis=1
    ).astype(bf16)


def natural_rows(x_ref, first, w, r, n, start=0, stop=SLOT):
    rows = 2 * w
    lanes = r * SLOT // rows
    count = n * r
    j, x = grid_of((count, n * rows))
    s = x >> log2(rows)
    q = x & (rows - 1)
    if lanes <= SLOT:
        pieces = []
        for t in range(SLOT // lanes):
            low, high = max(start, t * lanes), min(stop, (t + 1) * lanes)
            if low < high:
                values = x_ref[:, first + low - t * lanes : first + high - t * lanes]
                pieces.append(dot(onehot((j == s * r + q - t * r) & ((q >> log2(r)) == t)), values))
        return pieces[0] if len(pieces) == 1 else jnp.concatenate(pieces, axis=1)
    total = None
    for t in range(lanes // SLOT):
        values = x_ref[:, first + t * SLOT + start : first + t * SLOT + stop]
        one = dot(onehot(j == s * r + t * rows + q), values)
        total = one if total is None else total + one
    return total


def frame_pieces(frame):
    high = frame.astype(bf16).astype(f32)
    rest = frame - high
    middle = rest.astype(bf16).astype(f32)
    low = (rest - middle).astype(bf16).astype(f32)
    return high + pltpu.roll(middle, 32, 1) + pltpu.roll(low, 64, 1)


def slots_of(state, frame):
    _, lane = grid_of((IP, 128))
    tail = state[:, 256:CS]
    mask = jnp.where(lane == 127, frame[:, MASK_AT : MASK_AT + 1], 0.0)
    moved = jnp.where((lane >= 112) & (lane < 120), pltpu.roll(tail, 120, 1), mask)
    last = jnp.where(lane < 96, frame_pieces(frame), moved)
    both = jnp.concatenate([state[:, 0:256], jnp.where(lane < 120, tail, mask), last], axis=1)
    return jnp.concatenate([both, jnp.zeros_like(both)], axis=0).astype(bf16)


def state_of(slots):
    _, lane = grid_of((slots.shape[0], 128))
    tail = jnp.where(lane < 120, slots[:, 256:384], pltpu.roll(slots[:, 384:512], 8, 1))
    return jnp.concatenate([slots[:, 0:256], tail], axis=1).astype(bf16)


def half_rows(slots, w, r):
    rows = 2 * w
    x, i = grid_of((16, 16))
    parity = (x >> log2(rows)) & 1
    blocks = []
    for at in range(2 * r // rows):
        b = (x & (rows - 1)) * (2 * r // rows) + at
        total = None
        for quarter in range(4):
            take = onehot((i == (b & (r - 1))) & (parity + 2 * (b >> log2(r)) == quarter))
            one = dot(take, slots[:, quarter * 128 : (quarter + 1) * 128])
            total = one if total is None else total + one
        blocks.append(total)
    return (blocks[0] if len(blocks) == 1 else jnp.concatenate(blocks, axis=1)).astype(bf16)


def quarter_of(x, first, second, w, r, n):
    rows = 2 * w
    j, row = grid_of((n * r, n * rows))
    total = None
    for at in range(2 * r // rows):
        b = (row & (rows - 1)) * (2 * r // rows) + at
        take = onehot((j == (row >> log2(rows)) * r + (b & (r - 1))) & ((b >> log2(r)) == second))
        one = dot(take, x[:, first + at * 128 : first + (at + 1) * 128])
        total = one if total is None else total + one
    return total


def fill_rows(out_ref, first, tile):
    lanes = tile.shape[1]
    for t in range(out_ref.shape[0] // 16):
        out_ref[t * 16 : (t + 1) * 16, first : first + lanes] = tile


def piece_select(row_count, transposed=False):
    if transposed:
        lane, entry = grid_of((128, row_count))
    else:
        entry, lane = grid_of((row_count, 128))
    return onehot(((lane & 31) == entry) & (lane < 96))


def copies(sems, *pairs):
    started = [pltpu.make_async_copy(src, dst, sems.at[at]) for at, (src, dst) in enumerate(pairs)]
    for copy in started:
        copy.start()
    return started


def gate_kernel(
    w, n, pair_any, tri_any, single_any, quats_any, translate_any, mask_any, chain_any, send_ref, frame_ref,
    pair_ref, tri_ref, single_ref, quats_ref, translate_ref, mask_ref, chain_ref, scr, sems,
):
    r, count, _ = pair_ref.shape
    loads = copies(
        sems,
        (quats_any, quats_ref),
        (translate_any, translate_ref),
        (mask_any, mask_ref),
        (chain_any, chain_ref),
        (single_any, single_ref),
        (tri_any.at[:, 0 : 4 * CH], tri_ref),
        (pair_any, pair_ref),
    )
    row, column = grid_of((2 * CH, 2 * CH))
    d = row >> log2(2 * w)
    side = (row >> log2(w)) & 1
    take = onehot(column == side * CH + d * w + (row & (w - 1)))
    for load in loads:
        load.wait()
    gate_weight = jnp.concatenate([tri_ref[:, 0:CH], tri_ref[:, 2 * CH : 3 * CH]], axis=1)
    value_weight = jnp.concatenate([tri_ref[:, CH : 2 * CH], tri_ref[:, 3 * CH : 4 * CH]], axis=1)
    gate_weight = dot_nt(take, gate_weight).astype(bf16)
    value_weight = dot_nt(take, value_weight).astype(bf16)
    normed = layer_norm(pair_ref[...].reshape(r * count, CH)).astype(bf16)
    gates = dot_nt(gate_weight, normed)
    values = dot_nt(value_weight, normed)
    mask = jnp.concatenate([jnp.full((1, count), mask_ref[i].astype(f32)) for i in range(r)], axis=1)
    send_ref[:, 0 : r * count] = (sigmoid(gates) * values * mask).astype(bf16)

    scr[...] = jnp.zeros_like(scr)
    quats = quats_ref[...]
    real = lax.rsqrt(1.0 + jnp.sum(quats * quats, axis=0, keepdims=True))
    unit = quats * real
    entries = quat_entries(unit[0:1], unit[1:2], unit[2:3], real)
    for at, entry in enumerate(entries):
        scr[at : at + 1, 0:r] = entry
    scr[9:12, 0:r] = translate_ref[...]
    frame = scr[...].T[0:IP, :]
    row, lane = grid_of((IP, 128))
    for i in range(r):
        frame = jnp.where((row == i) & (lane == MASK_AT), mask_ref[i].astype(f32), frame)
        frame = jnp.where((row == i) & (lane == CHAIN_AT), chain_ref[i].astype(f32), frame)
    frame_ref[...] = frame
    fill_rows(send_ref, r * count, half_rows(slots_of(pad_state(single_ref), frame), w, r))


def product_kernel(w, n, r, recv_ref, send_ref, slots_ref, right_ref):
    count = n * r
    slots_ref[...] = recv_ref[:, r * count :]
    rows = 2 * w
    pieces = quarter_of(recv_ref, r * count, 1, w, r, n).astype(bf16)
    _, lane = grid_of((16, 128))
    mask = dot_nt(onehot(lane == 127), pieces)[0:1, :]
    mask = jnp.concatenate([mask] * r, axis=1)
    order = swap_rows(n * rows, rows)
    sides = dot(order, recv_ref[:, 0 : r * count]) * mask
    row, column = grid_of((count, count))
    to_natural = onehot(row == (column & (n - 1)) * r + (column >> log2(n)))

    def stacked(block):
        part = sides[block * n : (block + 1) * n].astype(bf16)
        return jnp.concatenate([part[:, i * count : (i + 1) * count] for i in range(r)], axis=0)

    if by_channel(w, count):
        for c in range(w):
            for i in range(r):
                part = sides[(w + c) * n : (w + c + 1) * n, i * count : (i + 1) * count]
                right_ref[c, pl.ds(i, n, stride=r), :] = part

    def natural(c):
        if by_channel(w, count):
            return right_ref[c, 0:128].astype(bf16)
        return dot(to_natural, stacked(w + c)).astype(bf16)

    half = r // 2
    products = []
    for c in range(w):
        products.append(dot_nt(stacked(c), natural(c)))
    if by_channel(w, count):
        for high in range(2):
            for low in range(half):
                for c in range(w):
                    first = (high * half + low) * n
                    right_ref[low, pl.ds(high * w + c, n, stride=rows), :] = products[c][first : first + n]
        for low in range(half):
            send_ref[:, low * count : (low + 1) * count] = right_ref[low].astype(bf16)
        return
    products = [product.astype(bf16) for product in products]
    blocks = []
    for high in range(2):
        for c in range(w):
            first = high * half
            blocks.append(
                jnp.concatenate(
                    [products[c][(first + low) * n : (first + low + 1) * n] for low in range(half)], axis=1
                )
            )
    send_ref[...] = dot(swap_rows(n * rows, n), jnp.concatenate(blocks, axis=0)).astype(bf16)


def tiles(x):
    return [x[h * IP : (h + 1) * IP] for h in range(H)]


def own_side(state, frame, qkv_ref, point_weight):
    both = jnp.concatenate([state, jnp.zeros_like(state)], axis=0).astype(bf16)
    own = dot(both, jnp.concatenate([qkv_ref[:, 0:256], qkv_ref[:, 512:768]], axis=1))[0:IP]
    width = H * CHEAD
    count = H * PQ
    start = 3 * width - 256
    fill = jnp.zeros((IP, 128 - count), f32)
    own_local = [jnp.concatenate([own[:, start + a * count : start + (a + 1) * count], fill], axis=1) for a in range(3)]
    scalars = jnp.concatenate([jnp.zeros((IP, 256 - width), f32), own[:, 0:width]], axis=1)
    points = []
    for a in range(3):
        points.append(
            frame[:, 3 * a : 3 * a + 1] * own_local[0]
            + frame[:, 3 * a + 1 : 3 * a + 2] * own_local[1]
            + frame[:, 3 * a + 2 : 3 * a + 3] * own_local[2]
            + frame[:, 9 + a : 10 + a]
        )
    weight = jnp.broadcast_to(point_weight, (IP, 128))
    length = weight * (points[0] * points[0] + points[1] * points[1] + points[2] * points[2])
    everything = jnp.concatenate(
        [scalars * (third / math.sqrt(CHEAD))] + [2.0 * weight * p for p in points] + [-weight], axis=1
    )
    _, lane = grid_of((IP, 768))
    head = jnp.where(lane < 256, (lane - (256 - width)) >> log2(CHEAD), (lane & 127) >> log2(PQ))
    _, lane = grid_of((IP, 128))
    rows = []
    lengths = []
    for h in range(H):
        rows.append(jnp.where(head == h, everything, 0.0))
        lengths.append(-jnp.sum(jnp.where((lane >> log2(PQ)) == h, length, 0.0), axis=1, keepdims=True))
    return jnp.concatenate(rows, axis=0), jnp.concatenate(lengths, axis=0)


def logits_and_values(slots, own, frame, qkv, columns):
    query_rows, lengths = own
    pieces = slots[:, CS:SLOT].astype(bf16)
    entry = dot(pieces, piece_select(128, True))
    rows = dot_nt(piece_select(16), pieces)
    keys = dot(state_of(slots), qkv)
    points = H * PQ
    first = 3 * H * CHEAD + 3 * points
    _, lane = grid_of((keys.shape[0], 128))

    def block(start, size):
        at, offset = start // 128 * 128, start % 128
        one = keys[:, at : at + 128]
        if offset == 0:
            return one
        one = pltpu.roll(one, 128 - offset, 1)
        if offset + size <= 128:
            return one
        return jnp.where(lane < 128 - offset, one, pltpu.roll(keys[:, at + 128 : at + 256], 128 - offset, 1))

    local = []
    for a in range(3):
        value_points = block(first + 3 * points + a * H * PV, H * PV)
        local.append(jnp.concatenate([value_points, block(first + a * points, points)], axis=1))
    placed = []
    for a in range(3):
        placed.append(
            entry[:, 3 * a : 3 * a + 1] * local[0]
            + entry[:, 3 * a + 1 : 3 * a + 2] * local[1]
            + entry[:, 3 * a + 2 : 3 * a + 3] * local[2]
            + entry[:, 9 + a : 10 + a]
        )
    values = jnp.concatenate([keys[:, 384:640]] + [p[:, 0:128] for p in placed], axis=1)
    key_points = [p[:, 128:256] for p in placed]
    length = key_points[0] * key_points[0] + key_points[1] * key_points[1] + key_points[2] * key_points[2]
    key_side = jnp.concatenate([keys[:, 128:384]] + key_points + [length], axis=1)
    far = mask_fill * (rows[MASK_AT : MASK_AT + 1, :] - 1.0)
    chain = jnp.broadcast_to(rows[CHAIN_AT : CHAIN_AT + 1, :], (IP, rows.shape[1]))
    chain = jnp.concatenate([chain - frame[:, CHAIN_AT : CHAIN_AT + 1]] * H, axis=0)
    added = jnp.where(chain == 0.0, columns[:, ROWS + 1 : ROWS + 2], columns[:, ROWS : ROWS + 1]) + far + lengths
    return dot_nt(query_rows, key_side, highest) + added, values


def attend(r, logits, values, halves, state, frame, weights):
    top = jnp.max(logits, axis=1, keepdims=True)
    raised = jnp.exp(logits - top)
    share = 1.0 / jnp.sum(raised, axis=1, keepdims=True)
    row, _ = grid_of(raised.shape)
    parts = [jnp.where((row & (IP - 1)) == i, raised, 0.0).astype(bf16) for i in range(r)]
    out_pair = dot(jnp.concatenate(parts, axis=1), halves) * share
    summed = dot_close(raised, values) * share
    _, lane = grid_of((IP, 640))
    head = jnp.where(lane < 256, lane >> log2(CHEAD), (lane & 127) >> log2(PV))
    gathered = None
    for h, tile in enumerate(tiles(summed)):
        one = jnp.where(head == h, tile, 0.0)
        gathered = one if gathered is None else gathered + one
    relative = [
        gathered[:, 256 + 128 * a : 256 + 128 * a + H * PV] - frame[:, 9 + a : 10 + a] for a in range(3)
    ]
    out_local = [
        frame[:, a : a + 1] * relative[0]
        + frame[:, 3 + a : 4 + a] * relative[1]
        + frame[:, 6 + a : 7 + a] * relative[2]
        for a in range(3)
    ]
    out_norm = jnp.sqrt(
        out_local[0] * out_local[0] + out_local[1] * out_local[1] + out_local[2] * out_local[2] + 1e-08
    )
    out_ref, frame_weight = weights()

    def projected(blocks, first):
        rows = jnp.concatenate(blocks, axis=1)
        rows = jnp.concatenate([rows, jnp.zeros_like(rows)], axis=0).astype(bf16)
        return dot(rows, out_ref[first : first + rows.shape[1], :])[0:IP]

    from_pair = projected(tiles(out_pair), H * (CHEAD + 4 * PV))
    from_points = projected([gathered[:, 0 : H * CHEAD]] + out_local + [out_norm], 0)
    state = layer_norm(state + (from_points + from_pair))
    update = [jnp.sum(state * frame_weight[e : e + 1], axis=1, keepdims=True) for e in range(6)]
    quat = update[0:3]
    real = lax.rsqrt(1.0 + (quat[0] * quat[0] + quat[1] * quat[1] + quat[2] * quat[2]))
    step = quat_entries(quat[0] * real, quat[1] * real, quat[2] * real, real)
    old = [frame[:, e : e + 1] for e in range(9)]
    columns = []
    for target in range(3):
        for column in range(3):
            columns.append(
                old[target * 3] * step[column]
                + old[target * 3 + 1] * step[3 + column]
                + old[target * 3 + 2] * step[6 + column]
            )
    for target in range(3):
        columns.append(
            frame[:, 9 + target : 10 + target]
            + old[target * 3] * update[3]
            + old[target * 3 + 1] * update[4]
            + old[target * 3 + 2] * update[5]
        )
    _, lane = grid_of((IP, 128))
    for at, column in enumerate(columns):
        frame = jnp.where(lane == at, column, frame)
    return state, frame


def pad_state(single_ref):
    r = single_ref.shape[0]
    return jnp.concatenate([single_ref[...], jnp.zeros((IP - r, CS), f32)], axis=0)


PACK_ROWS = 192
BIAS, POINT_WEIGHT, FRAME_WEIGHT, STATE, FRAME = 0, 128, 136, 160, 184


def wide(pack_ref, first):
    return jnp.concatenate([pack_ref[first + IP * part : first + IP * (part + 1)] for part in range(3)], axis=1)


def by_channel(w, count):
    return w == 4 and count == 128


def own_kernel(
    w, pair_any, tri_any, qkv_any, single_any, frame_any, columns_any, tri_out_any, bias_weight_any, frame_weight_any,
    gate_ref, rows_ref, pack_ref, pair_copy_any,
    pair_ref, gate_weight_ref, qkv_ref, single_ref, columns_ref, tri_out_ref, bias_weight_ref, frame_weight_ref, sems,
):
    r, count, _ = pair_ref.shape
    frame_ref = pack_ref.at[FRAME : FRAME + IP]
    for copy in copies(
        sems,
        (pair_any, pair_ref),
        (tri_any.at[:, 4 * CH :], gate_weight_ref),
        (qkv_any, qkv_ref),
        (single_any, single_ref),
        (frame_any, frame_ref),
        (columns_any, columns_ref),
        (tri_out_any, tri_out_ref),
        (bias_weight_any, bias_weight_ref),
        (frame_weight_any, frame_weight_ref),
    ):
        copy.wait()
    back = pltpu.make_async_copy(pair_ref, pair_copy_any, sems.at[9])
    back.start()
    if by_channel(w, count):
        row, column = grid_of((CH, CH))
        n = CH // w
        take = onehot(column == (row & (n - 1)) * w + (row >> log2(n)))
        gate_ref[r * count :, :] = dot(take, tri_out_ref[...]).astype(bf16)
    else:
        gate_ref[r * count :, :] = tri_out_ref[...]
    bias_weight = bias_weight_ref[...]
    spread = [jnp.broadcast_to(bias_weight[h : h + 1], (IP, CH)) for h in range(H)]
    bias_weight = jnp.concatenate(spread + [jnp.zeros((128 - ROWS, CH), f32)], axis=0).T
    _, lane = grid_of((CH, 128))
    pack_ref[BIAS : BIAS + CH, :] = jnp.where(lane < ROWS, bias_weight, columns_ref[0:CH, :])
    pack_ref[POINT_WEIGHT : POINT_WEIGHT + IP, :] = columns_ref[CH : CH + IP, :]
    state = pad_state(single_ref)
    frame_weight = frame_weight_ref[...]
    frame_weight = jnp.concatenate([frame_weight, jnp.zeros((IP - 6, CS), f32)], axis=0)
    for part in range(3):
        lanes = slice(128 * part, 128 * (part + 1))
        pack_ref[FRAME_WEIGHT + IP * part : FRAME_WEIGHT + IP * (part + 1), :] = frame_weight[:, lanes]
        pack_ref[STATE + IP * part : STATE + IP * (part + 1), :] = state[:, lanes]
    rows, lengths = own_side(state, frame_ref[...], qkv_ref, pack_ref[POINT_WEIGHT : POINT_WEIGHT + 1])
    rows_ref[:, 0:768] = rows
    rows_ref[:, 768:896] = jnp.broadcast_to(lengths, (ROWS, 128))
    for i in range(r):
        normed = layer_norm(pair_ref[i]).astype(bf16)
        gate_ref[i * count : (i + 1) * count] = jax.nn.sigmoid(dot(normed, gate_weight_ref[...])).astype(bf16)
    back.wait()


def prepare_kernel(w, n, r, mine_ref, other_ref, rows_ref, qkv_ref, pack_ref, logits_ref, values_ref):
    odd = pack_ref[POINT_WEIGHT + 1 : POINT_WEIGHT + 2, 0:1] > 0.5
    mine, other = mine_ref[...].astype(f32), other_ref[...].astype(f32)
    halves = [jnp.where(odd, other, mine).astype(bf16), jnp.where(odd, mine, other).astype(bf16)]
    slots = jnp.concatenate([quarter_of(halves[q & 1], 0, q >> 1, w, r, n) for q in range(4)], axis=1)
    logits, values = logits_and_values(
        slots, (rows_ref[:, 0:768], rows_ref[:, 768:769]), pack_ref[FRAME : FRAME + IP], qkv_ref[...],
        pack_ref[BIAS : BIAS + ROWS],
    )
    logits_ref[...] = logits
    values_ref[...] = values


def update_kernel(
    w, n, recv_ref, pair_any, gate_ref, logits_ref, values_ref, pack_ref, out_weight_ref,
    pair_out_any, half_ref, bias_ref, state_ref, new_frame_ref, send_ref, pair_ref, wide_ref, sems,
):
    r, count, _ = pair_ref.shape
    load = pltpu.make_async_copy(pair_any, pair_ref, sems.at[0])
    load.start()
    tri_out = gate_ref[r * count :, :]
    row, column = grid_of((2 * CH, 2 * CH))
    c = row & (CH - 1)
    take = onehot(column == (c >> log2(w)) * 2 * w + (row >> log2(CH)) * w + (c & (w - 1)))
    if by_channel(w, count):
        for low in range(2):
            wide_ref[low] = recv_ref[:, low * count : (low + 1) * count].astype(f32)
        product = jnp.concatenate(
            [
                jnp.concatenate([wide_ref[low, pl.ds(q, n, stride=2 * w), :] for q in range(2 * w)], axis=0)
                for low in range(2)
            ],
            axis=1,
        )
    else:
        product = dot(take, recv_ref[...])
    updates = []
    for high in range(2):
        normed = layer_norm(product[high * CH : (high + 1) * CH], axis=0).astype(bf16)
        updates.append(dot_tn(normed, tri_out))
    update = jnp.concatenate(updates, axis=0)
    bias_weight = pack_ref[BIAS : BIAS + CH, :]
    _, lane = grid_of((CH, 128))
    bias_weight = jnp.concatenate(
        [jnp.where(((lane & (IP - 1)) == i) & (lane < ROWS), bias_weight, 0.0) for i in range(r)], axis=0
    )
    load.wait()
    pair = pair_ref[...].reshape(r * count, CH)
    pair_out = pair + gate_ref[0 : r * count, :].astype(f32) * update
    pair_ref[...] = pair_out.reshape(r, count, CH)
    store = pltpu.make_async_copy(pair_ref, pair_out_any, sems.at[1])
    store.start()
    normed_pair = layer_norm(pair_out)
    halves = normed_pair.astype(bf16)
    half_ref[...] = halves
    side_by_side = jnp.concatenate([normed_pair[i * count : (i + 1) * count] for i in range(r)], axis=1)
    bias = (dot_close(side_by_side, bias_weight) * third).T[0:ROWS]
    bias_ref[...] = bias
    state, frame = attend(
        r, logits_ref[...] + bias, values_ref[...], halves, wide(pack_ref, STATE), pack_ref[FRAME : FRAME + IP],
        lambda: (out_weight_ref, wide(pack_ref, FRAME_WEIGHT)),
    )
    state_ref[...] = state
    new_frame_ref[...] = frame
    fill_rows(send_ref, 0, spread_rows(slots_of(state, frame), w, r))
    store.wait()


def last_kernel(
    w, n, r, recv_ref, half_ref, bias_ref, state_ref, frame_ref, pack_ref, qkv_ref, out_weight_ref,
    single_out_ref, rotation_ref, translation_ref, scr,
):
    slots = natural_rows(recv_ref, 0, w, r, n)
    state, frame = state_ref[...], frame_ref[...]
    own = own_side(state, frame, qkv_ref, pack_ref[POINT_WEIGHT : POINT_WEIGHT + 1])
    logits, values = logits_and_values(slots, own, frame, qkv_ref[...], pack_ref[BIAS : BIAS + ROWS])
    state, frame = attend(
        r, logits + bias_ref[...], values, half_ref[...], state, frame,
        lambda: (out_weight_ref, wide(pack_ref, FRAME_WEIGHT)),
    )
    single_out_ref[...] = state[0:r]
    rotation_ref[...] = frame[0:r, 0:9]
    scr[...] = jnp.concatenate([frame, jnp.zeros((128 - IP, 128), f32)], axis=0).T
    translation_ref[...] = scr[9:12, 0:r]


VMEM = pl.BlockSpec(memory_space=pltpu.VMEM)
HBM = pl.BlockSpec(memory_space=pltpu.HBM)


def call(body, name, outs, args, outside=(), outside_outs=(), scratch=(), limit=32, alias=None, flops=0, moved=0):
    return pl.pallas_call(
        body,
        name=name,
        out_shape=[jax.ShapeDtypeStruct(s, d) for s, d in outs],
        in_specs=[HBM if at in outside else VMEM for at in range(len(args))],
        out_specs=[HBM if at in outside_outs else VMEM for at in range(len(outs))],
        scratch_shapes=list(scratch),
        input_output_aliases=alias or {},
        compiler_params=pltpu.CompilerParams(vmem_limit_bytes=limit * 2**20),
        cost_estimate=pl.CostEstimate(flops=flops, bytes_accessed=moved, transcendentals=0),
    )(*args)


def local(
    pair, single, quats, translate, res_mask, chain_ids, tri_weight, tri_out_weight, qkv_weight, bias_weight,
    head_gamma, chain_bias, out_weight, frame_weight,
):
    n = lax.axis_size("row")
    r, count, _ = pair.shape
    w = CH // n
    rows = 2 * w
    lanes = r * SLOT // rows
    limit = 24 if count == 128 else 56

    def exchange(sent):
        width = sent.shape[1]
        got = lax.all_to_all(sent.reshape(n, rows, width), "row", 0, 0, tiled=True)
        return got.reshape(n * rows, width)

    def like(array):
        return pltpu.VMEM(array.shape, array.dtype)

    dma = pltpu.SemaphoreType.DMA
    sent, frame = call(
        functools.partial(gate_kernel, w, n),
        "gate",
        [((n * rows, r * count + lanes // 2), bf16), ((IP, 128), f32)],
        [pair, tri_weight, single, quats, translate, res_mask, chain_ids],
        outside=range(7),
        scratch=[
            like(pair),
            pltpu.VMEM((CH, 4 * CH), bf16),
            like(single),
            like(quats),
            like(translate),
            pltpu.SMEM((r,), jnp.int32),
            pltpu.SMEM((r,), jnp.int32),
            pltpu.VMEM((128, 128), f32),
            dma((7,)),
        ],
        limit=60,
    )
    received = exchange(sent)

    point_weight = head_gamma * (math.sqrt(2.0 / (9.0 * PQ)) * 0.5 * third)
    columns = jnp.pad(jnp.repeat(chain_bias.T, IP, axis=0), ((0, CH - ROWS + IP), (ROWS, 126 - ROWS)))
    columns = columns.at[CH, 0 : H * PQ].set(jnp.repeat(point_weight, PQ))
    columns = columns.at[CH + 1, 0].set((lax.axis_index("row") & 1).astype(f32))
    gate, query_rows, pack, pair_copy = call(
        functools.partial(own_kernel, w),
        "own",
        [
            ((r * count + CH, CH), bf16),
            ((ROWS, 896), f32),
            ((PACK_ROWS, 128), f32),
            (pair.shape, f32),
        ],
        [pair, tri_weight, qkv_weight, single, frame, columns, tri_out_weight, bias_weight.T, frame_weight.T],
        outside=range(9),
        outside_outs=(3,),
        scratch=[
            like(pair),
            pltpu.VMEM((CH, CH), bf16),
            like(qkv_weight),
            like(single),
            like(columns),
            like(tri_out_weight),
            pltpu.VMEM((H, CH), f32),
            pltpu.VMEM((6, CS), f32),
            dma((10,)),
        ],
        limit=60,
        flops=2 * r * count * CH * CH,
        moved=16 * 2**20,
    )
    received, gate, query_rows, pack, pair_copy = lax.optimization_barrier(
        (received, gate, query_rows, pack, pair_copy)
    )
    formed, slots = call(
        functools.partial(product_kernel, w, n, r),
        "product",
        [((n * rows, (r // 2) * count), bf16), ((n * rows, lanes // 2), bf16)],
        [received],
        scratch=[pltpu.VMEM((w, 256, 128), f32)],
        limit=limit,
    )
    products = exchange(formed)
    other = lax.ppermute(slots, "row", [(i, i ^ 1) for i in range(n)])
    logits, values = call(
        functools.partial(prepare_kernel, w, n, r),
        "prepare",
        [((ROWS, count), f32), ((count, 640), f32)],
        [slots, other, query_rows, qkv_weight, pack],
        limit=limit,
        flops=2 * count * CS * 1152,
        moved=8 * 2**20,
    )
    pair_out, pair_half, bias, state, frame, sent = call(
        functools.partial(update_kernel, w, n),
        "update",
        [
            ((r, count, CH), f32),
            ((r * count, CH), bf16),
            ((ROWS, count), f32),
            ((IP, CS), f32),
            ((IP, 128), f32),
            ((n * rows, lanes), bf16),
        ],
        [products, pair_copy, gate, logits, values, pack, out_weight],
        outside=(1,),
        outside_outs=(0,),
        alias={1: 0},
        scratch=[like(pair), pltpu.VMEM((2, 2 * CH, 128), f32), dma((2,))],
        limit=limit,
    )
    received = exchange(sent)
    single_out, rotation, translation = call(
        functools.partial(last_kernel, w, n, r),
        "last",
        [((r, CS), f32), ((r, 9), f32), ((3, r), f32)],
        [received, pair_half, bias, state, frame, pack, qkv_weight, out_weight],
        scratch=[pltpu.VMEM((128, 128), f32)],
        limit=limit,
    )
    return (pair_out, single_out, rotation.T, translation)


def solution(mesh):
    rows = ("grp", "row")
    placed = (P(rows, None, None), P(rows, None), P(None, rows), P(None, rows), P(rows), P(rows)) + (P(),) * 8
    return jax.shard_map(
        local,
        mesh=mesh,
        in_specs=placed,
        out_specs=(P(rows, None, None), P(rows, None), P(None, rows), P(None, rows)),
        check_vma=False,
    )
```

```python
import functools
import math

import jax
import jax.numpy as jnp
from jax import lax
from jax.experimental import pallas as pl
from jax.experimental.pallas import tpu as pltpu
from jax.sharding import PartitionSpec as P

CH = 128
CS = 384
H = 12
CHEAD = 16
PQ = 4
PV = 8
SLOT = 512
IP = 8
ROWS = H * IP
MASK_AT = 12
CHAIN_AT = 13

f32 = jnp.float32
bf16 = jnp.bfloat16
highest = lax.Precision.HIGHEST
epsilon = 1e-05
mask_fill = 100000.0
third = math.sqrt(1.0 / 3.0)


def layer_norm(values, axis=-1):
    center = values - jnp.mean(values, axis=axis, keepdims=True)
    spread = jnp.mean(center * center, axis=axis, keepdims=True)
    return center * lax.rsqrt(spread + epsilon)


def quat_entries(one, two, three, real):
    return [
        1.0 - 2.0 * (two * two + three * three),
        2.0 * (one * two - real * three),
        2.0 * (one * three + real * two),
        2.0 * (one * two + real * three),
        1.0 - 2.0 * (one * one + three * three),
        2.0 * (two * three - real * one),
        2.0 * (one * three - real * two),
        2.0 * (two * three + real * one),
        1.0 - 2.0 * (one * one + two * two),
    ]


def dot(a, b, precision=None):
    return lax.dot_general(
        a, b, (((1,), (0,)), ((), ())), precision=precision, preferred_element_type=f32
    )


def dot_nt(a, b, precision=None):
    return lax.dot_general(
        a, b, (((1,), (1,)), ((), ())), precision=precision, preferred_element_type=f32
    )


def dot_tn(a, b):
    return lax.dot_general(a, b, (((0,), (0,)), ((), ())), preferred_element_type=f32)


def halves_of(x):
    high = x.astype(bf16)
    return high, (x - high.astype(f32)).astype(bf16)


def dot_close(a, b):
    a_high, a_low = halves_of(a)
    b_high, b_low = halves_of(b)
    return dot(jnp.concatenate([a_high, a_low, a_high], axis=1), jnp.concatenate([b_high, b_high, b_low], axis=0))


def sigmoid(x):
    return 0.5 * jnp.tanh(0.5 * x) + 0.5


def log2(number):
    assert number & (number - 1) == 0
    return number.bit_length() - 1


def grid_of(shape):
    return lax.broadcasted_iota(jnp.int32, shape, 0), lax.broadcasted_iota(jnp.int32, shape, 1)


def onehot(match):
    return jnp.where(match, 1.0, 0.0).astype(bf16)


def swap_rows(count, minor_count):
    row, column = grid_of((count, count))
    major_count = count // minor_count
    minor = row >> log2(major_count)
    major = row & (major_count - 1)
    return onehot(column == major * minor_count + minor)


def spread_rows(slots, w, r):
    rows = 2 * w
    lanes = r * SLOT // rows
    if rows == 8 and r == 4:
        low, high = slots[0:IP, 0:lanes].astype(f32), slots[0:IP, lanes:].astype(f32)
        row, _ = grid_of((IP, lanes))
        one = jnp.where(row < r, low, pltpu.roll(high, r, 0))
        return jnp.concatenate([one, one], axis=0).astype(bf16)
    x, i = grid_of((16, 16))
    q = x & (rows - 1)
    if lanes <= SLOT:
        total = None
        for t in range(SLOT // lanes):
            one = dot(onehot((q == t * r + i) & (i < r)), slots[:, t * lanes : (t + 1) * lanes])
            total = one if total is None else total + one
        return total.astype(bf16)
    return jnp.concatenate(
        [dot(onehot(i == t * rows + q), slots) for t in range(lanes // SLOT)], axis=1
    ).astype(bf16)


def natural_rows(x_ref, first, w, r, n, start=0, stop=SLOT):
    rows = 2 * w
    lanes = r * SLOT // rows
    count = n * r
    j, x = grid_of((count, n * rows))
    s = x >> log2(rows)
    q = x & (rows - 1)
    if lanes <= SLOT:
        pieces = []
        for t in range(SLOT // lanes):
            low, high = max(start, t * lanes), min(stop, (t + 1) * lanes)
            if low < high:
                values = x_ref[:, first + low - t * lanes : first + high - t * lanes]
                pieces.append(dot(onehot((j == s * r + q - t * r) & ((q >> log2(r)) == t)), values))
        return pieces[0] if len(pieces) == 1 else jnp.concatenate(pieces, axis=1)
    total = None
    for t in range(lanes // SLOT):
        values = x_ref[:, first + t * SLOT + start : first + t * SLOT + stop]
        one = dot(onehot(j == s * r + t * rows + q), values)
        total = one if total is None else total + one
    return total


def frame_pieces(frame):
    high = frame.astype(bf16).astype(f32)
    rest = frame - high
    middle = rest.astype(bf16).astype(f32)
    low = (rest - middle).astype(bf16).astype(f32)
    return high + pltpu.roll(middle, 32, 1) + pltpu.roll(low, 64, 1)


def slots_of(state, frame):
    _, lane = grid_of((IP, 128))
    tail = state[:, 256:CS]
    mask = jnp.where(lane == 127, frame[:, MASK_AT : MASK_AT + 1], 0.0)
    moved = jnp.where((lane >= 112) & (lane < 120), pltpu.roll(tail, 120, 1), mask)
    last = jnp.where(lane < 96, frame_pieces(frame), moved)
    both = jnp.concatenate([state[:, 0:256], jnp.where(lane < 120, tail, mask), last], axis=1)
    return jnp.concatenate([both, jnp.zeros_like(both)], axis=0).astype(bf16)


def state_of(slots):
    _, lane = grid_of((slots.shape[0], 128))
    tail = jnp.where(lane < 120, slots[:, 256:384], pltpu.roll(slots[:, 384:512], 8, 1))
    return jnp.concatenate([slots[:, 0:256], tail], axis=1).astype(bf16)


def half_rows(slots, w, r):
    rows = 2 * w
    x, i = grid_of((16, 16))
    parity = (x >> log2(rows)) & 1
    blocks = []
    for at in range(2 * r // rows):
        b = (x & (rows - 1)) * (2 * r // rows) + at
        total = None
        for quarter in range(4):
            take = onehot((i == (b & (r - 1))) & (parity + 2 * (b >> log2(r)) == quarter))
            one = dot(take, slots[:, quarter * 128 : (quarter + 1) * 128])
            total = one if total is None else total + one
        blocks.append(total)
    return (blocks[0] if len(blocks) == 1 else jnp.concatenate(blocks, axis=1)).astype(bf16)


def quarter_of(x, first, second, w, r, n):
    rows = 2 * w
    j, row = grid_of((n * r, n * rows))
    total = None
    for at in range(2 * r // rows):
        b = (row & (rows - 1)) * (2 * r // rows) + at
        take = onehot((j == (row >> log2(rows)) * r + (b & (r - 1))) & ((b >> log2(r)) == second))
        one = dot(take, x[:, first + at * 128 : first + (at + 1) * 128])
        total = one if total is None else total + one
    return total


def fill_rows(out_ref, first, tile):
    lanes = tile.shape[1]
    for t in range(out_ref.shape[0] // 16):
        out_ref[t * 16 : (t + 1) * 16, first : first + lanes] = tile


def piece_select(row_count, transposed=False):
    if transposed:
        lane, entry = grid_of((128, row_count))
    else:
        entry, lane = grid_of((row_count, 128))
    return onehot(((lane & 31) == entry) & (lane < 96))


def copies(sems, *pairs):
    started = [pltpu.make_async_copy(src, dst, sems.at[at]) for at, (src, dst) in enumerate(pairs)]
    for copy in started:
        copy.start()
    return started


def gate_kernel(
    w, n, pair_any, tri_any, single_any, quats_any, translate_any, mask_any, chain_any, send_ref, frame_ref,
    pair_ref, tri_ref, single_ref, quats_ref, translate_ref, mask_ref, chain_ref, scr, sems,
):
    r, count, _ = pair_ref.shape
    loads = copies(
        sems,
        (pair_any, pair_ref),
        (tri_any.at[:, 0 : 4 * CH], tri_ref),
        (single_any, single_ref),
        (quats_any, quats_ref),
        (translate_any, translate_ref),
        (mask_any, mask_ref),
        (chain_any, chain_ref),
    )
    row, column = grid_of((2 * CH, 2 * CH))
    d = row >> log2(2 * w)
    side = (row >> log2(w)) & 1
    take = onehot(column == side * CH + d * w + (row & (w - 1)))
    for load in loads:
        load.wait()
    gate_weight = jnp.concatenate([tri_ref[:, 0:CH], tri_ref[:, 2 * CH : 3 * CH]], axis=1)
    value_weight = jnp.concatenate([tri_ref[:, CH : 2 * CH], tri_ref[:, 3 * CH : 4 * CH]], axis=1)
    gate_weight = dot_nt(take, gate_weight).astype(bf16)
    value_weight = dot_nt(take, value_weight).astype(bf16)
    normed = layer_norm(pair_ref[...].reshape(r * count, CH)).astype(bf16)
    gates = dot_nt(gate_weight, normed)
    values = dot_nt(value_weight, normed)
    mask = jnp.concatenate([jnp.full((1, count), mask_ref[i].astype(f32)) for i in range(r)], axis=1)
    send_ref[:, 0 : r * count] = (sigmoid(gates) * values * mask).astype(bf16)

    scr[...] = jnp.zeros_like(scr)
    quats = quats_ref[...]
    real = lax.rsqrt(1.0 + jnp.sum(quats * quats, axis=0, keepdims=True))
    unit = quats * real
    entries = quat_entries(unit[0:1], unit[1:2], unit[2:3], real)
    for at, entry in enumerate(entries):
        scr[at : at + 1, 0:r] = entry
    scr[9:12, 0:r] = translate_ref[...]
    frame = scr[...].T[0:IP, :]
    row, lane = grid_of((IP, 128))
    for i in range(r):
        frame = jnp.where((row == i) & (lane == MASK_AT), mask_ref[i].astype(f32), frame)
        frame = jnp.where((row == i) & (lane == CHAIN_AT), chain_ref[i].astype(f32), frame)
    frame_ref[...] = frame
    fill_rows(send_ref, r * count, half_rows(slots_of(pad_state(single_ref), frame), w, r))


def product_kernel(w, n, r, recv_ref, send_ref, slots_ref, right_ref):
    count = n * r
    slots_ref[...] = recv_ref[:, r * count :]
    rows = 2 * w
    pieces = quarter_of(recv_ref, r * count, 1, w, r, n).astype(bf16)
    _, lane = grid_of((16, 128))
    mask = dot_nt(onehot(lane == 127), pieces)[0:1, :]
    mask = jnp.concatenate([mask] * r, axis=1)
    order = swap_rows(n * rows, rows)
    sides = dot(order, recv_ref[:, 0 : r * count]) * mask
    row, column = grid_of((count, count))
    to_natural = onehot(row == (column & (n - 1)) * r + (column >> log2(n)))

    def stacked(block):
        part = sides[block * n : (block + 1) * n].astype(bf16)
        return jnp.concatenate([part[:, i * count : (i + 1) * count] for i in range(r)], axis=0)

    if by_channel(w, count):
        for c in range(w):
            for i in range(r):
                part = sides[(w + c) * n : (w + c + 1) * n, i * count : (i + 1) * count]
                right_ref[c, pl.ds(i, n, stride=r), :] = part

    def natural(c):
        if by_channel(w, count):
            return right_ref[c, 0:128].astype(bf16)
        return dot(to_natural, stacked(w + c)).astype(bf16)

    half = r // 2
    products = []
    for c in range(w):
        products.append(dot_nt(stacked(c), natural(c)))
    if by_channel(w, count):
        for high in range(2):
            for low in range(half):
                for c in range(w):
                    first = (high * half + low) * n
                    right_ref[low, pl.ds(high * w + c, n, stride=rows), :] = products[c][first : first + n]
        for low in range(half):
            send_ref[:, low * count : (low + 1) * count] = right_ref[low].astype(bf16)
        return
    products = [product.astype(bf16) for product in products]
    blocks = []
    for high in range(2):
        for c in range(w):
            first = high * half
            blocks.append(
                jnp.concatenate(
                    [products[c][(first + low) * n : (first + low + 1) * n] for low in range(half)], axis=1
                )
            )
    send_ref[...] = dot(swap_rows(n * rows, n), jnp.concatenate(blocks, axis=0)).astype(bf16)


def tiles(x):
    return [x[h * IP : (h + 1) * IP] for h in range(H)]


def own_side(state, frame, qkv_ref, point_weight):
    both = jnp.concatenate([state, jnp.zeros_like(state)], axis=0).astype(bf16)
    own = dot(both, jnp.concatenate([qkv_ref[:, 0:256], qkv_ref[:, 512:768]], axis=1))[0:IP]
    width = H * CHEAD
    count = H * PQ
    start = 3 * width - 256
    fill = jnp.zeros((IP, 128 - count), f32)
    own_local = [jnp.concatenate([own[:, start + a * count : start + (a + 1) * count], fill], axis=1) for a in range(3)]
    scalars = jnp.concatenate([jnp.zeros((IP, 256 - width), f32), own[:, 0:width]], axis=1)
    points = []
    for a in range(3):
        points.append(
            frame[:, 3 * a : 3 * a + 1] * own_local[0]
            + frame[:, 3 * a + 1 : 3 * a + 2] * own_local[1]
            + frame[:, 3 * a + 2 : 3 * a + 3] * own_local[2]
            + frame[:, 9 + a : 10 + a]
        )
    weight = jnp.broadcast_to(point_weight, (IP, 128))
    length = weight * (points[0] * points[0] + points[1] * points[1] + points[2] * points[2])
    everything = jnp.concatenate(
        [scalars * (third / math.sqrt(CHEAD))] + [2.0 * weight * p for p in points] + [-weight], axis=1
    )
    _, lane = grid_of((IP, 768))
    head = jnp.where(lane < 256, (lane - (256 - width)) >> log2(CHEAD), (lane & 127) >> log2(PQ))
    _, lane = grid_of((IP, 128))
    rows = []
    lengths = []
    for h in range(H):
        rows.append(jnp.where(head == h, everything, 0.0))
        lengths.append(-jnp.sum(jnp.where((lane >> log2(PQ)) == h, length, 0.0), axis=1, keepdims=True))
    return jnp.concatenate(rows, axis=0), jnp.concatenate(lengths, axis=0)


def logits_and_values(slots, own, frame, qkv, columns):
    query_rows, lengths = own
    pieces = slots[:, CS:SLOT].astype(bf16)
    entry = dot(pieces, piece_select(128, True))
    rows = dot_nt(piece_select(16), pieces)
    keys = dot(state_of(slots), qkv)
    points = H * PQ
    first = 3 * H * CHEAD + 3 * points
    _, lane = grid_of((keys.shape[0], 128))

    def block(start, size):
        at, offset = start // 128 * 128, start % 128
        one = keys[:, at : at + 128]
        if offset == 0:
            return one
        one = pltpu.roll(one, 128 - offset, 1)
        if offset + size <= 128:
            return one
        return jnp.where(lane < 128 - offset, one, pltpu.roll(keys[:, at + 128 : at + 256], 128 - offset, 1))

    local = []
    for a in range(3):
        value_points = block(first + 3 * points + a * H * PV, H * PV)
        local.append(jnp.concatenate([value_points, block(first + a * points, points)], axis=1))
    placed = []
    for a in range(3):
        placed.append(
            entry[:, 3 * a : 3 * a + 1] * local[0]
            + entry[:, 3 * a + 1 : 3 * a + 2] * local[1]
            + entry[:, 3 * a + 2 : 3 * a + 3] * local[2]
            + entry[:, 9 + a : 10 + a]
        )
    values = jnp.concatenate([keys[:, 384:640]] + [p[:, 0:128] for p in placed], axis=1)
    key_points = [p[:, 128:256] for p in placed]
    length = key_points[0] * key_points[0] + key_points[1] * key_points[1] + key_points[2] * key_points[2]
    key_side = jnp.concatenate([keys[:, 128:384]] + key_points + [length], axis=1)
    far = mask_fill * (rows[MASK_AT : MASK_AT + 1, :] - 1.0)
    chain = jnp.broadcast_to(rows[CHAIN_AT : CHAIN_AT + 1, :], (IP, rows.shape[1]))
    chain = jnp.concatenate([chain - frame[:, CHAIN_AT : CHAIN_AT + 1]] * H, axis=0)
    added = jnp.where(chain == 0.0, columns[:, ROWS + 1 : ROWS + 2], columns[:, ROWS : ROWS + 1]) + far + lengths
    return dot_nt(query_rows, key_side, highest) + added, values


def attend(r, logits, values, halves, state, frame, weights):
    top = jnp.max(logits, axis=1, keepdims=True)
    raised = jnp.exp(logits - top)
    share = 1.0 / jnp.sum(raised, axis=1, keepdims=True)
    row, _ = grid_of(raised.shape)
    parts = [jnp.where((row & (IP - 1)) == i, raised, 0.0).astype(bf16) for i in range(r)]
    out_pair = dot(jnp.concatenate(parts, axis=1), halves) * share
    summed = dot_close(raised, values) * share
    _, lane = grid_of((IP, 640))
    head = jnp.where(lane < 256, lane >> log2(CHEAD), (lane & 127) >> log2(PV))
    gathered = None
    for h, tile in enumerate(tiles(summed)):
        one = jnp.where(head == h, tile, 0.0)
        gathered = one if gathered is None else gathered + one
    relative = [
        gathered[:, 256 + 128 * a : 256 + 128 * a + H * PV] - frame[:, 9 + a : 10 + a] for a in range(3)
    ]
    out_local = [
        frame[:, a : a + 1] * relative[0]
        + frame[:, 3 + a : 4 + a] * relative[1]
        + frame[:, 6 + a : 7 + a] * relative[2]
        for a in range(3)
    ]
    out_norm = jnp.sqrt(
        out_local[0] * out_local[0] + out_local[1] * out_local[1] + out_local[2] * out_local[2] + 1e-08
    )
    out_ref, frame_weight = weights()

    def projected(blocks, first):
        rows = jnp.concatenate(blocks, axis=1)
        rows = jnp.concatenate([rows, jnp.zeros_like(rows)], axis=0).astype(bf16)
        return dot(rows, out_ref[first : first + rows.shape[1], :])[0:IP]

    from_pair = projected(tiles(out_pair), H * (CHEAD + 4 * PV))
    from_points = projected([gathered[:, 0 : H * CHEAD]] + out_local + [out_norm], 0)
    state = layer_norm(state + (from_points + from_pair))
    update = [jnp.sum(state * frame_weight[e : e + 1], axis=1, keepdims=True) for e in range(6)]
    quat = update[0:3]
    real = lax.rsqrt(1.0 + (quat[0] * quat[0] + quat[1] * quat[1] + quat[2] * quat[2]))
    step = quat_entries(quat[0] * real, quat[1] * real, quat[2] * real, real)
    old = [frame[:, e : e + 1] for e in range(9)]
    columns = []
    for target in range(3):
        for column in range(3):
            columns.append(
                old[target * 3] * step[column]
                + old[target * 3 + 1] * step[3 + column]
                + old[target * 3 + 2] * step[6 + column]
            )
    for target in range(3):
        columns.append(
            frame[:, 9 + target : 10 + target]
            + old[target * 3] * update[3]
            + old[target * 3 + 1] * update[4]
            + old[target * 3 + 2] * update[5]
        )
    _, lane = grid_of((IP, 128))
    for at, column in enumerate(columns):
        frame = jnp.where(lane == at, column, frame)
    return state, frame


def pad_state(single_ref):
    r = single_ref.shape[0]
    return jnp.concatenate([single_ref[...], jnp.zeros((IP - r, CS), f32)], axis=0)


PACK_ROWS = 192
BIAS, POINT_WEIGHT, FRAME_WEIGHT, STATE, FRAME = 0, 128, 136, 160, 184


def wide(pack_ref, first):
    return jnp.concatenate([pack_ref[first + IP * part : first + IP * (part + 1)] for part in range(3)], axis=1)


def by_channel(w, count):
    return w == 4 and count == 128


def own_kernel(
    w, pair_any, tri_any, qkv_any, single_any, frame_any, columns_any, tri_out_any, bias_weight_any, frame_weight_any,
    gate_ref, rows_ref, pack_ref, pair_copy_any,
    pair_ref, gate_weight_ref, qkv_ref, single_ref, columns_ref, tri_out_ref, bias_weight_ref, frame_weight_ref, sems,
):
    r, count, _ = pair_ref.shape
    frame_ref = pack_ref.at[FRAME : FRAME + IP]
    for copy in copies(
        sems,
        (pair_any, pair_ref),
        (tri_any.at[:, 4 * CH :], gate_weight_ref),
        (qkv_any, qkv_ref),
        (single_any, single_ref),
        (frame_any, frame_ref),
        (columns_any, columns_ref),
        (tri_out_any, tri_out_ref),
        (bias_weight_any, bias_weight_ref),
        (frame_weight_any, frame_weight_ref),
    ):
        copy.wait()
    back = pltpu.make_async_copy(pair_ref, pair_copy_any, sems.at[9])
    back.start()
    if by_channel(w, count):
        row, column = grid_of((CH, CH))
        n = CH // w
        take = onehot(column == (row & (n - 1)) * w + (row >> log2(n)))
        gate_ref[r * count :, :] = dot(take, tri_out_ref[...]).astype(bf16)
    else:
        gate_ref[r * count :, :] = tri_out_ref[...]
    bias_weight = bias_weight_ref[...]
    spread = [jnp.broadcast_to(bias_weight[h : h + 1], (IP, CH)) for h in range(H)]
    bias_weight = jnp.concatenate(spread + [jnp.zeros((128 - ROWS, CH), f32)], axis=0).T
    _, lane = grid_of((CH, 128))
    pack_ref[BIAS : BIAS + CH, :] = jnp.where(lane < ROWS, bias_weight, columns_ref[0:CH, :])
    pack_ref[POINT_WEIGHT : POINT_WEIGHT + IP, :] = columns_ref[CH : CH + IP, :]
    state = pad_state(single_ref)
    frame_weight = frame_weight_ref[...]
    frame_weight = jnp.concatenate([frame_weight, jnp.zeros((IP - 6, CS), f32)], axis=0)
    for part in range(3):
        lanes = slice(128 * part, 128 * (part + 1))
        pack_ref[FRAME_WEIGHT + IP * part : FRAME_WEIGHT + IP * (part + 1), :] = frame_weight[:, lanes]
        pack_ref[STATE + IP * part : STATE + IP * (part + 1), :] = state[:, lanes]
    rows, lengths = own_side(state, frame_ref[...], qkv_ref, pack_ref[POINT_WEIGHT : POINT_WEIGHT + 1])
    rows_ref[:, 0:768] = rows
    rows_ref[:, 768:896] = jnp.broadcast_to(lengths, (ROWS, 128))
    for i in range(r):
        normed = layer_norm(pair_ref[i]).astype(bf16)
        gate_ref[i * count : (i + 1) * count] = jax.nn.sigmoid(dot(normed, gate_weight_ref[...])).astype(bf16)
    back.wait()


def prepare_kernel(w, n, r, mine_ref, other_ref, rows_ref, qkv_ref, pack_ref, logits_ref, values_ref):
    odd = pack_ref[POINT_WEIGHT + 1 : POINT_WEIGHT + 2, 0:1] > 0.5
    mine, other = mine_ref[...].astype(f32), other_ref[...].astype(f32)
    halves = [jnp.where(odd, other, mine).astype(bf16), jnp.where(odd, mine, other).astype(bf16)]
    slots = jnp.concatenate([quarter_of(halves[q & 1], 0, q >> 1, w, r, n) for q in range(4)], axis=1)
    logits, values = logits_and_values(
        slots, (rows_ref[:, 0:768], rows_ref[:, 768:769]), pack_ref[FRAME : FRAME + IP], qkv_ref[...],
        pack_ref[BIAS : BIAS + ROWS],
    )
    logits_ref[...] = logits
    values_ref[...] = values


def update_kernel(
    w, n, recv_ref, pair_any, gate_ref, logits_ref, values_ref, pack_ref, out_weight_ref,
    pair_out_any, half_ref, bias_ref, state_ref, new_frame_ref, send_ref, pair_ref, wide_ref, sems,
):
    r, count, _ = pair_ref.shape
    load = pltpu.make_async_copy(pair_any, pair_ref, sems.at[0])
    load.start()
    tri_out = gate_ref[r * count :, :]
    row, column = grid_of((2 * CH, 2 * CH))
    c = row & (CH - 1)
    take = onehot(column == (c >> log2(w)) * 2 * w + (row >> log2(CH)) * w + (c & (w - 1)))
    if by_channel(w, count):
        for low in range(2):
            wide_ref[low] = recv_ref[:, low * count : (low + 1) * count].astype(f32)
        product = jnp.concatenate(
            [
                jnp.concatenate([wide_ref[low, pl.ds(q, n, stride=2 * w), :] for q in range(2 * w)], axis=0)
                for low in range(2)
            ],
            axis=1,
        )
    else:
        product = dot(take, recv_ref[...])
    updates = []
    for high in range(2):
        normed = layer_norm(product[high * CH : (high + 1) * CH], axis=0).astype(bf16)
        updates.append(dot_tn(normed, tri_out))
    update = jnp.concatenate(updates, axis=0)
    bias_weight = pack_ref[BIAS : BIAS + CH, :]
    _, lane = grid_of((CH, 128))
    bias_weight = jnp.concatenate(
        [jnp.where(((lane & (IP - 1)) == i) & (lane < ROWS), bias_weight, 0.0) for i in range(r)], axis=0
    )
    load.wait()
    pair = pair_ref[...].reshape(r * count, CH)
    pair_out = pair + gate_ref[0 : r * count, :].astype(f32) * update
    pair_ref[...] = pair_out.reshape(r, count, CH)
    store = pltpu.make_async_copy(pair_ref, pair_out_any, sems.at[1])
    store.start()
    normed_pair = layer_norm(pair_out)
    halves = normed_pair.astype(bf16)
    half_ref[...] = halves
    side_by_side = jnp.concatenate([normed_pair[i * count : (i + 1) * count] for i in range(r)], axis=1)
    bias = (dot_close(side_by_side, bias_weight) * third).T[0:ROWS]
    bias_ref[...] = bias
    state, frame = attend(
        r, logits_ref[...] + bias, values_ref[...], halves, wide(pack_ref, STATE), pack_ref[FRAME : FRAME + IP],
        lambda: (out_weight_ref, wide(pack_ref, FRAME_WEIGHT)),
    )
    state_ref[...] = state
    new_frame_ref[...] = frame
    fill_rows(send_ref, 0, spread_rows(slots_of(state, frame), w, r))
    store.wait()


def last_kernel(
    w, n, r, recv_ref, half_ref, bias_ref, state_ref, frame_ref, pack_ref, qkv_ref, out_weight_ref,
    single_out_ref, rotation_ref, translation_ref, scr, wide_ref, slots_ref,
):
    if by_channel(w, n * r):
        for low in range(2):
            wide_ref[low] = recv_ref[:, low * 128 : (low + 1) * 128].astype(f32)
        for quarter in range(4):
            for i in range(r):
                part = wide_ref[quarter & 1, pl.ds((quarter >> 1) * r + i, n, stride=2 * w), :]
                slots_ref[quarter, pl.ds(i, n, stride=r), :] = part
        slots = jnp.concatenate([slots_ref[quarter] for quarter in range(4)], axis=1)
    else:
        slots = natural_rows(recv_ref, 0, w, r, n)
    state, frame = state_ref[...], frame_ref[...]
    own = own_side(state, frame, qkv_ref, pack_ref[POINT_WEIGHT : POINT_WEIGHT + 1])
    logits, values = logits_and_values(slots, own, frame, qkv_ref[...], pack_ref[BIAS : BIAS + ROWS])
    state, frame = attend(
        r, logits + bias_ref[...], values, half_ref[...], state, frame,
        lambda: (out_weight_ref, wide(pack_ref, FRAME_WEIGHT)),
    )
    single_out_ref[...] = state[0:r]
    rotation_ref[...] = frame[0:r, 0:9]
    scr[...] = jnp.concatenate([frame, jnp.zeros((128 - IP, 128), f32)], axis=0).T
    translation_ref[...] = scr[9:12, 0:r]


VMEM = pl.BlockSpec(memory_space=pltpu.VMEM)
HBM = pl.BlockSpec(memory_space=pltpu.HBM)


def call(body, name, outs, args, outside=(), outside_outs=(), scratch=(), limit=32, alias=None, flops=0, moved=0):
    return pl.pallas_call(
        body,
        name=name,
        out_shape=[jax.ShapeDtypeStruct(s, d) for s, d in outs],
        in_specs=[HBM if at in outside else VMEM for at in range(len(args))],
        out_specs=[HBM if at in outside_outs else VMEM for at in range(len(outs))],
        scratch_shapes=list(scratch),
        input_output_aliases=alias or {},
        compiler_params=pltpu.CompilerParams(vmem_limit_bytes=limit * 2**20),
        cost_estimate=pl.CostEstimate(flops=flops, bytes_accessed=moved, transcendentals=0),
    )(*args)


def local(
    pair, single, quats, translate, res_mask, chain_ids, tri_weight, tri_out_weight, qkv_weight, bias_weight,
    head_gamma, chain_bias, out_weight, frame_weight,
):
    n = lax.axis_size("row")
    r, count, _ = pair.shape
    w = CH // n
    rows = 2 * w
    lanes = r * SLOT // rows
    limit = 24 if count == 128 else 56

    def exchange(sent):
        width = sent.shape[1]
        got = lax.all_to_all(sent.reshape(n, rows, width), "row", 0, 0, tiled=True)
        return got.reshape(n * rows, width)

    def like(array):
        return pltpu.VMEM(array.shape, array.dtype)

    dma = pltpu.SemaphoreType.DMA
    sent, frame = call(
        functools.partial(gate_kernel, w, n),
        "gate",
        [((n * rows, r * count + lanes // 2), bf16), ((IP, 128), f32)],
        [pair, tri_weight, single, quats, translate, res_mask, chain_ids],
        outside=range(7),
        scratch=[
            like(pair),
            pltpu.VMEM((CH, 4 * CH), bf16),
            like(single),
            like(quats),
            like(translate),
            pltpu.SMEM((r,), jnp.int32),
            pltpu.SMEM((r,), jnp.int32),
            pltpu.VMEM((128, 128), f32),
            dma((7,)),
        ],
        limit=60,
    )
    received = exchange(sent)

    point_weight = head_gamma * (math.sqrt(2.0 / (9.0 * PQ)) * 0.5 * third)
    columns = jnp.pad(jnp.repeat(chain_bias.T, IP, axis=0), ((0, CH - ROWS + IP), (ROWS, 126 - ROWS)))
    columns = columns.at[CH, 0 : H * PQ].set(jnp.repeat(point_weight, PQ))
    columns = columns.at[CH + 1, 0].set((lax.axis_index("row") & 1).astype(f32))
    gate, query_rows, pack, pair_copy = call(
        functools.partial(own_kernel, w),
        "own",
        [
            ((r * count + CH, CH), bf16),
            ((ROWS, 896), f32),
            ((PACK_ROWS, 128), f32),
            (pair.shape, f32),
        ],
        [pair, tri_weight, qkv_weight, single, frame, columns, tri_out_weight, bias_weight.T, frame_weight.T],
        outside=range(9),
        outside_outs=(3,),
        scratch=[
            like(pair),
            pltpu.VMEM((CH, CH), bf16),
            like(qkv_weight),
            like(single),
            like(columns),
            like(tri_out_weight),
            pltpu.VMEM((H, CH), f32),
            pltpu.VMEM((6, CS), f32),
            dma((10,)),
        ],
        limit=60,
        flops=2 * r * count * CH * CH,
        moved=16 * 2**20,
    )
    received, gate, query_rows, pack, pair_copy = lax.optimization_barrier(
        (received, gate, query_rows, pack, pair_copy)
    )
    formed, slots = call(
        functools.partial(product_kernel, w, n, r),
        "product",
        [((n * rows, (r // 2) * count), bf16), ((n * rows, lanes // 2), bf16)],
        [received],
        scratch=[pltpu.VMEM((w, 256, 128), f32)],
        limit=limit,
    )
    products = exchange(formed)
    other = lax.ppermute(slots, "row", [(i, i ^ 1) for i in range(n)])
    logits, values = call(
        functools.partial(prepare_kernel, w, n, r),
        "prepare",
        [((ROWS, count), f32), ((count, 640), f32)],
        [slots, other, query_rows, qkv_weight, pack],
        limit=limit,
        flops=2 * count * CS * 1152,
        moved=8 * 2**20,
    )
    pair_out, pair_half, bias, state, frame, sent = call(
        functools.partial(update_kernel, w, n),
        "update",
        [
            ((r, count, CH), f32),
            ((r * count, CH), bf16),
            ((ROWS, count), f32),
            ((IP, CS), f32),
            ((IP, 128), f32),
            ((n * rows, lanes), bf16),
        ],
        [products, pair_copy, gate, logits, values, pack, out_weight],
        outside=(1,),
        outside_outs=(0,),
        alias={1: 0},
        scratch=[like(pair), pltpu.VMEM((2, 2 * CH, 128), f32), dma((2,))],
        limit=limit,
    )
    received = exchange(sent)
    single_out, rotation, translation = call(
        functools.partial(last_kernel, w, n, r),
        "last",
        [((r, CS), f32), ((r, 9), f32), ((3, r), f32)],
        [received, pair_half, bias, state, frame, pack, qkv_weight, out_weight],
        scratch=[pltpu.VMEM((128, 128), f32), pltpu.VMEM((2, 256, 128), f32), pltpu.VMEM((4, 128, 128), f32)],
        limit=limit,
    )
    return (pair_out, single_out, rotation.T, translation)


def solution(mesh):
    rows = ("grp", "row")
    placed = (P(rows, None, None), P(rows, None), P(None, rows), P(None, rows), P(rows), P(rows)) + (P(),) * 8
    return jax.shard_map(
        local,
        mesh=mesh,
        in_specs=placed,
        out_specs=(P(rows, None, None), P(rows, None), P(None, rows), P(None, rows)),
        check_vma=False,
    )
```

```python
import functools
import math

import jax
import jax.numpy as jnp
from jax import lax
from jax.experimental import pallas as pl
from jax.experimental.pallas import tpu as pltpu
from jax.sharding import PartitionSpec as P

CH = 128
CS = 384
H = 12
CHEAD = 16
PQ = 4
PV = 8
SLOT = 512
IP = 8
ROWS = H * IP
MASK_AT = 12
CHAIN_AT = 13

f32 = jnp.float32
bf16 = jnp.bfloat16
highest = lax.Precision.HIGHEST
epsilon = 1e-05
mask_fill = 100000.0
third = math.sqrt(1.0 / 3.0)


def layer_norm(values, axis=-1):
    center = values - jnp.mean(values, axis=axis, keepdims=True)
    spread = jnp.mean(center * center, axis=axis, keepdims=True)
    return center * lax.rsqrt(spread + epsilon)


def quat_entries(one, two, three, real):
    return [
        1.0 - 2.0 * (two * two + three * three),
        2.0 * (one * two - real * three),
        2.0 * (one * three + real * two),
        2.0 * (one * two + real * three),
        1.0 - 2.0 * (one * one + three * three),
        2.0 * (two * three - real * one),
        2.0 * (one * three - real * two),
        2.0 * (two * three + real * one),
        1.0 - 2.0 * (one * one + two * two),
    ]


def dot(a, b, precision=None):
    return lax.dot_general(
        a, b, (((1,), (0,)), ((), ())), precision=precision, preferred_element_type=f32
    )


def dot_nt(a, b, precision=None):
    return lax.dot_general(
        a, b, (((1,), (1,)), ((), ())), precision=precision, preferred_element_type=f32
    )


def dot_tn(a, b):
    return lax.dot_general(a, b, (((0,), (0,)), ((), ())), preferred_element_type=f32)


def halves_of(x):
    high = x.astype(bf16)
    return high, (x - high.astype(f32)).astype(bf16)


def dot_close(a, b):
    a_high, a_low = halves_of(a)
    b_high, b_low = halves_of(b)
    return dot(jnp.concatenate([a_high, a_low, a_high], axis=1), jnp.concatenate([b_high, b_high, b_low], axis=0))


def sigmoid(x):
    return 0.5 * jnp.tanh(0.5 * x) + 0.5


def log2(number):
    assert number & (number - 1) == 0
    return number.bit_length() - 1


def grid_of(shape):
    return lax.broadcasted_iota(jnp.int32, shape, 0), lax.broadcasted_iota(jnp.int32, shape, 1)


def onehot(match):
    return jnp.where(match, 1.0, 0.0).astype(bf16)


def swap_rows(count, minor_count):
    row, column = grid_of((count, count))
    major_count = count // minor_count
    minor = row >> log2(major_count)
    major = row & (major_count - 1)
    return onehot(column == major * minor_count + minor)


def spread_rows(slots, w, r):
    rows = 2 * w
    lanes = r * SLOT // rows
    if rows == 8 and r == 4:
        low, high = slots[0:IP, 0:lanes].astype(f32), slots[0:IP, lanes:].astype(f32)
        row, _ = grid_of((IP, lanes))
        one = jnp.where(row < r, low, pltpu.roll(high, r, 0))
        return jnp.concatenate([one, one], axis=0).astype(bf16)
    x, i = grid_of((16, 16))
    q = x & (rows - 1)
    if lanes <= SLOT:
        total = None
        for t in range(SLOT // lanes):
            one = dot(onehot((q == t * r + i) & (i < r)), slots[:, t * lanes : (t + 1) * lanes])
            total = one if total is None else total + one
        return total.astype(bf16)
    return jnp.concatenate(
        [dot(onehot(i == t * rows + q), slots) for t in range(lanes // SLOT)], axis=1
    ).astype(bf16)


def natural_rows(x_ref, first, w, r, n, start=0, stop=SLOT):
    rows = 2 * w
    lanes = r * SLOT // rows
    count = n * r
    j, x = grid_of((count, n * rows))
    s = x >> log2(rows)
    q = x & (rows - 1)
    if lanes <= SLOT:
        pieces = []
        for t in range(SLOT // lanes):
            low, high = max(start, t * lanes), min(stop, (t + 1) * lanes)
            if low < high:
                values = x_ref[:, first + low - t * lanes : first + high - t * lanes]
                pieces.append(dot(onehot((j == s * r + q - t * r) & ((q >> log2(r)) == t)), values))
        return pieces[0] if len(pieces) == 1 else jnp.concatenate(pieces, axis=1)
    total = None
    for t in range(lanes // SLOT):
        values = x_ref[:, first + t * SLOT + start : first + t * SLOT + stop]
        one = dot(onehot(j == s * r + t * rows + q), values)
        total = one if total is None else total + one
    return total


def frame_pieces(frame):
    high = frame.astype(bf16).astype(f32)
    rest = frame - high
    middle = rest.astype(bf16).astype(f32)
    low = (rest - middle).astype(bf16).astype(f32)
    return high + pltpu.roll(middle, 32, 1) + pltpu.roll(low, 64, 1)


def slots_of(state, frame):
    _, lane = grid_of((IP, 128))
    tail = state[:, 256:CS]
    mask = jnp.where(lane == 127, frame[:, MASK_AT : MASK_AT + 1], 0.0)
    moved = jnp.where((lane >= 112) & (lane < 120), pltpu.roll(tail, 120, 1), mask)
    last = jnp.where(lane < 96, frame_pieces(frame), moved)
    both = jnp.concatenate([state[:, 0:256], jnp.where(lane < 120, tail, mask), last], axis=1)
    return jnp.concatenate([both, jnp.zeros_like(both)], axis=0).astype(bf16)


def state_of(slots):
    _, lane = grid_of((slots.shape[0], 128))
    tail = jnp.where(lane < 120, slots[:, 256:384], pltpu.roll(slots[:, 384:512], 8, 1))
    return jnp.concatenate([slots[:, 0:256], tail], axis=1).astype(bf16)


def half_rows(slots, w, r):
    rows = 2 * w
    x, i = grid_of((16, 16))
    parity = (x >> log2(rows)) & 1
    blocks = []
    for at in range(2 * r // rows):
        b = (x & (rows - 1)) * (2 * r // rows) + at
        total = None
        for quarter in range(4):
            take = onehot((i == (b & (r - 1))) & (parity + 2 * (b >> log2(r)) == quarter))
            one = dot(take, slots[:, quarter * 128 : (quarter + 1) * 128])
            total = one if total is None else total + one
        blocks.append(total)
    return (blocks[0] if len(blocks) == 1 else jnp.concatenate(blocks, axis=1)).astype(bf16)


def quarter_of(x, first, second, w, r, n):
    rows = 2 * w
    j, row = grid_of((n * r, n * rows))
    total = None
    for at in range(2 * r // rows):
        b = (row & (rows - 1)) * (2 * r // rows) + at
        take = onehot((j == (row >> log2(rows)) * r + (b & (r - 1))) & ((b >> log2(r)) == second))
        one = dot(take, x[:, first + at * 128 : first + (at + 1) * 128])
        total = one if total is None else total + one
    return total


def fill_rows(out_ref, first, tile):
    lanes = tile.shape[1]
    for t in range(out_ref.shape[0] // 16):
        out_ref[t * 16 : (t + 1) * 16, first : first + lanes] = tile


def piece_select(row_count, transposed=False):
    if transposed:
        lane, entry = grid_of((128, row_count))
    else:
        entry, lane = grid_of((row_count, 128))
    return onehot(((lane & 31) == entry) & (lane < 96))


def copies(sems, *pairs):
    started = [pltpu.make_async_copy(src, dst, sems.at[at]) for at, (src, dst) in enumerate(pairs)]
    for copy in started:
        copy.start()
    return started


def gate_kernel(
    w, n, pair_any, tri_any, single_any, quats_any, translate_any, mask_any, chain_any, send_ref, frame_ref,
    pair_ref, tri_ref, single_ref, quats_ref, translate_ref, mask_ref, chain_ref, scr, sems,
):
    r, count, _ = pair_ref.shape
    loads = copies(
        sems,
        *((pair_any.at[i], pair_ref.at[i]) for i in range(r)),
        (tri_any.at[:, 0 : 4 * CH], tri_ref),
        (single_any, single_ref),
        (quats_any, quats_ref),
        (translate_any, translate_ref),
        (mask_any, mask_ref),
        (chain_any, chain_ref),
    )
    row, column = grid_of((2 * CH, 2 * CH))
    d = row >> log2(2 * w)
    side = (row >> log2(w)) & 1
    take = onehot(column == side * CH + d * w + (row & (w - 1)))
    for load in loads:
        load.wait()
    gate_weight = jnp.concatenate([tri_ref[:, 0:CH], tri_ref[:, 2 * CH : 3 * CH]], axis=1)
    value_weight = jnp.concatenate([tri_ref[:, CH : 2 * CH], tri_ref[:, 3 * CH : 4 * CH]], axis=1)
    gate_weight = dot_nt(take, gate_weight).astype(bf16)
    value_weight = dot_nt(take, value_weight).astype(bf16)
    normed = layer_norm(pair_ref[...].reshape(r * count, CH)).astype(bf16)
    gates = dot_nt(gate_weight, normed)
    values = dot_nt(value_weight, normed)
    mask = jnp.concatenate([jnp.full((1, count), mask_ref[i].astype(f32)) for i in range(r)], axis=1)
    send_ref[:, 0 : r * count] = (sigmoid(gates) * values * mask).astype(bf16)

    scr[...] = jnp.zeros_like(scr)
    quats = quats_ref[...]
    real = lax.rsqrt(1.0 + jnp.sum(quats * quats, axis=0, keepdims=True))
    unit = quats * real
    entries = quat_entries(unit[0:1], unit[1:2], unit[2:3], real)
    for at, entry in enumerate(entries):
        scr[at : at + 1, 0:r] = entry
    scr[9:12, 0:r] = translate_ref[...]
    frame = scr[...].T[0:IP, :]
    row, lane = grid_of((IP, 128))
    for i in range(r):
        frame = jnp.where((row == i) & (lane == MASK_AT), mask_ref[i].astype(f32), frame)
        frame = jnp.where((row == i) & (lane == CHAIN_AT), chain_ref[i].astype(f32), frame)
    frame_ref[...] = frame
    fill_rows(send_ref, r * count, half_rows(slots_of(pad_state(single_ref), frame), w, r))


def product_kernel(w, n, r, recv_ref, send_ref, slots_ref, right_ref):
    count = n * r
    slots_ref[...] = recv_ref[:, r * count :]
    rows = 2 * w
    pieces = quarter_of(recv_ref, r * count, 1, w, r, n).astype(bf16)
    _, lane = grid_of((16, 128))
    mask = dot_nt(onehot(lane == 127), pieces)[0:1, :]
    mask = jnp.concatenate([mask] * r, axis=1)
    order = swap_rows(n * rows, rows)
    sides = dot(order, recv_ref[:, 0 : r * count]) * mask
    row, column = grid_of((count, count))
    to_natural = onehot(row == (column & (n - 1)) * r + (column >> log2(n)))

    def stacked(block):
        part = sides[block * n : (block + 1) * n].astype(bf16)
        return jnp.concatenate([part[:, i * count : (i + 1) * count] for i in range(r)], axis=0)

    if by_channel(w, count):
        for c in range(w):
            for i in range(r):
                part = sides[(w + c) * n : (w + c + 1) * n, i * count : (i + 1) * count]
                right_ref[c, pl.ds(i, n, stride=r), :] = part

    def natural(c):
        if by_channel(w, count):
            return right_ref[c, 0:128].astype(bf16)
        return dot(to_natural, stacked(w + c)).astype(bf16)

    half = r // 2
    products = []
    for c in range(w):
        products.append(dot_nt(stacked(c), natural(c)))
    if by_channel(w, count):
        for high in range(2):
            for low in range(half):
                for c in range(w):
                    first = (high * half + low) * n
                    right_ref[low, pl.ds(high * w + c, n, stride=rows), :] = products[c][first : first + n]
        for low in range(half):
            send_ref[:, low * count : (low + 1) * count] = right_ref[low].astype(bf16)
        return
    products = [product.astype(bf16) for product in products]
    blocks = []
    for high in range(2):
        for c in range(w):
            first = high * half
            blocks.append(
                jnp.concatenate(
                    [products[c][(first + low) * n : (first + low + 1) * n] for low in range(half)], axis=1
                )
            )
    send_ref[...] = dot(swap_rows(n * rows, n), jnp.concatenate(blocks, axis=0)).astype(bf16)


def tiles(x):
    return [x[h * IP : (h + 1) * IP] for h in range(H)]


def own_side(state, frame, qkv_ref, point_weight):
    both = jnp.concatenate([state, jnp.zeros_like(state)], axis=0).astype(bf16)
    own = dot(both, jnp.concatenate([qkv_ref[:, 0:256], qkv_ref[:, 512:768]], axis=1))[0:IP]
    width = H * CHEAD
    count = H * PQ
    start = 3 * width - 256
    fill = jnp.zeros((IP, 128 - count), f32)
    own_local = [jnp.concatenate([own[:, start + a * count : start + (a + 1) * count], fill], axis=1) for a in range(3)]
    scalars = jnp.concatenate([jnp.zeros((IP, 256 - width), f32), own[:, 0:width]], axis=1)
    points = []
    for a in range(3):
        points.append(
            frame[:, 3 * a : 3 * a + 1] * own_local[0]
            + frame[:, 3 * a + 1 : 3 * a + 2] * own_local[1]
            + frame[:, 3 * a + 2 : 3 * a + 3] * own_local[2]
            + frame[:, 9 + a : 10 + a]
        )
    weight = jnp.broadcast_to(point_weight, (IP, 128))
    length = weight * (points[0] * points[0] + points[1] * points[1] + points[2] * points[2])
    everything = jnp.concatenate(
        [scalars * (third / math.sqrt(CHEAD))] + [2.0 * weight * p for p in points] + [-weight], axis=1
    )
    _, lane = grid_of((IP, 768))
    head = jnp.where(lane < 256, (lane - (256 - width)) >> log2(CHEAD), (lane & 127) >> log2(PQ))
    _, lane = grid_of((IP, 128))
    rows = []
    lengths = []
    for h in range(H):
        rows.append(jnp.where(head == h, everything, 0.0))
        lengths.append(-jnp.sum(jnp.where((lane >> log2(PQ)) == h, length, 0.0), axis=1, keepdims=True))
    return jnp.concatenate(rows, axis=0), jnp.concatenate(lengths, axis=0)


def logits_and_values(slots, own, frame, qkv, columns):
    query_rows, lengths = own
    pieces = slots[:, CS:SLOT].astype(bf16)
    entry = dot(pieces, piece_select(128, True))
    rows = dot_nt(piece_select(16), pieces)
    keys = dot(state_of(slots), qkv)
    points = H * PQ
    first = 3 * H * CHEAD + 3 * points
    _, lane = grid_of((keys.shape[0], 128))

    def block(start, size):
        at, offset = start // 128 * 128, start % 128
        one = keys[:, at : at + 128]
        if offset == 0:
            return one
        one = pltpu.roll(one, 128 - offset, 1)
        if offset + size <= 128:
            return one
        return jnp.where(lane < 128 - offset, one, pltpu.roll(keys[:, at + 128 : at + 256], 128 - offset, 1))

    local = []
    for a in range(3):
        value_points = block(first + 3 * points + a * H * PV, H * PV)
        local.append(jnp.concatenate([value_points, block(first + a * points, points)], axis=1))
    placed = []
    for a in range(3):
        placed.append(
            entry[:, 3 * a : 3 * a + 1] * local[0]
            + entry[:, 3 * a + 1 : 3 * a + 2] * local[1]
            + entry[:, 3 * a + 2 : 3 * a + 3] * local[2]
            + entry[:, 9 + a : 10 + a]
        )
    values = jnp.concatenate([keys[:, 384:640]] + [p[:, 0:128] for p in placed], axis=1)
    key_points = [p[:, 128:256] for p in placed]
    length = key_points[0] * key_points[0] + key_points[1] * key_points[1] + key_points[2] * key_points[2]
    key_side = jnp.concatenate([keys[:, 128:384]] + key_points + [length], axis=1)
    far = mask_fill * (rows[MASK_AT : MASK_AT + 1, :] - 1.0)
    chain = jnp.broadcast_to(rows[CHAIN_AT : CHAIN_AT + 1, :], (IP, rows.shape[1]))
    chain = jnp.concatenate([chain - frame[:, CHAIN_AT : CHAIN_AT + 1]] * H, axis=0)
    added = jnp.where(chain == 0.0, columns[:, ROWS + 1 : ROWS + 2], columns[:, ROWS : ROWS + 1]) + far + lengths
    return dot_nt(query_rows, key_side, highest) + added, values


def attend(r, logits, values, halves, state, frame, weights):
    top = jnp.max(logits, axis=1, keepdims=True)
    raised = jnp.exp(logits - top)
    share = 1.0 / jnp.sum(raised, axis=1, keepdims=True)
    row, _ = grid_of(raised.shape)
    parts = [jnp.where((row & (IP - 1)) == i, raised, 0.0).astype(bf16) for i in range(r)]
    out_pair = dot(jnp.concatenate(parts, axis=1), halves) * share
    summed = dot_close(raised, values) * share
    _, lane = grid_of((IP, 640))
    head = jnp.where(lane < 256, lane >> log2(CHEAD), (lane & 127) >> log2(PV))
    gathered = None
    for h, tile in enumerate(tiles(summed)):
        one = jnp.where(head == h, tile, 0.0)
        gathered = one if gathered is None else gathered + one
    relative = [
        gathered[:, 256 + 128 * a : 256 + 128 * a + H * PV] - frame[:, 9 + a : 10 + a] for a in range(3)
    ]
    out_local = [
        frame[:, a : a + 1] * relative[0]
        + frame[:, 3 + a : 4 + a] * relative[1]
        + frame[:, 6 + a : 7 + a] * relative[2]
        for a in range(3)
    ]
    out_norm = jnp.sqrt(
        out_local[0] * out_local[0] + out_local[1] * out_local[1] + out_local[2] * out_local[2] + 1e-08
    )
    out_ref, frame_weight = weights()

    def projected(blocks, first):
        rows = jnp.concatenate(blocks, axis=1)
        rows = jnp.concatenate([rows, jnp.zeros_like(rows)], axis=0).astype(bf16)
        return dot(rows, out_ref[first : first + rows.shape[1], :])[0:IP]

    from_pair = projected(tiles(out_pair), H * (CHEAD + 4 * PV))
    from_points = projected([gathered[:, 0 : H * CHEAD]] + out_local + [out_norm], 0)
    state = layer_norm(state + (from_points + from_pair))
    update = [jnp.sum(state * frame_weight[e : e + 1], axis=1, keepdims=True) for e in range(6)]
    quat = update[0:3]
    real = lax.rsqrt(1.0 + (quat[0] * quat[0] + quat[1] * quat[1] + quat[2] * quat[2]))
    step = quat_entries(quat[0] * real, quat[1] * real, quat[2] * real, real)
    old = [frame[:, e : e + 1] for e in range(9)]
    columns = []
    for target in range(3):
        for column in range(3):
            columns.append(
                old[target * 3] * step[column]
                + old[target * 3 + 1] * step[3 + column]
                + old[target * 3 + 2] * step[6 + column]
            )
    for target in range(3):
        columns.append(
            frame[:, 9 + target : 10 + target]
            + old[target * 3] * update[3]
            + old[target * 3 + 1] * update[4]
            + old[target * 3 + 2] * update[5]
        )
    _, lane = grid_of((IP, 128))
    for at, column in enumerate(columns):
        frame = jnp.where(lane == at, column, frame)
    return state, frame


def pad_state(single_ref):
    r = single_ref.shape[0]
    return jnp.concatenate([single_ref[...], jnp.zeros((IP - r, CS), f32)], axis=0)


PACK_ROWS = 192
BIAS, POINT_WEIGHT, FRAME_WEIGHT, STATE, FRAME = 0, 128, 136, 160, 184


def wide(pack_ref, first):
    return jnp.concatenate([pack_ref[first + IP * part : first + IP * (part + 1)] for part in range(3)], axis=1)


def by_channel(w, count):
    return w == 4 and count == 128


def own_kernel(
    w, pair_any, tri_any, qkv_any, single_any, frame_any, columns_any, tri_out_any, bias_weight_any, frame_weight_any,
    gate_ref, rows_ref, pack_ref, pair_copy_any,
    pair_ref, gate_weight_ref, qkv_ref, single_ref, columns_ref, tri_out_ref, bias_weight_ref, frame_weight_ref, sems,
):
    r, count, _ = pair_ref.shape
    frame_ref = pack_ref.at[FRAME : FRAME + IP]
    for copy in copies(
        sems,
        (pair_any, pair_ref),
        (tri_any.at[:, 4 * CH :], gate_weight_ref),
        (qkv_any, qkv_ref),
        (single_any, single_ref),
        (frame_any, frame_ref),
        (columns_any, columns_ref),
        (tri_out_any, tri_out_ref),
        (bias_weight_any, bias_weight_ref),
        (frame_weight_any, frame_weight_ref),
    ):
        copy.wait()
    back = pltpu.make_async_copy(pair_ref, pair_copy_any, sems.at[9])
    back.start()
    if by_channel(w, count):
        row, column = grid_of((CH, CH))
        n = CH // w
        take = onehot(column == (row & (n - 1)) * w + (row >> log2(n)))
        gate_ref[r * count :, :] = dot(take, tri_out_ref[...]).astype(bf16)
    else:
        gate_ref[r * count :, :] = tri_out_ref[...]
    bias_weight = bias_weight_ref[...]
    spread = [jnp.broadcast_to(bias_weight[h : h + 1], (IP, CH)) for h in range(H)]
    bias_weight = jnp.concatenate(spread + [jnp.zeros((128 - ROWS, CH), f32)], axis=0).T
    _, lane = grid_of((CH, 128))
    pack_ref[BIAS : BIAS + CH, :] = jnp.where(lane < ROWS, bias_weight, columns_ref[0:CH, :])
    pack_ref[POINT_WEIGHT : POINT_WEIGHT + IP, :] = columns_ref[CH : CH + IP, :]
    state = pad_state(single_ref)
    frame_weight = frame_weight_ref[...]
    frame_weight = jnp.concatenate([frame_weight, jnp.zeros((IP - 6, CS), f32)], axis=0)
    for part in range(3):
        lanes = slice(128 * part, 128 * (part + 1))
        pack_ref[FRAME_WEIGHT + IP * part : FRAME_WEIGHT + IP * (part + 1), :] = frame_weight[:, lanes]
        pack_ref[STATE + IP * part : STATE + IP * (part + 1), :] = state[:, lanes]
    rows, lengths = own_side(state, frame_ref[...], qkv_ref, pack_ref[POINT_WEIGHT : POINT_WEIGHT + 1])
    rows_ref[:, 0:768] = rows
    rows_ref[:, 768:896] = jnp.broadcast_to(lengths, (ROWS, 128))
    for i in range(r):
        normed = layer_norm(pair_ref[i]).astype(bf16)
        gate_ref[i * count : (i + 1) * count] = jax.nn.sigmoid(dot(normed, gate_weight_ref[...])).astype(bf16)
    back.wait()


def prepare_kernel(w, n, r, mine_ref, other_ref, rows_ref, qkv_ref, pack_ref, logits_ref, values_ref):
    odd = pack_ref[POINT_WEIGHT + 1 : POINT_WEIGHT + 2, 0:1] > 0.5
    mine, other = mine_ref[...].astype(f32), other_ref[...].astype(f32)
    halves = [jnp.where(odd, other, mine).astype(bf16), jnp.where(odd, mine, other).astype(bf16)]
    slots = jnp.concatenate([quarter_of(halves[q & 1], 0, q >> 1, w, r, n) for q in range(4)], axis=1)
    logits, values = logits_and_values(
        slots, (rows_ref[:, 0:768], rows_ref[:, 768:769]), pack_ref[FRAME : FRAME + IP], qkv_ref[...],
        pack_ref[BIAS : BIAS + ROWS],
    )
    logits_ref[...] = logits
    values_ref[...] = values


def update_kernel(
    w, n, recv_ref, pair_any, gate_ref, logits_ref, values_ref, pack_ref, out_weight_ref,
    pair_out_any, half_ref, bias_ref, state_ref, new_frame_ref, send_ref, pair_ref, wide_ref, sems,
):
    r, count, _ = pair_ref.shape
    loads = copies(sems, *((pair_any.at[i], pair_ref.at[i]) for i in range(r)))
    tri_out = gate_ref[r * count :, :]
    row, column = grid_of((2 * CH, 2 * CH))
    c = row & (CH - 1)
    take = onehot(column == (c >> log2(w)) * 2 * w + (row >> log2(CH)) * w + (c & (w - 1)))
    if by_channel(w, count):
        for low in range(2):
            wide_ref[low] = recv_ref[:, low * count : (low + 1) * count].astype(f32)
        product = jnp.concatenate(
            [
                jnp.concatenate([wide_ref[low, pl.ds(q, n, stride=2 * w), :] for q in range(2 * w)], axis=0)
                for low in range(2)
            ],
            axis=1,
        )
    else:
        product = dot(take, recv_ref[...])
    updates = []
    for high in range(2):
        normed = layer_norm(product[high * CH : (high + 1) * CH], axis=0).astype(bf16)
        updates.append(dot_tn(normed, tri_out))
    update = jnp.concatenate(updates, axis=0)
    bias_weight = pack_ref[BIAS : BIAS + CH, :]
    _, lane = grid_of((CH, 128))
    bias_weight = jnp.concatenate(
        [jnp.where(((lane & (IP - 1)) == i) & (lane < ROWS), bias_weight, 0.0) for i in range(r)], axis=0
    )
    for load in loads:
        load.wait()
    pair = pair_ref[...].reshape(r * count, CH)
    pair_out = pair + gate_ref[0 : r * count, :].astype(f32) * update
    pair_ref[...] = pair_out.reshape(r, count, CH)
    store = pltpu.make_async_copy(pair_ref, pair_out_any, sems.at[r])
    store.start()
    normed_pair = layer_norm(pair_out)
    halves = normed_pair.astype(bf16)
    half_ref[...] = halves
    side_by_side = jnp.concatenate([normed_pair[i * count : (i + 1) * count] for i in range(r)], axis=1)
    bias = (dot_close(side_by_side, bias_weight) * third).T[0:ROWS]
    bias_ref[...] = bias
    state, frame = attend(
        r, logits_ref[...] + bias, values_ref[...], halves, wide(pack_ref, STATE), pack_ref[FRAME : FRAME + IP],
        lambda: (out_weight_ref, wide(pack_ref, FRAME_WEIGHT)),
    )
    state_ref[...] = state
    new_frame_ref[...] = frame
    fill_rows(send_ref, 0, spread_rows(slots_of(state, frame), w, r))
    store.wait()


def last_kernel(
    w, n, r, recv_ref, half_ref, bias_ref, state_ref, frame_ref, pack_ref, qkv_ref, out_weight_ref,
    single_out_ref, rotation_ref, translation_ref, scr, wide_ref, slots_ref,
):
    if by_channel(w, n * r):
        for low in range(2):
            wide_ref[low] = recv_ref[:, low * 128 : (low + 1) * 128].astype(f32)
        for quarter in range(4):
            for i in range(r):
                part = wide_ref[quarter & 1, pl.ds((quarter >> 1) * r + i, n, stride=2 * w), :]
                slots_ref[quarter, pl.ds(i, n, stride=r), :] = part
        slots = jnp.concatenate([slots_ref[quarter] for quarter in range(4)], axis=1)
    else:
        slots = natural_rows(recv_ref, 0, w, r, n)
    state, frame = state_ref[...], frame_ref[...]
    own = own_side(state, frame, qkv_ref, pack_ref[POINT_WEIGHT : POINT_WEIGHT + 1])
    logits, values = logits_and_values(slots, own, frame, qkv_ref[...], pack_ref[BIAS : BIAS + ROWS])
    state, frame = attend(
        r, logits + bias_ref[...], values, half_ref[...], state, frame,
        lambda: (out_weight_ref, wide(pack_ref, FRAME_WEIGHT)),
    )
    single_out_ref[...] = state[0:r]
    rotation_ref[...] = frame[0:r, 0:9]
    scr[...] = jnp.concatenate([frame, jnp.zeros((128 - IP, 128), f32)], axis=0).T
    translation_ref[...] = scr[9:12, 0:r]


VMEM = pl.BlockSpec(memory_space=pltpu.VMEM)
HBM = pl.BlockSpec(memory_space=pltpu.HBM)


def call(body, name, outs, args, outside=(), outside_outs=(), scratch=(), limit=32, alias=None, flops=0, moved=0):
    return pl.pallas_call(
        body,
        name=name,
        out_shape=[jax.ShapeDtypeStruct(s, d) for s, d in outs],
        in_specs=[HBM if at in outside else VMEM for at in range(len(args))],
        out_specs=[HBM if at in outside_outs else VMEM for at in range(len(outs))],
        scratch_shapes=list(scratch),
        input_output_aliases=alias or {},
        compiler_params=pltpu.CompilerParams(vmem_limit_bytes=limit * 2**20),
        cost_estimate=pl.CostEstimate(flops=flops, bytes_accessed=moved, transcendentals=0),
    )(*args)


def local(
    pair, single, quats, translate, res_mask, chain_ids, tri_weight, tri_out_weight, qkv_weight, bias_weight,
    head_gamma, chain_bias, out_weight, frame_weight,
):
    n = lax.axis_size("row")
    r, count, _ = pair.shape
    w = CH // n
    rows = 2 * w
    lanes = r * SLOT // rows
    limit = 24 if count == 128 else 56

    def exchange(sent):
        width = sent.shape[1]
        got = lax.all_to_all(sent.reshape(n, rows, width), "row", 0, 0, tiled=True)
        return got.reshape(n * rows, width)

    def like(array):
        return pltpu.VMEM(array.shape, array.dtype)

    dma = pltpu.SemaphoreType.DMA
    sent, frame = call(
        functools.partial(gate_kernel, w, n),
        "gate",
        [((n * rows, r * count + lanes // 2), bf16), ((IP, 128), f32)],
        [pair, tri_weight, single, quats, translate, res_mask, chain_ids],
        outside=range(7),
        scratch=[
            like(pair),
            pltpu.VMEM((CH, 4 * CH), bf16),
            like(single),
            like(quats),
            like(translate),
            pltpu.SMEM((r,), jnp.int32),
            pltpu.SMEM((r,), jnp.int32),
            pltpu.VMEM((128, 128), f32),
            dma((r + 6,)),
        ],
        limit=60,
    )
    received = exchange(sent)

    point_weight = head_gamma * (math.sqrt(2.0 / (9.0 * PQ)) * 0.5 * third)
    columns = jnp.pad(jnp.repeat(chain_bias.T, IP, axis=0), ((0, CH - ROWS + IP), (ROWS, 126 - ROWS)))
    columns = columns.at[CH, 0 : H * PQ].set(jnp.repeat(point_weight, PQ))
    columns = columns.at[CH + 1, 0].set((lax.axis_index("row") & 1).astype(f32))
    gate, query_rows, pack, pair_copy = call(
        functools.partial(own_kernel, w),
        "own",
        [
            ((r * count + CH, CH), bf16),
            ((ROWS, 896), f32),
            ((PACK_ROWS, 128), f32),
            (pair.shape, f32),
        ],
        [pair, tri_weight, qkv_weight, single, frame, columns, tri_out_weight, bias_weight.T, frame_weight.T],
        outside=range(9),
        outside_outs=(3,),
        scratch=[
            like(pair),
            pltpu.VMEM((CH, CH), bf16),
            like(qkv_weight),
            like(single),
            like(columns),
            like(tri_out_weight),
            pltpu.VMEM((H, CH), f32),
            pltpu.VMEM((6, CS), f32),
            dma((10,)),
        ],
        limit=60,
        flops=2 * r * count * CH * CH,
        moved=16 * 2**20,
    )
    received, gate, query_rows, pack, pair_copy = lax.optimization_barrier(
        (received, gate, query_rows, pack, pair_copy)
    )
    formed, slots = call(
        functools.partial(product_kernel, w, n, r),
        "product",
        [((n * rows, (r // 2) * count), bf16), ((n * rows, lanes // 2), bf16)],
        [received],
        scratch=[pltpu.VMEM((w, 256, 128), f32)],
        limit=limit,
    )
    products = exchange(formed)
    other = lax.ppermute(slots, "row", [(i, i ^ 1) for i in range(n)])
    logits, values = call(
        functools.partial(prepare_kernel, w, n, r),
        "prepare",
        [((ROWS, count), f32), ((count, 640), f32)],
        [slots, other, query_rows, qkv_weight, pack],
        limit=limit,
        flops=2 * count * CS * 1152,
        moved=8 * 2**20,
    )
    pair_out, pair_half, bias, state, frame, sent = call(
        functools.partial(update_kernel, w, n),
        "update",
        [
            ((r, count, CH), f32),
            ((r * count, CH), bf16),
            ((ROWS, count), f32),
            ((IP, CS), f32),
            ((IP, 128), f32),
            ((n * rows, lanes), bf16),
        ],
        [products, pair_copy, gate, logits, values, pack, out_weight],
        outside=(1,),
        outside_outs=(0,),
        alias={1: 0},
        scratch=[like(pair), pltpu.VMEM((2, 2 * CH, 128), f32), dma((r + 1,))],
        limit=limit,
    )
    received = exchange(sent)
    single_out, rotation, translation = call(
        functools.partial(last_kernel, w, n, r),
        "last",
        [((r, CS), f32), ((r, 9), f32), ((3, r), f32)],
        [received, pair_half, bias, state, frame, pack, qkv_weight, out_weight],
        scratch=[pltpu.VMEM((128, 128), f32), pltpu.VMEM((2, 256, 128), f32), pltpu.VMEM((4, 128, 128), f32)],
        limit=limit,
    )
    return (pair_out, single_out, rotation.T, translation)


def solution(mesh):
    rows = ("grp", "row")
    placed = (P(rows, None, None), P(rows, None), P(None, rows), P(None, rows), P(rows), P(rows)) + (P(),) * 8
    return jax.shard_map(
        local,
        mesh=mesh,
        in_specs=placed,
        out_specs=(P(rows, None, None), P(rows, None), P(None, rows), P(None, rows)),
        check_vma=False,
    )
```
